32 devices in a mesh: dp: 16 (over z, y, core), tensor: 2 (over x).
Axes of the slice: x: 2, y: 2, z: 4, core: 2. Of those that a mesh axis runs over, the one named last changes fastest.
Arguments:
- inputs: bfloat16 [1024, 16, 1024], P('tensor', 'dp'), may hold values from -6 to 6
- segment_ids: int32 [1024, 16], P(None, 'dp'), may hold values from 0 to 512, as said below
- first_gain: bfloat16 [1024], replicated, may hold values from 0.25 to 1.75
- first_shift: bfloat16 [1024], replicated, may hold values from -1.75 to 1.75
- qkv_weight: bfloat16 [1024, 3, 1024], P(None, None, 'tensor'), may hold values from -0.1875 to 0.1875
- qv_bias: bfloat16 [2, 1024], P(None, 'tensor'), may hold values from -3 to 3
- out_weight: bfloat16 [1024, 1024], P('tensor'), may hold values from -1 to 1
- out_bias: bfloat16 [1024], replicated, may hold values from -3 to 3
- second_gain: bfloat16 [1024], replicated, may hold values from 0.25 to 1.75
- second_shift: bfloat16 [1024], replicated, may hold values from -1.75 to 1.75
- up_weight: bfloat16 [1024, 4096], P(None, 'tensor'), may hold values from -0.1875 to 0.1875
- up_bias: bfloat16 [4096], P('tensor'), may hold values from -3 to 3
- down_weight: bfloat16 [4096, 1024], P('tensor'), may hold values from -0.09375 to 0.09375
- down_bias: bfloat16 [1024], replicated, may hold values from -3 to 3
- cotangent: bfloat16 [1024, 16, 1024], P('tensor', 'dp'), may hold values from -6 to 6
Outputs:
- layer_output: bfloat16 [1024, 16, 1024], P('tensor', 'dp')
- input_grad: float32 [1024, 16, 1024], P('tensor', 'dp')
- first_gain_grad: float32 [1024], replicated
- first_shift_grad: float32 [1024], replicated
- qkv_weight_grad: float32 [1024, 3, 1024], P('dp', None, 'tensor')
- qv_bias_grad: float32 [2, 1024], P(None, 'tensor')
- out_weight_grad: float32 [1024, 1024], P('tensor', 'dp')
- out_bias_grad: float32 [1024], replicated
- second_gain_grad: float32 [1024], replicated
- second_shift_grad: float32 [1024], replicated
- up_weight_grad: float32 [1024, 4096], P('dp', 'tensor')
- up_bias_grad: float32 [4096], P('tensor')
- down_weight_grad: float32 [4096, 1024], P('tensor', 'dp')
- down_bias_grad: float32 [1024], replicated
The draws below stay inside these ranges and needn't reach their ends.
Inputs may be any that keep to these rules, and one draw needn't show every extreme that they name: `segment_ids`: along each sequence the ids start at 0, never fall and rise by one at the start of each new document. Each sequence has one long document that starts at one of its first 257 positions and ends at one of its last 257 positions; the others are short. In one sequence, chosen by the seed, every position outside the long document is a document of its own.
All inputs are finite; a program needn't handle non-finite values.
Results may differ from the reference program's by a relative error of at most 0.012.
The reference program's roundings to bfloat16 on the way count: a program that leaves them out, or rounds other values in their place, can miss the bound.
Values may be sent and summed in bfloat16 or wider, within the bound.
A program may use at most 192 MiB of HBM per device.

```python
import jax
import jax.numpy as jnp
from jax import lax

D = 1024
HEADS = 16
HEAD_DIM = 64
FF = 4096
SEQ_LEN = 1024
ROWS_DEV = 512
SEQS = 16


def draw_segment_ids(key, part):
    key = jax.random.fold_in(key, 7)
    key_start, key_end, key_breaks, key_pick = jax.random.split(key, 4)
    half_rows = max(ROWS_DEV // 2, 1)
    chosen = jax.random.randint(key_pick, (), 0, SEQS)
    seq_pos = jnp.arange(SEQS, dtype=jnp.int32)
    is_full = seq_pos == chosen
    doc_start = jax.random.randint(key_start, (SEQS,), 0, half_rows + 1)
    doc_end = jax.random.randint(key_end, (SEQS,), SEQ_LEN - 1 - half_rows, SEQ_LEN)
    doc_start = jnp.where(is_full, half_rows, doc_start)
    doc_end = jnp.where(is_full, SEQ_LEN - 1 - half_rows, doc_end)
    breaks = (jax.random.randint(key_breaks, (SEQ_LEN, SEQS), 0, 64) == 0).astype(jnp.int32)
    breaks = jnp.where(is_full[None, :], 1, breaks)
    positions = jnp.arange(SEQ_LEN, dtype=jnp.int32)[:, None]
    inside = (positions > doc_start[None, :]) & (positions <= doc_end[None, :])
    breaks = jnp.where(inside, 0, breaks)
    breaks = jnp.where(positions == doc_start[None, :], 1, breaks)
    breaks = jnp.where(positions == doc_end[None, :] + 1, 1, breaks)
    breaks = jnp.where(positions == 0, 0, breaks)
    return jnp.cumsum(breaks, axis=0).astype(jnp.int32)


def levels(own_key, shape, shards, least, largest):
    loudness = 1.0
    for axis_at, shards_of in shards:
        heights = jax.random.uniform(jax.random.fold_in(jax.random.fold_in(own_key, 6), axis_at), (shards_of,), jnp.float32, least / len(shards), largest / len(shards))
        loudness = loudness * jnp.repeat(jnp.exp(heights), shape[axis_at] // shards_of).reshape((-1,) + (1,) * (len(shape) - 1 - axis_at))
    return loudness


def gaussian(rng, dims, scale, bound, cuts=(), kind=jnp.bfloat16):
    values = jax.random.normal(rng, dims, jnp.float32) * scale
    if len(cuts) > 0:
        values = levels(rng, dims, cuts, -0.22, 0.18) * values
    return jnp.clip(values, min=-bound, max=bound).astype(kind)


def setup_inputs(seed: int = 0) -> dict:
    arg_keys = jax.random.split(jax.random.key(seed), 16)
    inputs = gaussian(arg_keys[0], (SEQ_LEN, SEQS, D), 1.0, 6.0, ((0, 2), (1, 16)))
    segment_ids = draw_segment_ids(jax.random.fold_in(arg_keys[15], 71), 0)
    first_gain = jnp.clip(1.0 + 0.15 * jax.random.normal(arg_keys[2], (D,), jnp.float32), 0.25, 1.75).astype(jnp.bfloat16)
    first_shift = gaussian(arg_keys[3], (D,), 0.3, 1.75)
    qkv_weight = gaussian(arg_keys[4], (D, 3, D), D ** -0.5, 0.1875, ((2, 2),))
    qv_bias = gaussian(arg_keys[5], (2, D), 0.5, 3.0, ((1, 2),))
    out_weight = gaussian(arg_keys[6], (D, D), (D // 32) ** -0.5, 1.0, ((0, 2),))
    out_bias = gaussian(arg_keys[7], (D,), 0.5, 3.0)
    second_gain = jnp.clip(1.0 + 0.15 * jax.random.normal(arg_keys[8], (D,), jnp.float32), 0.25, 1.75).astype(jnp.bfloat16)
    second_shift = gaussian(arg_keys[9], (D,), 0.3, 1.75)
    up_weight = gaussian(arg_keys[10], (D, FF), D ** -0.5, 0.1875, ((1, 2),))
    up_bias = gaussian(arg_keys[11], (FF,), 0.5, 3.0, ((0, 2),))
    down_weight = gaussian(arg_keys[12], (FF, D), FF ** -0.5, 0.09375, ((0, 2),))
    down_bias = gaussian(arg_keys[13], (D,), 0.5, 3.0)
    cotangent = gaussian(arg_keys[14], (SEQ_LEN, SEQS, D), 1.0, 6.0, ((0, 2), (1, 16)))
    return {"inputs": inputs, "segment_ids": segment_ids, "first_gain": first_gain, "first_shift": first_shift, "qkv_weight": qkv_weight, "qv_bias": qv_bias, "out_weight": out_weight, "out_bias": out_bias, "second_gain": second_gain, "second_shift": second_shift, "up_weight": up_weight, "up_bias": up_bias, "down_weight": down_weight, "down_bias": down_bias, "cotangent": cotangent}


@jax.custom_vjp
def low(v):
    return lax.optimization_barrier(v.astype(jnp.bfloat16)).astype(jnp.float32)

@jax.custom_vjp
def low_back(v):
    return v

def low_keep(v):
    return (low(v), None)

def low_pass(kept, grad):
    return (grad,)

def back_keep(v):
    return (v, None)

def back_low(kept, grad):
    return (low(grad),)
low.defvjp(low_keep, low_pass)
low_back.defvjp(back_keep, back_low)
highest = lax.Precision.HIGHEST
norm_eps = 1e-05

def layer_norm(value, gain, shift):
    row_mean = lax.optimization_barrier(jnp.mean(value, axis=-1, keepdims=True))
    centred = value - row_mean
    variance = lax.optimization_barrier(jnp.mean(centred * centred, axis=-1, keepdims=True))
    return centred * lax.rsqrt(variance + norm_eps) * gain + shift

def gelu_tanh(value):
    return 0.5 * value * (1.0 + jnp.tanh(0.7978845608028654 * (value + 0.044715 * value * value * value)))

def attention(queries, keys_all, values_all, seg_row):
    block_rows = min(512, SEQ_LEN)
    score_scale = HEAD_DIM ** (-0.5)
    key_pos = jnp.arange(SEQ_LEN, dtype=jnp.int32)

    def one_block(block_index):
        row_start = block_index * block_rows
        query_block = lax.dynamic_slice_in_dim(queries, row_start, block_rows, 0)
        seg_block = lax.dynamic_slice_in_dim(seg_row, row_start, block_rows, 0)
        query_pos = row_start + jnp.arange(block_rows, dtype=jnp.int32)
        scores = low_back(jnp.einsum('qhd,khd->hqk', query_block, keys_all, precision=highest) * score_scale)
        allowed = (seg_block[:, None] == seg_row[None, :]) & (query_pos[:, None] >= key_pos[None, :])
        scores = jnp.where(allowed[None], scores, -1e+30)
        row_top = lax.optimization_barrier(jnp.max(scores, axis=-1, keepdims=True))
        weights = jnp.exp(scores - row_top)
        probs = low(weights / lax.optimization_barrier(jnp.sum(weights, axis=-1, keepdims=True)))
        return jnp.einsum('hqk,khd->qhd', probs, values_all, precision=highest)
    mixed = lax.map(jax.checkpoint(one_block), jnp.arange(SEQ_LEN // block_rows, dtype=jnp.int32))
    return mixed.reshape(SEQ_LEN, D)

def sequence_layer(seg_row, inputs_row, first_gain, first_shift, qkv_weight, qv_bias, out_weight, out_bias, second_gain, second_shift, up_weight, up_bias, down_weight, down_bias):
    first_norm = low(layer_norm(inputs_row, first_gain, first_shift))
    qkv_bias = jnp.concatenate([qv_bias[0], jnp.zeros((D,), jnp.float32), qv_bias[1]])
    qkv_pre = jnp.dot(first_norm, qkv_weight.reshape(D, 3 * D), precision=highest) + qkv_bias
    qkv = low(low_back(qkv_pre))
    queries = qkv[:, :D].reshape(SEQ_LEN, HEADS, HEAD_DIM)
    keys_all = qkv[:, D:2 * D].reshape(SEQ_LEN, HEADS, HEAD_DIM)
    values_all = qkv[:, 2 * D:].reshape(SEQ_LEN, HEADS, HEAD_DIM)
    mixed = low(low_back(attention(queries, keys_all, values_all, seg_row)))
    attn_branch = low_back(jnp.dot(mixed, out_weight, precision=highest) + out_bias)
    residual_mid = inputs_row + attn_branch
    second_norm = low(layer_norm(residual_mid, second_gain, second_shift))
    hidden_pre = low_back(jnp.dot(second_norm, up_weight, precision=highest) + up_bias)
    hidden = low(gelu_tanh(hidden_pre))
    mlp_branch = low_back(jnp.dot(hidden, down_weight, precision=highest) + down_bias)
    return residual_mid + mlp_branch

def reference(inputs, segment_ids, first_gain, first_shift, qkv_weight, qv_bias, out_weight, out_bias, second_gain, second_shift, up_weight, up_bias, down_weight, down_bias, cotangent):
    params = tuple((p.astype(jnp.float32) for p in (first_gain, first_shift, qkv_weight, qv_bias, out_weight, out_bias, second_gain, second_shift, up_weight, up_bias, down_weight, down_bias)))

    def one_sequence(totals, seq_index):
        inputs_row = lax.dynamic_index_in_dim(inputs, seq_index, 1, keepdims=False).astype(jnp.float32)
        seg_row = lax.dynamic_index_in_dim(segment_ids, seq_index, 1, keepdims=False).astype(jnp.int32)
        grad_row = lax.dynamic_index_in_dim(cotangent, seq_index, 1, keepdims=False).astype(jnp.float32)
        layer_row, pull_back = jax.vjp(partial_layer(seg_row), inputs_row, *params)
        grads = pull_back(grad_row)
        totals = tuple((t + g for t, g in zip(totals, grads[1:])))
        return (totals, (layer_row.astype(jnp.bfloat16), grads[0]))
    zeros_init = tuple((jnp.zeros_like(p) for p in params))
    totals, (layer_rows, input_rows) = lax.scan(one_sequence, zeros_init, jnp.arange(SEQS, dtype=jnp.int32))
    layer_output = jnp.transpose(layer_rows, (1, 0, 2))
    input_grad = jnp.transpose(input_rows, (1, 0, 2))
    return (layer_output, input_grad, totals[0], totals[1], totals[2], totals[3], totals[4], totals[5], totals[6], totals[7], totals[8], totals[9], totals[10], totals[11])

def partial_layer(seg_row):

    def layer_of(*values):
        return sequence_layer(seg_row, *values)
    return layer_of
```

```python
import functools

import jax
import jax.numpy as jnp
from jax import lax
from jax.experimental import pallas as pl
from jax.experimental.pallas import tpu as pltpu
from jax.sharding import PartitionSpec as P

HEAD_DIM = 64
MESH = pl.DeviceIdType.MESH
F32 = jnp.float32
BF16 = jnp.bfloat16
VMEM_LIMIT = 60 << 20


norm_eps = 1e-05


def layer_norm(value, gain, shift):
    row_mean = jnp.mean(value, axis=-1, keepdims=True)
    centred = value - row_mean
    variance = jnp.mean(centred * centred, axis=-1, keepdims=True)
    return centred * lax.rsqrt(variance + norm_eps) * gain + shift


def gelu_tanh(value):
    return (
        0.5
        * value
        * (1.0 + jnp.tanh(0.7978845608028654 * (value + 0.044715 * value * value * value)))
    )


def masked_scores(query_block, keys_all, seg_block, seg_all, row_start, block_rows, score_scale):
    scores = (
        jnp.einsum("qhd,khd->hqk", query_block, keys_all, preferred_element_type=jnp.float32)
        * score_scale
    )
    key_pos = jnp.arange(keys_all.shape[0], dtype=jnp.int32)
    query_pos = row_start + jnp.arange(block_rows, dtype=jnp.int32)
    allowed = (seg_block[:, None] == seg_all[None, :]) & (query_pos[:, None] >= key_pos[None, :])
    return jnp.where(allowed[None], scores, -1e30)


def attend_forward(queries, keys_all, values_all, seg_all, score_scale):
    seq_len = queries.shape[0]
    block_rows = min(512, seq_len)

    def one_block(block_index):
        row_start = block_index * block_rows
        query_block = lax.dynamic_slice_in_dim(queries, row_start, block_rows, 0)
        seg_block = lax.dynamic_slice_in_dim(seg_all, row_start, block_rows, 0)
        scores = masked_scores(
            query_block, keys_all, seg_block, seg_all, row_start, block_rows, score_scale
        )
        row_top = jnp.max(scores, axis=-1, keepdims=True)
        weights = jnp.exp(scores - row_top)
        row_total = jnp.sum(weights, axis=-1, keepdims=True)
        probs_low = (weights / row_total).astype(jnp.bfloat16)
        mixed = jnp.einsum(
            "hqk,khd->qhd", probs_low, values_all, preferred_element_type=jnp.float32
        )
        return (mixed, row_top + jnp.log(row_total))

    mixed, log_total = lax.map(one_block, jnp.arange(seq_len // block_rows, dtype=jnp.int32))
    return (mixed.reshape(seq_len, -1), log_total)


def attend_backward(queries, keys_all, values_all, seg_all, log_total, out_grad, score_scale):
    seq_len = queries.shape[0]
    block_rows = min(512, seq_len)

    def one_block(carry, block_index):
        key_grad, value_grad = carry
        row_start = block_index * block_rows
        query_block = lax.dynamic_slice_in_dim(queries, row_start, block_rows, 0)
        seg_block = lax.dynamic_slice_in_dim(seg_all, row_start, block_rows, 0)
        grad_block = lax.dynamic_slice_in_dim(out_grad, row_start, block_rows, 0)
        scores = masked_scores(
            query_block, keys_all, seg_block, seg_all, row_start, block_rows, score_scale
        )
        probs = jnp.exp(scores - log_total[block_index])
        probs_low = probs.astype(jnp.bfloat16)
        value_grad = value_grad + jnp.einsum(
            "hqk,qhd->khd", probs_low, grad_block, preferred_element_type=jnp.float32
        )
        prob_grad = jnp.einsum(
            "qhd,khd->hqk", grad_block, values_all, preferred_element_type=jnp.float32
        )
        row_dot = jnp.sum(probs * prob_grad, axis=-1, keepdims=True)
        score_grad = (probs * (prob_grad - row_dot)).astype(jnp.bfloat16)
        query_grad = (
            jnp.einsum("hqk,khd->qhd", score_grad, keys_all, preferred_element_type=jnp.float32)
            * score_scale
        )
        key_grad = (
            key_grad
            + jnp.einsum(
                "hqk,qhd->khd", score_grad, query_block, preferred_element_type=jnp.float32
            )
            * score_scale
        )
        return ((key_grad, value_grad), query_grad)

    zero_grads = jnp.zeros(keys_all.shape, jnp.float32)
    (key_grad, value_grad), query_grad = lax.scan(
        one_block, (zero_grads, zero_grads), jnp.arange(seq_len // block_rows, dtype=jnp.int32)
    )
    return (
        query_grad.reshape(seq_len, -1),
        key_grad.reshape(seq_len, -1),
        value_grad.reshape(seq_len, -1),
    )


def row_product(left, right, contract):
    return lax.dot_general(
        left, right, (((1,), (contract,)), ((), ())), preferred_element_type=jnp.float32
    )


def rows_contract(left, right):
    return lax.dot_general(
        left, right, (((0,), (0,)), ((), ())), preferred_element_type=jnp.float32
    )


def on_device(
    inputs,
    segment_ids,
    first_gain,
    first_shift,
    qkv_weight,
    qv_bias,
    out_weight,
    out_bias,
    second_gain,
    second_shift,
    up_weight,
    up_bias,
    down_weight,
    down_bias,
    cotangent,
):
    rows_dev, seq_count, model_width = inputs.shape
    tensor_count = lax.axis_size("tensor")
    tensor_rank = lax.axis_index("tensor")
    seq_len = rows_dev * tensor_count
    local_width = out_weight.shape[0]
    heads_dev = local_width // HEAD_DIM
    hidden_dev = up_weight.shape[1]
    local_rows = rows_dev * seq_count
    score_scale = HEAD_DIM ** (-0.5)
    residual_in = inputs.reshape(local_rows, model_width).astype(jnp.float32)
    gain_one = first_gain.astype(jnp.float32)
    shift_one = first_shift.astype(jnp.float32)
    gain_two = second_gain.astype(jnp.float32)
    shift_two = second_shift.astype(jnp.float32)
    normed_one, pull_one = jax.vjp(layer_norm, residual_in, gain_one, shift_one)
    first_local = normed_one.astype(jnp.bfloat16)
    first_rows = lax.all_gather(first_local, "tensor", axis=0, tiled=True)
    qkv_flat = qkv_weight.reshape(model_width, 3 * local_width)
    qkv_bias = jnp.concatenate(
        [
            qv_bias[0].astype(jnp.float32),
            jnp.zeros((local_width,), jnp.float32),
            qv_bias[1].astype(jnp.float32),
        ]
    )
    qkv_low = (jnp.dot(first_rows, qkv_flat, preferred_element_type=jnp.float32) + qkv_bias).astype(
        jnp.bfloat16
    )
    qkv_split = qkv_low.reshape(seq_len, seq_count, 3, heads_dev, HEAD_DIM)
    seq_index = 0
    mixed_one, log_one = attend_forward(
        qkv_split[:, seq_index, 0],
        qkv_split[:, seq_index, 1],
        qkv_split[:, seq_index, 2],
        segment_ids[:, seq_index],
        score_scale,
    )
    mixed_list = [mixed_one]
    log_list = [log_one]
    mixed_low = (
        jnp.stack(mixed_list, axis=1).reshape(seq_len * seq_count, local_width).astype(jnp.bfloat16)
    )
    attn_local = lax.psum_scatter(
        row_product(mixed_low, out_weight, 0), "tensor", scatter_dimension=0, tiled=True
    )
    residual_mid = residual_in + attn_local + out_bias.astype(jnp.float32)
    normed_two, pull_two = jax.vjp(layer_norm, residual_mid, gain_two, shift_two)
    second_local = normed_two.astype(jnp.bfloat16)
    second_rows = lax.all_gather(second_local, "tensor", axis=0, tiled=True)
    hidden_pre = jnp.dot(
        second_rows, up_weight, preferred_element_type=jnp.float32
    ) + up_bias.astype(jnp.float32)
    activated, pull_gelu = jax.vjp(gelu_tanh, hidden_pre)
    hidden_low = activated.astype(jnp.bfloat16)
    mlp_local = lax.psum_scatter(
        row_product(hidden_low, down_weight, 0).astype(jnp.bfloat16),
        "tensor",
        scatter_dimension=0,
        tiled=True,
    ).astype(jnp.float32)
    layer_output = (residual_mid + mlp_local + down_bias.astype(jnp.float32)).astype(jnp.bfloat16)
    layer_output = layer_output.reshape(rows_dev, seq_count, model_width)
    grad_local = cotangent.reshape(local_rows, model_width)
    grad_rows = lax.all_gather(grad_local, "tensor", axis=0, tiled=True)
    down_grad = rows_contract(hidden_low, grad_rows)
    hidden_grad = lax.dot_general(
        grad_rows, down_weight, (((1,), (1,)), ((), ())), preferred_element_type=jnp.float32
    )
    (pre_grad,) = pull_gelu(hidden_grad)
    pre_low = pre_grad.astype(jnp.bfloat16)
    up_sums = jnp.sum(pre_low, axis=0, dtype=jnp.float32)
    second_back = lax.all_gather(second_local, "tensor", axis=0, tiled=True)
    up_grad = rows_contract(second_back, pre_low)
    second_norm_grad = lax.psum_scatter(
        row_product(pre_low, up_weight, 1), "tensor", scatter_dimension=0, tiled=True
    )
    mid_from_norm, gain_two_grad, shift_two_grad = pull_two(second_norm_grad)
    residual_grad = grad_local.astype(jnp.float32) + mid_from_norm
    residual_low = residual_grad.astype(jnp.bfloat16)
    residual_rows = lax.all_gather(residual_low, "tensor", axis=0, tiled=True)
    out_grad_weight = rows_contract(mixed_low, residual_rows)
    mixed_grad = lax.dot_general(
        residual_rows, out_weight, (((1,), (1,)), ((), ())), preferred_element_type=jnp.float32
    ).astype(jnp.bfloat16)
    mixed_grad = mixed_grad.reshape(seq_len, seq_count, heads_dev, HEAD_DIM)
    seq_index = 0
    query_grad, key_grad, value_grad = attend_backward(
        qkv_split[:, seq_index, 0],
        qkv_split[:, seq_index, 1],
        qkv_split[:, seq_index, 2],
        segment_ids[:, seq_index],
        log_list[seq_index],
        mixed_grad[:, seq_index],
        score_scale,
    )
    query_list = [query_grad]
    key_list = [key_grad]
    value_list = [value_grad]
    qkv_grad = jnp.concatenate(
        [jnp.stack(query_list, axis=1), jnp.stack(key_list, axis=1), jnp.stack(value_list, axis=1)],
        axis=-1,
    )
    qkv_grad_low = qkv_grad.reshape(seq_len * seq_count, 3 * local_width).astype(jnp.bfloat16)
    qkv_sums = jnp.sum(qkv_grad_low, axis=0, dtype=jnp.float32)
    qv_sums = jnp.stack([qkv_sums[:local_width], qkv_sums[2 * local_width :]], axis=0)
    first_back = lax.all_gather(first_local, "tensor", axis=0, tiled=True)
    qkv_grad_weight = rows_contract(first_back, qkv_grad_low).reshape(model_width, 3, local_width)
    first_norm_grad = lax.psum_scatter(
        row_product(qkv_grad_low, qkv_flat, 1), "tensor", scatter_dimension=0, tiled=True
    )
    in_from_norm, gain_one_grad, shift_one_grad = pull_one(first_norm_grad)
    input_grad = (residual_grad + in_from_norm).reshape(rows_dev, seq_count, model_width)
    qkv_share, out_share, up_share, down_share = (
        lax.psum_scatter(qkv_grad_weight, "dp", scatter_dimension=0, tiled=True),
        lax.psum_scatter(out_grad_weight, "dp", scatter_dimension=1, tiled=True),
        lax.psum_scatter(up_grad, "dp", scatter_dimension=0, tiled=True),
        lax.psum_scatter(down_grad, "dp", scatter_dimension=1, tiled=True),
    )
    out_bias_part = jnp.sum(residual_low, axis=0, dtype=jnp.float32)
    down_bias_part = jnp.sum(grad_local, axis=0, dtype=jnp.float32)
    stacked = jnp.stack(
        [
            gain_one_grad,
            shift_one_grad,
            gain_two_grad,
            shift_two_grad,
            out_bias_part,
            down_bias_part,
        ],
        axis=0,
    )
    qv_full = lax.dynamic_update_slice(
        jnp.zeros((2, model_width), jnp.float32), qv_sums, (jnp.int32(0), tensor_rank * local_width)
    )
    up_full = lax.dynamic_update_slice(
        jnp.zeros((hidden_dev * tensor_count,), jnp.float32), up_sums, (tensor_rank * hidden_dev,)
    )
    stacked, qv_total, up_total = lax.psum((stacked, qv_full, up_full), ("dp", "tensor"))
    qv_share = lax.dynamic_slice_in_dim(qv_total, tensor_rank * local_width, local_width, 1)
    up_bias_share = lax.dynamic_slice_in_dim(up_total, tensor_rank * hidden_dev, hidden_dev, 0)
    return (
        layer_output,
        input_grad,
        stacked[0],
        stacked[1],
        qkv_share,
        qv_share,
        out_share,
        stacked[4],
        stacked[2],
        stacked[3],
        up_share,
        up_bias_share,
        down_share,
        stacked[5],
    )


Z_SIZE, Y_SIZE, CORES = 4, 2, 2


def place():
    dp = lax.axis_index("dp")
    side = lax.axis_index("tensor")
    return dp // 4, (dp // 2) % 2, dp % 2, side


def dev(z, y, core, side):
    return (z * 4 + y * 2 + core, side)


def peer_x():
    z, y, core, side = place()
    return dev(z, y, core, 1 - side)


def peer_y():
    z, y, core, side = place()
    return dev(z, 1 - y, core, side)


def peer_core():
    z, y, core, side = place()
    return dev(z, y, 1 - core, side)


def peer_z(step):
    z, y, core, side = place()
    return dev((z + step) % 4, y, core, side)


def greet(peers):
    barrier = pltpu.get_barrier_semaphore()
    for peer in peers:
        pl.semaphore_signal(barrier, inc=1, device_id=peer, device_id_type=MESH)
    pl.semaphore_wait(barrier, len(peers))


def remote(src, dst, send_sem, recv_sem, peer):
    return pltpu.make_async_remote_copy(
        src_ref=src, dst_ref=dst, send_sem=send_sem, recv_sem=recv_sem, device_id=peer, device_id_type=MESH
    )


def dot_nn(a, b):
    return lax.dot_general(a, b, (((1,), (0,)), ((), ())), preferred_element_type=F32)


def dot_nt(a, b):
    return lax.dot_general(a, b, (((1,), (1,)), ((), ())), preferred_element_type=F32)


def dot_tn(a, b):
    return lax.dot_general(a, b, (((0,), (0,)), ((), ())), preferred_element_type=F32)


def norm_parts(value):
    mean = jnp.mean(value, axis=-1, keepdims=True)
    centred = value - mean
    rstd = lax.rsqrt(jnp.mean(centred * centred, axis=-1, keepdims=True) + norm_eps)
    return centred * rstd, rstd


def head_lanes(h):
    lane = lax.broadcasted_iota(jnp.int32, (1, 2 * HEAD_DIM), 1)
    return (lane // HEAD_DIM) == h


def only_head(value, h):
    return jnp.where(head_lanes(h), value, jnp.zeros_like(value))


def attend_kernel(
    x_ref, gain_ref, shift_ref, wqkv_ref, bias_ref, segc_ref, segr_ref, wout_ref, ob_ref,
    a1_ref, qkv_ref, mix_ref, h_ref,
    mask_ref, send_ref, recv_ref, acc_ref, a_send, a_recv, o_send, o_recv,
):
    rows, width = x_ref.shape
    seq = 2 * rows
    local = wout_ref.shape[0]
    block = rows // 2
    piece = rows // 4
    side = lax.axis_index("tensor")
    partner = peer_x()
    own = pl.multiple_of(side * rows, rows)
    theirs = pl.multiple_of((1 - side) * rows, rows)
    greet([partner])

    def a1_copy(base, b):
        part = a1_ref.at[pl.ds(pl.multiple_of(base + b * piece, piece), piece)]
        return remote(part, part, a_send.at[b], a_recv.at[b], partner)

    gain = gain_ref[...].astype(F32)
    shift = shift_ref[...].astype(F32)
    for b in range(4):
        xhat, _ = norm_parts(x_ref[pl.ds(b * piece, piece)].astype(F32))
        at = pl.ds(pl.multiple_of(own + b * piece, piece), piece)
        a1_ref[at] = (xhat * gain + shift).astype(BF16)
        a1_copy(own, b).start()

    def project(base, count):
        at = pl.ds(pl.multiple_of(base, block), count)
        left = a1_ref[at]
        for part in range(3):
            cols = pl.ds(part * local, local)
            qkv_ref[at, cols] = (dot_nn(left, wqkv_ref[:, cols]) + bias_ref[:, cols]).astype(BF16)

    project(own, rows)

    for i in range(4):
        lo = i * block
        keys = lo + block
        is_theirs = side == (1 if i < 2 else 0)
        at = pl.ds(lo, block)

        @pl.when(is_theirs)
        def _():
            for b in (2 * (i % 2), 2 * (i % 2) + 1):
                a1_copy(theirs, b).wait_recv()
            project(lo, block)

        same = segc_ref[at] == segr_ref[:, pl.ds(0, keys)]
        q_pos = lo + lax.broadcasted_iota(jnp.int32, (block, keys), 0)
        k_pos = lax.broadcasted_iota(jnp.int32, (block, keys), 1)
        mask_ref[:, pl.ds(0, keys)] = jnp.where(same & (q_pos >= k_pos), 0.0, -1e30)

        def pair(hp, _):
            base = pl.multiple_of(hp * 2 * HEAD_DIM, 2 * HEAD_DIM)
            cols = pl.ds(base, 2 * HEAD_DIM)
            q2 = qkv_ref[at, cols]
            k2 = qkv_ref[pl.ds(0, keys), pl.ds(pl.multiple_of(local + base, 128), 2 * HEAD_DIM)]
            v2 = qkv_ref[pl.ds(0, keys), pl.ds(pl.multiple_of(2 * local + base, 128), 2 * HEAD_DIM)]
            outs = []
            for h in range(2):
                scores = dot_nt(only_head(q2, h), k2) * HEAD_DIM**-0.5 + mask_ref[:, pl.ds(0, keys)]
                weights = jnp.exp(scores - jnp.max(scores, axis=-1, keepdims=True))
                probs = weights * (1.0 / jnp.sum(weights, axis=-1, keepdims=True))
                outs.append(dot_nn(probs.astype(BF16), v2))
            mix_ref[at, cols] = jnp.where(head_lanes(0), outs[0], outs[1]).astype(BF16)
            return 0

        lax.fori_loop(0, local // (2 * HEAD_DIM), pair, 0)
        product = dot_nn(mix_ref[at], wout_ref[...])

        @pl.when(is_theirs)
        def _():
            send_ref[i % 2] = product.astype(BF16)
            remote(send_ref.at[i % 2], recv_ref.at[i % 2], o_send.at[i % 2], o_recv.at[i % 2], partner).start()

        @pl.when(jnp.logical_not(is_theirs))
        def _():
            acc_ref[pl.ds((i % 2) * block, block)] = product

    for j in range(2):
        at = pl.ds(j * block, block)
        remote(send_ref.at[j], recv_ref.at[j], o_send.at[j], o_recv.at[j], partner).wait()
        h_ref[at] = (
            x_ref[at].astype(F32) + (acc_ref[at] + recv_ref[j].astype(F32)) + ob_ref[...].astype(F32)
        )
    for b in range(4):
        a1_copy(own, b).wait_send()


def attend_call(x, gain, shift, wqkv, bias, segc, segr, wout, ob):
    rows, width = x.shape
    local = wout.shape[0]
    seq = 2 * rows
    block = rows // 2
    vm = pl.BlockSpec(memory_space=pltpu.VMEM)
    return pl.pallas_call(
        attend_kernel,
        out_shape=(
            jax.ShapeDtypeStruct((seq, width), BF16),
            jax.ShapeDtypeStruct((seq, 3 * local), BF16),
            jax.ShapeDtypeStruct((seq, local), BF16),
            jax.ShapeDtypeStruct((rows, width), F32),
        ),
        in_specs=[vm] * 9,
        out_specs=(vm,) * 4,
        scratch_shapes=[
            pltpu.VMEM((block, seq), F32),
            pltpu.VMEM((2, block, width), BF16),
            pltpu.VMEM((2, block, width), BF16),
            pltpu.VMEM((rows, width), F32),
            pltpu.SemaphoreType.DMA((4,)),
            pltpu.SemaphoreType.DMA((4,)),
            pltpu.SemaphoreType.DMA((2,)),
            pltpu.SemaphoreType.DMA((2,)),
        ],
        compiler_params=pltpu.CompilerParams(
            collective_id=0, has_side_effects=True, vmem_limit_bytes=VMEM_LIMIT
        ),
        name="attend_forward",
    )(x, gain, shift, wqkv, bias, segc, segr, wout, ob)


GATHER_CHUNKS = 2


def gather_kernel(up_ref, down_ref, ub_ref, up_o, down_o, ub_o, x_s, x_r, z_s, z_r, y_s, y_r, c_s, c_r, b_s, b_r):
    z, y, core, side = place()
    greet([peer_x(), peer_y(), peer_core()] + [peer_z(k) for k in (1, 2, 3)])
    pieces = 16
    up_rows = up_ref.shape[0] // pieces // GATHER_CHUNKS
    down_rows = down_ref.shape[0] // pieces // GATHER_CHUNKS

    def views(up, down, dp, q):
        lo_u = pl.multiple_of((dp * GATHER_CHUNKS + q) * up_rows, up_rows)
        lo_d = pl.multiple_of((dp * GATHER_CHUNKS + q) * down_rows, down_rows)
        return up.at[pl.ds(lo_u, up_rows)], down.at[pl.ds(lo_d, down_rows)]

    def copies(dp, q, send, recv, peer, source=None):
        src = views(*(source or (up_o, down_o)), dp, q)
        dst = views(up_o, down_o, dp, q)
        return [remote(src[a], dst[a], send.at[a], recv.at[a], peer) for a in range(2)]

    def piece(zz, yy, cc):
        return zz * 4 + yy * 2 + cc

    def x_copies(q):
        return copies(piece(z, y, core), q, x_s.at[q], x_r.at[q], peer_x(), (up_ref, down_ref))

    def z_sends(q, k):
        return copies(piece(z, y, core), q, z_s.at[q, k], z_r.at[q, k], peer_z(k))

    def z_recvs(q, k):
        return copies(piece((z + 4 - k) % 4, y, core), q, z_s.at[q, k], z_r.at[q, k], peer_z(k))

    def y_copies(q, k, yy):
        return copies(piece((z + 4 - k) % 4, yy, core), q, y_s.at[q, k], y_r.at[q, k], peer_y())

    def c_copies(q, k, yy, cc):
        slot = (yy + y) % 2 * 4 + k
        return copies(piece((z + 4 - k) % 4, yy, cc), q, c_s.at[q, slot], c_r.at[q, slot], peer_core())

    def start(list_of):
        for copy in list_of:
            copy.start()

    bias_copy = remote(ub_ref, ub_o, b_s, b_r, peer_x())
    bias_copy.start()
    for q in range(GATHER_CHUNKS):
        start(x_copies(q))

    def first(q):
        for copy in x_copies(q):
            copy.wait()
        for k in (2, 1, 3):
            start(z_sends(q, k))
        start(y_copies(q, 0, y))
        start(c_copies(q, 0, y, core))

    def second(q):
        for k in (1, 3, 2):
            for copy in z_recvs(q, k):
                copy.wait_recv()
            start(y_copies(q, k, y))
            start(c_copies(q, k, y, core))

    def third(q):
        for k in range(4):
            for copy in y_copies(q, k, 1 - y):
                copy.wait_recv()
            start(c_copies(q, k, 1 - y, core))

    def last(q):
        for k in range(4):
            for yy in (y, 1 - y):
                for copy in c_copies(q, k, yy, 1 - core):
                    copy.wait_recv()

    for n in range(GATHER_CHUNKS + 3):
        for stage, at in ((first, n), (second, n - 1), (third, n - 2), (last, n - 3)):
            if 0 <= at < GATHER_CHUNKS:
                stage(at)
    for q in range(GATHER_CHUNKS):
        for k in range(4):
            if k > 0:
                for copy in z_sends(q, k):
                    copy.wait_send()
            for copy in y_copies(q, k, y):
                copy.wait_send()
            for yy in (y, 1 - y):
                for copy in c_copies(q, k, yy, core):
                    copy.wait_send()
    bias_copy.wait()


def gather_call(up, down, ub):
    hbm = pl.BlockSpec(memory_space=pltpu.HBM)
    q = GATHER_CHUNKS
    sem = pltpu.SemaphoreType.DMA
    return pl.pallas_call(
        gather_kernel,
        out_shape=tuple(jax.ShapeDtypeStruct(a.shape, a.dtype) for a in (up, down, ub)),
        in_specs=[hbm] * 3,
        out_specs=(hbm,) * 3,
        scratch_shapes=[
            sem((q, 2)), sem((q, 2)), sem((q, 4, 2)), sem((q, 4, 2)), sem((q, 4, 2)), sem((q, 4, 2)),
            sem((q, 8, 2)), sem((q, 8, 2)), sem, sem,
        ],
        compiler_params=pltpu.CompilerParams(
            collective_id=1, has_side_effects=True, vmem_limit_bytes=VMEM_LIMIT
        ),
        name="gather_weights",
    )(up, down, ub)


HIDDEN_BLOCK = 512


def feed_kernel(
    h_ref, g_ref, gain_ref, shift_ref, db_ref, ub_ref, up_own, down_own, up_oth, down_oth,
    out_ref, dh_ref, vec_ref, usum_ref, keep_ref, recv_ref,
    a2_ref, a2t_ref, gt_ref, acc_ref, da2_ref, wu_ref, wd_ref, grad_ref, w_sem, k_sem, s_sem, r_sem,
):
    rows, width = h_ref.shape
    z, y, core, side = place()
    half = up_own.shape[1] // HIDDEN_BLOCK
    blocks = 2 * half
    hb = HIDDEN_BLOCK
    other = peer_core()
    greet([other])

    def fetch(j, up, down, slot):
        at = pl.ds(pl.multiple_of((j % half) * hb, hb), hb)
        return (
            pltpu.make_async_copy(up.at[:, at], wu_ref.at[slot], w_sem.at[slot, 0]),
            pltpu.make_async_copy(down.at[at], wd_ref.at[slot], w_sem.at[slot, 1]),
        )

    def fetch_start(j, slot):
        @pl.when(j < half)
        def _():
            for copy in fetch(j, up_own, down_own, slot):
                copy.start()

        @pl.when(j >= half)
        def _():
            for copy in fetch(j, up_oth, down_oth, slot):
                copy.start()

    fetch_start(0, 0)
    gain = gain_ref[...].astype(F32)
    xhat, _ = norm_parts(h_ref[...])
    a2 = (xhat * gain + shift_ref[...].astype(F32)).astype(BF16)
    a2_ref[...] = a2
    a2t_ref[...] = a2.T
    gt_ref[...] = g_ref[...].T
    acc_ref[...] = jnp.zeros_like(acc_ref)
    da2_ref[...] = jnp.zeros_like(da2_ref)

    def grad_copies(j, slot):
        return (
            pltpu.make_async_copy(grad_ref.at[slot, :, core], keep_ref.at[j], k_sem.at[slot]),
            remote(grad_ref.at[slot, :, 1 - core], recv_ref.at[j], s_sem.at[slot], r_sem.at[j], other),
        )

    def step(j, _):
        slot = j % 2
        for copy in fetch(j, up_own, down_own, slot):
            copy.wait()

        @pl.when(j + 1 < blocks)
        def _():
            fetch_start(j + 1, 1 - slot)

        wu, wd = wu_ref[slot], wd_ref[slot]
        u = dot_nn(a2_ref[...], wu) + ub_ref[pl.ds(j, 1)]
        cube = 0.044715 * u * u * u
        tanh = jnp.tanh(0.7978845608028654 * (u + cube))
        hidden = (0.5 * u * (1.0 + tanh)).astype(BF16)
        slope = 0.5 * (1.0 + tanh) + 0.5 * u * (1.0 - tanh * tanh) * (
            0.7978845608028654 * (1.0 + 3.0 * 0.044715 * u * u)
        )
        acc_ref[...] += dot_nn(hidden, wd)
        du = (dot_nt(g_ref[...], wd) * slope).astype(BF16)
        where_side = jnp.where(j < half, side, 1 - side)
        usum_ref[pl.ds(where_side * half + j % half, 1)] = jnp.sum(du.astype(F32), axis=0, keepdims=True)
        da2_ref[...] += dot_nt(du, wu)

        @pl.when(j >= 2)
        def _():
            local, far = grad_copies(j - 2, slot)
            local.wait()
            far.wait_send()

        grad_ref[slot, :, :, :, pl.ds(0, hb)] = dot_nn(a2t_ref[...], du).astype(BF16).reshape(8, 2, 64, hb)
        grad_ref[slot, :, :, :, pl.ds(hb, hb)] = dot_nn(gt_ref[...], hidden).astype(BF16).reshape(8, 2, 64, hb)
        for copy in grad_copies(j, slot):
            copy.start()
        return 0

    lax.fori_loop(0, blocks, step, 0)

    piece = rows // 4
    sums = [jnp.zeros((1, width), F32) for _ in range(4)]
    for b in range(4):
        at = pl.ds(b * piece, piece)
        h = h_ref[at]
        g = g_ref[at].astype(F32)
        out_ref[at] = (h + acc_ref[at] + db_ref[...].astype(F32)).astype(BF16)
        xhat, rstd = norm_parts(h)
        da2 = da2_ref[at]
        e = da2 * gain
        dh = g + rstd * (
            e - jnp.mean(e, axis=-1, keepdims=True) - xhat * jnp.mean(e * xhat, axis=-1, keepdims=True)
        )
        dh_ref[at] = dh
        for n, term in enumerate((da2 * xhat, da2, dh.astype(BF16).astype(F32), g)):
            sums[n] = sums[n] + jnp.sum(term, axis=0, keepdims=True)
    vec_ref[...] = jnp.concatenate(sums + [jnp.zeros((4, width), F32)], axis=0)

    for j in (blocks - 2, blocks - 1):
        local, far = grad_copies(j, j % 2)
        local.wait()
        far.wait_send()
    for j in range(blocks):
        grad_copies(j, j % 2)[1].wait_recv()


def feed_call(h, g, gain, shift, db, ub, up_own, down_own, up_oth, down_oth):
    rows, width = h.shape
    hb = HIDDEN_BLOCK
    blocks = 2 * up_own.shape[1] // hb
    vm = pl.BlockSpec(memory_space=pltpu.VMEM)
    hbm = pl.BlockSpec(memory_space=pltpu.HBM)
    sem = pltpu.SemaphoreType.DMA
    grads = jax.ShapeDtypeStruct((blocks, 8, width // 16, 2 * hb), BF16)
    return pl.pallas_call(
        feed_kernel,
        out_shape=(
            jax.ShapeDtypeStruct((rows, width), BF16),
            jax.ShapeDtypeStruct((rows, width), F32),
            jax.ShapeDtypeStruct((8, width), F32),
            jax.ShapeDtypeStruct((blocks, hb), F32),
            grads,
            grads,
        ),
        in_specs=[vm] * 6 + [hbm] * 4,
        out_specs=(vm,) * 4 + (hbm,) * 2,
        scratch_shapes=[
            pltpu.VMEM((rows, width), BF16),
            pltpu.VMEM((width, rows), BF16),
            pltpu.VMEM((width, rows), BF16),
            pltpu.VMEM((rows, width), F32),
            pltpu.VMEM((rows, width), F32),
            pltpu.VMEM((2, width, hb), BF16),
            pltpu.VMEM((2, hb, width), BF16),
            pltpu.VMEM((2, 8, 2, width // 16, 2 * hb), BF16),
            sem((2, 2)), sem((2,)), sem((2,)), sem((blocks,)),
        ],
        compiler_params=pltpu.CompilerParams(
            collective_id=2, has_side_effects=True, vmem_limit_bytes=VMEM_LIMIT
        ),
        name="feed_forward_backward",
    )(h, g, gain, shift, db, ub, up_own, down_own, up_oth, down_oth)


def back_kernel(
    dh_ref, x_ref, gain_ref, qkv_ref, mix_ref, a1_ref, wout_ref, wqkv_ref, segc_ref, segr_ref,
    din_ref, vec_ref, keep_ref, recv_ref,
    dhl_ref, dm_ref, mask_ref, dk_ref, dv_ref, dqkv_ref, acc_ref, send_buf, recv_buf, grad_ref,
    d_send, d_recv, o_send, o_recv, k_sem, s_sem, r_sem,
):
    rows, width = dh_ref.shape
    seq = 2 * rows
    local = wout_ref.shape[0]
    block = rows // 2
    z, y, core, side = place()
    partner = peer_x()
    other = peer_core()
    own = pl.multiple_of(side * rows, rows)
    scale = HEAD_DIM**-0.5
    greet([partner, other])

    def dh_copy(base, b):
        part = dhl_ref.at[pl.ds(pl.multiple_of(base + b * block, block), block)]
        return remote(part, part, d_send.at[b], d_recv.at[b], partner)

    dhl_ref[pl.ds(own, rows)] = dh_ref[...].astype(BF16)
    for b in (1, 0):
        dh_copy(own, b).start()
    dk_ref[...] = jnp.zeros_like(dk_ref)
    dv_ref[...] = jnp.zeros_like(dv_ref)

    for i in (3, 2, 1, 0):
        lo = i * block
        keys = lo + block
        is_theirs = side == (1 if i < 2 else 0)
        at = pl.ds(lo, block)

        @pl.when(is_theirs)
        def _():
            dh_copy((1 - side) * rows, i % 2).wait_recv()

        dm_ref[...] = dot_nt(dhl_ref[at], wout_ref[...]).astype(BF16)
        same = segc_ref[pl.ds(0, keys)] == segr_ref[:, at]
        k_pos = lax.broadcasted_iota(jnp.int32, (keys, block), 0)
        q_pos = lo + lax.broadcasted_iota(jnp.int32, (keys, block), 1)
        mask_ref[pl.ds(0, keys)] = jnp.where(same & (q_pos >= k_pos), 0.0, -1e30)

        def pair(hp, _):
            base = pl.multiple_of(hp * 2 * HEAD_DIM, 2 * HEAD_DIM)
            cols = pl.ds(base, 2 * HEAD_DIM)
            q2 = qkv_ref[at, cols]
            k2 = qkv_ref[pl.ds(0, keys), pl.ds(pl.multiple_of(local + base, 128), 2 * HEAD_DIM)]
            v2 = qkv_ref[pl.ds(0, keys), pl.ds(pl.multiple_of(2 * local + base, 128), 2 * HEAD_DIM)]
            g2 = dm_ref[:, cols]
            dq = jnp.zeros((block, 2 * HEAD_DIM), F32)
            dk = jnp.zeros((keys, 2 * HEAD_DIM), F32)
            dv = jnp.zeros((keys, 2 * HEAD_DIM), F32)
            for h in range(2):
                qh = only_head(q2, h)
                gh = only_head(g2, h)
                scores = dot_nt(k2, qh) * scale + mask_ref[pl.ds(0, keys)]
                weights = jnp.exp(scores - jnp.max(scores, axis=0, keepdims=True))
                probs = weights * (1.0 / jnp.sum(weights, axis=0, keepdims=True))
                dprob = dot_nt(v2, gh)
                row_dot = jnp.sum(probs * dprob, axis=0, keepdims=True)
                dscore = (probs * (dprob - row_dot)).astype(BF16)
                dv += dot_nn(probs.astype(BF16), gh)
                dk += dot_nn(dscore, qh)
                dq += dot_tn(dscore, only_head(k2, h))
            dqkv_ref[at, cols] = (dq * scale).astype(BF16)
            dk_ref[pl.ds(0, keys), cols] += dk
            dv_ref[pl.ds(0, keys), cols] += dv
            return 0

        lax.fori_loop(0, local // (2 * HEAD_DIM), pair, 0)
        dqkv_ref[at, pl.ds(local, local)] = (dk_ref[at] * scale).astype(BF16)
        dqkv_ref[at, pl.ds(2 * local, local)] = dv_ref[at].astype(BF16)
        product = dot_nt(dqkv_ref[at], wqkv_ref[...])

        @pl.when(is_theirs)
        def _():
            send_buf[i % 2] = product.astype(BF16)
            remote(send_buf.at[i % 2], recv_buf.at[i % 2], o_send.at[i % 2], o_recv.at[i % 2], partner).start()

        @pl.when(jnp.logical_not(is_theirs))
        def _():
            acc_ref[pl.ds((i % 2) * block, block)] = product

    def grad_copies(j):
        return (
            pltpu.make_async_copy(grad_ref.at[j, :, core], keep_ref.at[j], k_sem.at[j]),
            remote(grad_ref.at[j, :, 1 - core], recv_ref.at[j], s_sem.at[j], r_sem.at[j], other),
        )

    for part in range(4):
        if part < 3:
            grad = dot_tn(a1_ref[...], dqkv_ref[:, pl.ds(part * local, local)])
        else:
            grad = dot_tn(dhl_ref[...], mix_ref[...])
        grad_ref[part // 2, :, :, :, pl.ds((part % 2) * local, local)] = grad.astype(BF16).reshape(8, 2, 64, local)
        if part % 2 == 1:
            for copy in grad_copies(part // 2):
                copy.start()

    gain = gain_ref[...].astype(F32)
    gain_sum = jnp.zeros((1, width), F32)
    shift_sum = jnp.zeros((1, width), F32)
    for j in (1, 0):
        at = pl.ds(j * block, block)
        remote(send_buf.at[j], recv_buf.at[j], o_send.at[j], o_recv.at[j], partner).wait()
        da1 = acc_ref[at] + recv_buf[j].astype(F32)
        xhat, rstd = norm_parts(x_ref[at].astype(F32))
        e = da1 * gain
        din_ref[at] = dh_ref[at] + rstd * (
            e - jnp.mean(e, axis=-1, keepdims=True) - xhat * jnp.mean(e * xhat, axis=-1, keepdims=True)
        )
        gain_sum = gain_sum + jnp.sum(da1 * xhat, axis=0, keepdims=True)
        shift_sum = shift_sum + jnp.sum(da1, axis=0, keepdims=True)
    vec_ref[...] = jnp.zeros_like(vec_ref)
    vec_ref[pl.ds(0, 1)] = gain_sum
    vec_ref[pl.ds(1, 1)] = shift_sum
    q_sum = jnp.sum(dqkv_ref[:, pl.ds(0, local)].astype(F32), axis=0, keepdims=True)
    v_sum = jnp.sum(dqkv_ref[:, pl.ds(2 * local, local)].astype(F32), axis=0, keepdims=True)
    cols = pl.ds(pl.multiple_of(side * local, local), local)
    vec_ref[pl.ds(2, 1), cols] = q_sum
    vec_ref[pl.ds(3, 1), cols] = v_sum

    for b in range(2):
        dh_copy(own, b).wait_send()
    for j in range(2):
        near, far = grad_copies(j)
        near.wait()
        far.wait()


def back_call(dh, x, gain, qkv, mix, a1, wout, wqkv, segc, segr):
    rows, width = dh.shape
    seq = 2 * rows
    local = wout.shape[0]
    block = rows // 2
    vm = pl.BlockSpec(memory_space=pltpu.VMEM)
    hbm = pl.BlockSpec(memory_space=pltpu.HBM)
    sem = pltpu.SemaphoreType.DMA
    grads = jax.ShapeDtypeStruct((2, 8, width // 16, 2 * local), BF16)
    return pl.pallas_call(
        back_kernel,
        out_shape=(
            jax.ShapeDtypeStruct((rows, width), F32),
            jax.ShapeDtypeStruct((8, width), F32),
            grads,
            grads,
        ),
        in_specs=[vm] * 10,
        out_specs=(vm,) * 2 + (hbm,) * 2,
        scratch_shapes=[
            pltpu.VMEM((seq, width), BF16),
            pltpu.VMEM((block, local), BF16),
            pltpu.VMEM((seq, block), F32),
            pltpu.VMEM((seq, local), F32),
            pltpu.VMEM((seq, local), F32),
            pltpu.VMEM((seq, 3 * local), BF16),
            pltpu.VMEM((rows, width), F32),
            pltpu.VMEM((2, block, width), BF16),
            pltpu.VMEM((2, block, width), BF16),
            pltpu.VMEM((2, 8, 2, width // 16, 2 * local), BF16),
            sem((2,)), sem((2,)), sem((2,)), sem((2,)), sem((2,)), sem((2,)), sem((2,)),
        ],
        compiler_params=pltpu.CompilerParams(
            collective_id=3, has_side_effects=True, vmem_limit_bytes=VMEM_LIMIT
        ),
        name="attend_backward",
    )(dh, x, gain, qkv, mix, a1, wout, wqkv, segc, segr)


def scatter_kernel(n_own, n_other, with_vec, *refs):
    refs = list(refs)
    keep_ref, recv_ref = refs[:2]
    refs = refs[2:]
    if with_vec:
        vec_in = refs.pop(0)
        out_ref, vec_out = refs[:2]
        refs = refs[2:]
    else:
        out_ref = refs.pop(0)
    (keep_v, recv_v, sum_ref, ybuf, part_ref, zbuf, fin_ref, l_sem, y_s, y_r, z_s, z_r) = refs[:12]
    refs = refs[12:]
    if n_other:
        xsend, xbuf, x_s, x_r = refs[:4]
        refs = refs[4:]
    if with_vec:
        vsum, vrecv, v_s, v_r = refs
    z, y, core, side = place()
    nb = n_own + n_other
    need_x = n_other > 0 or with_vec
    greet(
        [peer_y()] + [peer_z(k) for k in (1, 2, 3)] + ([peer_x()] if need_x else [])
        + ([peer_core()] if with_vec else [])
    )

    def loads(b):
        slot = b % 2
        return (
            pltpu.make_async_copy(keep_ref.at[b], keep_v.at[slot], l_sem.at[slot, 0]),
            pltpu.make_async_copy(recv_ref.at[b], recv_v.at[slot], l_sem.at[slot, 1]),
        )

    def y_copy(b):
        return remote(sum_ref.at[b, :, 1 - y], ybuf.at[b], y_s.at[b], y_r.at[b], peer_y())

    def z_copy(b, k):
        return remote(
            part_ref.at[b, (z + k) % 4], zbuf.at[b, k - 1], z_s.at[b, k - 1], z_r.at[b, k - 1], peer_z(k)
        )

    def x_copy(b):
        return remote(xsend.at[b], xbuf.at[b], x_s.at[b], x_r.at[b], peer_x())

    def first(b):
        for copy in loads(b):
            copy.wait()
        total = keep_v[b % 2].astype(F32) + recv_v[b % 2].astype(F32)
        sum_ref[b] = total.astype(BF16).reshape(sum_ref.shape[1:])
        y_copy(b).start()
        if b + 2 < nb:
            for copy in loads(b + 2):
                copy.start()

    def second(b):
        y_copy(b).wait_recv()
        part_ref[b] = (sum_ref[b, :, y].astype(F32) + ybuf[b].astype(F32)).astype(BF16)
        for k in (2, 1, 3):
            z_copy(b, k).start()

    def third(b):
        for k in (1, 2, 3):
            z_copy(b, k).wait_recv()
        total = part_ref[b, z].astype(F32)
        for k in (1, 2, 3):
            total = total + zbuf[b, k - 1].astype(F32)
        if b < n_own:
            fin_ref[b] = total
        else:
            xsend[b - n_own] = total.astype(BF16)
            x_copy(b - n_own).start()

    def last(b):
        total = fin_ref[b]
        if n_other:
            x_copy(b).wait_recv()
            total = total + xbuf[b].astype(F32)
        out_ref[b] = total

    for b in range(min(2, nb)):
        for copy in loads(b):
            copy.start()

    if with_vec:
        count = vec_in.shape[0]

        def v_copy(n, peer, slot):
            return remote(vsum.at[n], vrecv.at[slot], v_s.at[slot], v_r.at[slot], peer)

        def z_vec(k):
            return remote(vsum.at[2], vrecv.at[2 + z], v_s.at[2 + k], v_r.at[2 + z], peer_z(k))

        def z_vec_from(zz, k):
            return remote(vsum.at[2], vrecv.at[2 + zz], v_s.at[2 + k], v_r.at[2 + zz], peer_z(k))

        def vec_step(n):
            if n == 0:
                vsum[0] = vec_in[...]
                v_copy(0, peer_core(), 0).start()
            elif n == 1:
                v_copy(0, peer_core(), 0).wait()
                vsum[1] = vsum[0] + vrecv[0]
                v_copy(1, peer_y(), 1).start()
            elif n == 2:
                v_copy(1, peer_y(), 1).wait()
                vsum[2] = vsum[1] + vrecv[1]
                for k in (1, 2, 3):
                    z_vec(k).start()
            elif n == 3:
                for k in (1, 2, 3):
                    z_vec(k).wait_send()
                    z_vec_from((z + k) % 4, k).wait_recv()
                vrecv[2 + z] = vsum[2]
                vsum[3] = (vrecv[2] + vrecv[3]) + (vrecv[4] + vrecv[5])
                v_copy(3, peer_x(), 6).start()
            elif n == 4:
                v_copy(3, peer_x(), 6).wait()
                vec_out[...] = vsum[3] + vrecv[6]
    else:

        def vec_step(n):
            pass

    for n in range(max(nb + 3, 5)):
        if n < nb:
            first(n)
        vec_step(n)
        if 0 <= n - 1 < nb:
            second(n - 1)
        if 0 <= n - 2 < nb:
            third(n - 2)
        if n - 3 >= 0 and n_other and n_own <= n - 3 < nb:
            last(n - 3 - n_own)
        if not n_other and 0 <= n - 3 < nb:
            last(n - 3)
    for b in range(nb):
        y_copy(b).wait_send()
        for k in (1, 2, 3):
            z_copy(b, k).wait_send()
    for b in range(n_other):
        x_copy(b).wait_send()


def scatter_call(keep, recv, n_own, n_other, vec, cid):
    nb, chunks, height, cols = keep.shape
    vm = pl.BlockSpec(memory_space=pltpu.VMEM)
    hbm = pl.BlockSpec(memory_space=pltpu.HBM)
    sem = pltpu.SemaphoreType.DMA
    with_vec = vec is not None
    out_shape = [jax.ShapeDtypeStruct((n_own, height, cols), F32)]
    in_specs = [hbm, hbm]
    args = [keep, recv]
    scratch = [
        pltpu.VMEM((2, chunks, height, cols), BF16),
        pltpu.VMEM((2, chunks, height, cols), BF16),
        pltpu.VMEM((nb, 4, 2, height, cols), BF16),
        pltpu.VMEM((nb, 4, height, cols), BF16),
        pltpu.VMEM((nb, 4, height, cols), BF16),
        pltpu.VMEM((nb, 3, height, cols), BF16),
        pltpu.VMEM((n_own, height, cols), F32),
        sem((2, 2)), sem((nb,)), sem((nb,)), sem((nb, 3)), sem((nb, 3)),
    ]
    if n_other:
        scratch += [
            pltpu.VMEM((n_other, height, cols), BF16),
            pltpu.VMEM((n_other, height, cols), BF16),
            sem((n_other,)), sem((n_other,)),
        ]
    if with_vec:
        out_shape.append(jax.ShapeDtypeStruct(vec.shape, F32))
        in_specs.append(vm)
        args.append(vec)
        scratch += [pltpu.VMEM((4,) + vec.shape, F32), pltpu.VMEM((7,) + vec.shape, F32), sem((7,)), sem((7,))]
    return pl.pallas_call(
        functools.partial(scatter_kernel, n_own, n_other, with_vec),
        out_shape=tuple(out_shape),
        in_specs=in_specs,
        out_specs=(vm,) * len(out_shape),
        scratch_shapes=scratch,
        compiler_params=pltpu.CompilerParams(
            collective_id=cid, has_side_effects=True, vmem_limit_bytes=VMEM_LIMIT
        ),
        name="scatter_grads",
    )(*args)


def on_device_pair(
    inputs, segment_ids, first_gain, first_shift, qkv_weight, qv_bias, out_weight, out_bias,
    second_gain, second_shift, up_weight, up_bias, down_weight, down_bias, cotangent,
):
    rows, _, width = inputs.shape
    seq = segment_ids.shape[0]
    local = out_weight.shape[0]
    hidden = up_weight.shape[1]
    side = lax.axis_index("tensor")
    x = inputs.reshape(rows, width)
    g = cotangent.reshape(rows, width)
    segc = segment_ids.reshape(seq, 1)
    segr = segment_ids.reshape(1, seq)
    row = lambda v: v.reshape(1, width)
    wqkv = qkv_weight.reshape(width, 3 * local)
    zero = jnp.zeros((local,), F32)
    bias = jnp.concatenate([qv_bias[0].astype(F32), zero, qv_bias[1].astype(F32)]).reshape(1, 3 * local)

    up_oth, down_oth, ub_oth = gather_call(up_weight, down_weight, up_bias.reshape(16, hidden // 16))
    ub = jnp.concatenate([up_bias, ub_oth.reshape(hidden)]).astype(F32).reshape(-1, HIDDEN_BLOCK)
    a1, qkv, mix, h = attend_call(
        x, row(first_gain), row(first_shift), wqkv, bias, segc, segr, out_weight, row(out_bias)
    )
    layer_output, dh, vec_b, up_sums, keep_m, recv_m = feed_call(
        h, g, row(second_gain), row(second_shift), row(down_bias), ub, up_weight, down_weight, up_oth, down_oth
    )
    half = hidden // HIDDEN_BLOCK
    (mlp,) = scatter_call(keep_m, recv_m, half, half, None, 4)
    input_grad, vec_c, keep_a, recv_a = back_call(
        dh, x, row(first_gain), qkv, mix, a1, out_weight, wqkv, segc, segr
    )
    vec = jnp.concatenate([vec_b, vec_c, up_sums.reshape(-1, width), jnp.zeros((4, width), F32)], axis=0)
    attn, total = scatter_call(keep_a, recv_a, 2, 0, vec, 5)

    height = width // 16
    up_share = jnp.transpose(mlp[:, :, :HIDDEN_BLOCK], (1, 0, 2)).reshape(height, hidden)
    down_share = jnp.transpose(mlp[:, :, HIDDEN_BLOCK:], (0, 2, 1)).reshape(hidden, height)
    qkv_share = jnp.concatenate([attn[0], attn[1][:, :local]], axis=1).reshape(height, 3, local)
    out_share = attn[1][:, local:].T
    qv_share = lax.dynamic_slice_in_dim(total[10:12], side * local, local, 1)
    up_bias_share = lax.dynamic_slice_in_dim(total[16:20].reshape(2 * hidden), side * hidden, hidden, 0)
    return (
        layer_output.reshape(rows, 1, width),
        input_grad.reshape(rows, 1, width),
        total[8],
        total[9],
        qkv_share,
        qv_share,
        out_share,
        total[2],
        total[0],
        total[1],
        up_share,
        up_bias_share,
        down_share,
        total[3],
    )


def solution(mesh):
    in_specs = (
        P("tensor", "dp", None),
        P(None, "dp"),
        P(),
        P(),
        P(None, None, "tensor"),
        P(None, "tensor"),
        P("tensor", None),
        P(),
        P(),
        P(),
        P(None, "tensor"),
        P("tensor"),
        P("tensor", None),
        P(),
        P("tensor", "dp", None),
    )
    out_specs = (
        P("tensor", "dp", None),
        P("tensor", "dp", None),
        P(),
        P(),
        P("dp", None, "tensor"),
        P(None, "tensor"),
        P("tensor", "dp"),
        P(),
        P(),
        P(),
        P("dp", "tensor"),
        P("tensor"),
        P("tensor", "dp"),
        P(),
    )
    pair = mesh.shape["tensor"] == 2 and mesh.shape["dp"] == Z_SIZE * Y_SIZE * CORES
    return jax.shard_map(
        on_device_pair if pair else on_device, mesh=mesh, in_specs=in_specs, out_specs=out_specs, check_vma=False
    )
```

```python
import functools

import jax
import jax.numpy as jnp
from jax import lax
from jax.experimental import pallas as pl
from jax.experimental.pallas import tpu as pltpu
from jax.sharding import PartitionSpec as P

HEAD_DIM = 64
MESH = pl.DeviceIdType.MESH
F32 = jnp.float32
BF16 = jnp.bfloat16
VMEM_LIMIT = 63 << 20


norm_eps = 1e-05


def layer_norm(value, gain, shift):
    row_mean = jnp.mean(value, axis=-1, keepdims=True)
    centred = value - row_mean
    variance = jnp.mean(centred * centred, axis=-1, keepdims=True)
    return centred * lax.rsqrt(variance + norm_eps) * gain + shift


def gelu_tanh(value):
    return (
        0.5
        * value
        * (1.0 + jnp.tanh(0.7978845608028654 * (value + 0.044715 * value * value * value)))
    )


def masked_scores(query_block, keys_all, seg_block, seg_all, row_start, block_rows, score_scale):
    scores = (
        jnp.einsum("qhd,khd->hqk", query_block, keys_all, preferred_element_type=jnp.float32)
        * score_scale
    )
    key_pos = jnp.arange(keys_all.shape[0], dtype=jnp.int32)
    query_pos = row_start + jnp.arange(block_rows, dtype=jnp.int32)
    allowed = (seg_block[:, None] == seg_all[None, :]) & (query_pos[:, None] >= key_pos[None, :])
    return jnp.where(allowed[None], scores, -1e30)


def attend_forward(queries, keys_all, values_all, seg_all, score_scale):
    seq_len = queries.shape[0]
    block_rows = min(512, seq_len)

    def one_block(block_index):
        row_start = block_index * block_rows
        query_block = lax.dynamic_slice_in_dim(queries, row_start, block_rows, 0)
        seg_block = lax.dynamic_slice_in_dim(seg_all, row_start, block_rows, 0)
        scores = masked_scores(
            query_block, keys_all, seg_block, seg_all, row_start, block_rows, score_scale
        )
        row_top = jnp.max(scores, axis=-1, keepdims=True)
        weights = jnp.exp(scores - row_top)
        row_total = jnp.sum(weights, axis=-1, keepdims=True)
        probs_low = (weights / row_total).astype(jnp.bfloat16)
        mixed = jnp.einsum(
            "hqk,khd->qhd", probs_low, values_all, preferred_element_type=jnp.float32
        )
        return (mixed, row_top + jnp.log(row_total))

    mixed, log_total = lax.map(one_block, jnp.arange(seq_len // block_rows, dtype=jnp.int32))
    return (mixed.reshape(seq_len, -1), log_total)


def attend_backward(queries, keys_all, values_all, seg_all, log_total, out_grad, score_scale):
    seq_len = queries.shape[0]
    block_rows = min(512, seq_len)

    def one_block(carry, block_index):
        key_grad, value_grad = carry
        row_start = block_index * block_rows
        query_block = lax.dynamic_slice_in_dim(queries, row_start, block_rows, 0)
        seg_block = lax.dynamic_slice_in_dim(seg_all, row_start, block_rows, 0)
        grad_block = lax.dynamic_slice_in_dim(out_grad, row_start, block_rows, 0)
        scores = masked_scores(
            query_block, keys_all, seg_block, seg_all, row_start, block_rows, score_scale
        )
        probs = jnp.exp(scores - log_total[block_index])
        probs_low = probs.astype(jnp.bfloat16)
        value_grad = value_grad + jnp.einsum(
            "hqk,qhd->khd", probs_low, grad_block, preferred_element_type=jnp.float32
        )
        prob_grad = jnp.einsum(
            "qhd,khd->hqk", grad_block, values_all, preferred_element_type=jnp.float32
        )
        row_dot = jnp.sum(probs * prob_grad, axis=-1, keepdims=True)
        score_grad = (probs * (prob_grad - row_dot)).astype(jnp.bfloat16)
        query_grad = (
            jnp.einsum("hqk,khd->qhd", score_grad, keys_all, preferred_element_type=jnp.float32)
            * score_scale
        )
        key_grad = (
            key_grad
            + jnp.einsum(
                "hqk,qhd->khd", score_grad, query_block, preferred_element_type=jnp.float32
            )
            * score_scale
        )
        return ((key_grad, value_grad), query_grad)

    zero_grads = jnp.zeros(keys_all.shape, jnp.float32)
    (key_grad, value_grad), query_grad = lax.scan(
        one_block, (zero_grads, zero_grads), jnp.arange(seq_len // block_rows, dtype=jnp.int32)
    )
    return (
        query_grad.reshape(seq_len, -1),
        key_grad.reshape(seq_len, -1),
        value_grad.reshape(seq_len, -1),
    )


def row_product(left, right, contract):
    return lax.dot_general(
        left, right, (((1,), (contract,)), ((), ())), preferred_element_type=jnp.float32
    )


def rows_contract(left, right):
    return lax.dot_general(
        left, right, (((0,), (0,)), ((), ())), preferred_element_type=jnp.float32
    )


def on_device(
    inputs,
    segment_ids,
    first_gain,
    first_shift,
    qkv_weight,
    qv_bias,
    out_weight,
    out_bias,
    second_gain,
    second_shift,
    up_weight,
    up_bias,
    down_weight,
    down_bias,
    cotangent,
):
    rows_dev, seq_count, model_width = inputs.shape
    tensor_count = lax.axis_size("tensor")
    tensor_rank = lax.axis_index("tensor")
    seq_len = rows_dev * tensor_count
    local_width = out_weight.shape[0]
    heads_dev = local_width // HEAD_DIM
    hidden_dev = up_weight.shape[1]
    local_rows = rows_dev * seq_count
    score_scale = HEAD_DIM ** (-0.5)
    residual_in = inputs.reshape(local_rows, model_width).astype(jnp.float32)
    gain_one = first_gain.astype(jnp.float32)
    shift_one = first_shift.astype(jnp.float32)
    gain_two = second_gain.astype(jnp.float32)
    shift_two = second_shift.astype(jnp.float32)
    normed_one, pull_one = jax.vjp(layer_norm, residual_in, gain_one, shift_one)
    first_local = normed_one.astype(jnp.bfloat16)
    first_rows = lax.all_gather(first_local, "tensor", axis=0, tiled=True)
    qkv_flat = qkv_weight.reshape(model_width, 3 * local_width)
    qkv_bias = jnp.concatenate(
        [
            qv_bias[0].astype(jnp.float32),
            jnp.zeros((local_width,), jnp.float32),
            qv_bias[1].astype(jnp.float32),
        ]
    )
    qkv_low = (jnp.dot(first_rows, qkv_flat, preferred_element_type=jnp.float32) + qkv_bias).astype(
        jnp.bfloat16
    )
    qkv_split = qkv_low.reshape(seq_len, seq_count, 3, heads_dev, HEAD_DIM)
    seq_index = 0
    mixed_one, log_one = attend_forward(
        qkv_split[:, seq_index, 0],
        qkv_split[:, seq_index, 1],
        qkv_split[:, seq_index, 2],
        segment_ids[:, seq_index],
        score_scale,
    )
    mixed_list = [mixed_one]
    log_list = [log_one]
    mixed_low = (
        jnp.stack(mixed_list, axis=1).reshape(seq_len * seq_count, local_width).astype(jnp.bfloat16)
    )
    attn_local = lax.psum_scatter(
        row_product(mixed_low, out_weight, 0), "tensor", scatter_dimension=0, tiled=True
    )
    residual_mid = residual_in + attn_local + out_bias.astype(jnp.float32)
    normed_two, pull_two = jax.vjp(layer_norm, residual_mid, gain_two, shift_two)
    second_local = normed_two.astype(jnp.bfloat16)
    second_rows = lax.all_gather(second_local, "tensor", axis=0, tiled=True)
    hidden_pre = jnp.dot(
        second_rows, up_weight, preferred_element_type=jnp.float32
    ) + up_bias.astype(jnp.float32)
    activated, pull_gelu = jax.vjp(gelu_tanh, hidden_pre)
    hidden_low = activated.astype(jnp.bfloat16)
    mlp_local = lax.psum_scatter(
        row_product(hidden_low, down_weight, 0).astype(jnp.bfloat16),
        "tensor",
        scatter_dimension=0,
        tiled=True,
    ).astype(jnp.float32)
    layer_output = (residual_mid + mlp_local + down_bias.astype(jnp.float32)).astype(jnp.bfloat16)
    layer_output = layer_output.reshape(rows_dev, seq_count, model_width)
    grad_local = cotangent.reshape(local_rows, model_width)
    grad_rows = lax.all_gather(grad_local, "tensor", axis=0, tiled=True)
    down_grad = rows_contract(hidden_low, grad_rows)
    hidden_grad = lax.dot_general(
        grad_rows, down_weight, (((1,), (1,)), ((), ())), preferred_element_type=jnp.float32
    )
    (pre_grad,) = pull_gelu(hidden_grad)
    pre_low = pre_grad.astype(jnp.bfloat16)
    up_sums = jnp.sum(pre_low, axis=0, dtype=jnp.float32)
    second_back = lax.all_gather(second_local, "tensor", axis=0, tiled=True)
    up_grad = rows_contract(second_back, pre_low)
    second_norm_grad = lax.psum_scatter(
        row_product(pre_low, up_weight, 1), "tensor", scatter_dimension=0, tiled=True
    )
    mid_from_norm, gain_two_grad, shift_two_grad = pull_two(second_norm_grad)
    residual_grad = grad_local.astype(jnp.float32) + mid_from_norm
    residual_low = residual_grad.astype(jnp.bfloat16)
    residual_rows = lax.all_gather(residual_low, "tensor", axis=0, tiled=True)
    out_grad_weight = rows_contract(mixed_low, residual_rows)
    mixed_grad = lax.dot_general(
        residual_rows, out_weight, (((1,), (1,)), ((), ())), preferred_element_type=jnp.float32
    ).astype(jnp.bfloat16)
    mixed_grad = mixed_grad.reshape(seq_len, seq_count, heads_dev, HEAD_DIM)
    seq_index = 0
    query_grad, key_grad, value_grad = attend_backward(
        qkv_split[:, seq_index, 0],
        qkv_split[:, seq_index, 1],
        qkv_split[:, seq_index, 2],
        segment_ids[:, seq_index],
        log_list[seq_index],
        mixed_grad[:, seq_index],
        score_scale,
    )
    query_list = [query_grad]
    key_list = [key_grad]
    value_list = [value_grad]
    qkv_grad = jnp.concatenate(
        [jnp.stack(query_list, axis=1), jnp.stack(key_list, axis=1), jnp.stack(value_list, axis=1)],
        axis=-1,
    )
    qkv_grad_low = qkv_grad.reshape(seq_len * seq_count, 3 * local_width).astype(jnp.bfloat16)
    qkv_sums = jnp.sum(qkv_grad_low, axis=0, dtype=jnp.float32)
    qv_sums = jnp.stack([qkv_sums[:local_width], qkv_sums[2 * local_width :]], axis=0)
    first_back = lax.all_gather(first_local, "tensor", axis=0, tiled=True)
    qkv_grad_weight = rows_contract(first_back, qkv_grad_low).reshape(model_width, 3, local_width)
    first_norm_grad = lax.psum_scatter(
        row_product(qkv_grad_low, qkv_flat, 1), "tensor", scatter_dimension=0, tiled=True
    )
    in_from_norm, gain_one_grad, shift_one_grad = pull_one(first_norm_grad)
    input_grad = (residual_grad + in_from_norm).reshape(rows_dev, seq_count, model_width)
    qkv_share, out_share, up_share, down_share = (
        lax.psum_scatter(qkv_grad_weight, "dp", scatter_dimension=0, tiled=True),
        lax.psum_scatter(out_grad_weight, "dp", scatter_dimension=1, tiled=True),
        lax.psum_scatter(up_grad, "dp", scatter_dimension=0, tiled=True),
        lax.psum_scatter(down_grad, "dp", scatter_dimension=1, tiled=True),
    )
    out_bias_part = jnp.sum(residual_low, axis=0, dtype=jnp.float32)
    down_bias_part = jnp.sum(grad_local, axis=0, dtype=jnp.float32)
    stacked = jnp.stack(
        [
            gain_one_grad,
            shift_one_grad,
            gain_two_grad,
            shift_two_grad,
            out_bias_part,
            down_bias_part,
        ],
        axis=0,
    )
    qv_full = lax.dynamic_update_slice(
        jnp.zeros((2, model_width), jnp.float32), qv_sums, (jnp.int32(0), tensor_rank * local_width)
    )
    up_full = lax.dynamic_update_slice(
        jnp.zeros((hidden_dev * tensor_count,), jnp.float32), up_sums, (tensor_rank * hidden_dev,)
    )
    stacked, qv_total, up_total = lax.psum((stacked, qv_full, up_full), ("dp", "tensor"))
    qv_share = lax.dynamic_slice_in_dim(qv_total, tensor_rank * local_width, local_width, 1)
    up_bias_share = lax.dynamic_slice_in_dim(up_total, tensor_rank * hidden_dev, hidden_dev, 0)
    return (
        layer_output,
        input_grad,
        stacked[0],
        stacked[1],
        qkv_share,
        qv_share,
        out_share,
        stacked[4],
        stacked[2],
        stacked[3],
        up_share,
        up_bias_share,
        down_share,
        stacked[5],
    )


Z_SIZE, Y_SIZE, CORES = 4, 2, 2


def place():
    dp = lax.axis_index("dp")
    side = lax.axis_index("tensor")
    return dp // 4, (dp // 2) % 2, dp % 2, side


def dev(z, y, core, side):
    return (z * 4 + y * 2 + core, side)


def peer_x():
    z, y, core, side = place()
    return dev(z, y, core, 1 - side)


def peer_y():
    z, y, core, side = place()
    return dev(z, 1 - y, core, side)


def peer_core():
    z, y, core, side = place()
    return dev(z, y, 1 - core, side)


def peer_z(step):
    z, y, core, side = place()
    return dev((z + step) % 4, y, core, side)


def greet():
    peers = [peer_x(), peer_y(), peer_core()] + [peer_z(k) for k in (1, 2, 3)]
    barrier = pltpu.get_barrier_semaphore()
    for peer in peers:
        pl.semaphore_signal(barrier, inc=1, device_id=peer, device_id_type=MESH)
    pl.semaphore_wait(barrier, len(peers))


def remote(src, dst, send_sem, recv_sem, peer):
    return pltpu.make_async_remote_copy(
        src_ref=src, dst_ref=dst, send_sem=send_sem, recv_sem=recv_sem, device_id=peer, device_id_type=MESH
    )


def dot_nn(a, b):
    return lax.dot_general(a, b, (((1,), (0,)), ((), ())), preferred_element_type=F32)


def dot_nt(a, b):
    return lax.dot_general(a, b, (((1,), (1,)), ((), ())), preferred_element_type=F32)


def dot_tn(a, b):
    return lax.dot_general(a, b, (((0,), (0,)), ((), ())), preferred_element_type=F32)


def norm_parts(value):
    mean = jnp.mean(value, axis=-1, keepdims=True)
    centred = value - mean
    rstd = lax.rsqrt(jnp.mean(centred * centred, axis=-1, keepdims=True) + norm_eps)
    return centred * rstd, rstd


def norm_back(grad, gain, xhat, rstd):
    e = grad * gain
    return rstd * (e - jnp.mean(e, axis=-1, keepdims=True) - xhat * jnp.mean(e * xhat, axis=-1, keepdims=True))


def head_lanes(h):
    lane = lax.broadcasted_iota(jnp.int32, (1, 2 * HEAD_DIM), 1)
    return (lane // HEAD_DIM) == h


def only_head(value, h):
    return jnp.where(head_lanes(h), value, jnp.zeros_like(value))


def total_of(row):
    return jnp.sum(row, axis=0, keepdims=True)


GAIN_1, SHIFT_1, OUT_BIAS, GAIN_2, SHIFT_2, DOWN_BIAS = range(6)
PIECES = 16
HIDDEN_BLOCK = 512
GATHERED_AHEAD = 3


def gather(source, target, sems):
    x_s, x_r, z_s, z_r, y_s, y_r, c_s, c_r = sems
    z, y, core, side = place()

    def copies(dp, q, send, recv, peer, views=target):
        pairs = zip(views(dp, q), target(dp, q))
        return [remote(s, d, send.at[a], recv.at[a], peer) for a, (s, d) in enumerate(pairs)]

    def number(zz, yy, cc):
        return zz * 4 + yy * 2 + cc

    def from_z(k):
        return (z + 4 - k) % 4

    def x_copies(q):
        return copies(number(z, y, core), q, x_s.at[q], x_r.at[q], peer_x(), source)

    def z_sends(q, k):
        return copies(number(z, y, core), q, z_s.at[q, k], z_r.at[q, k], peer_z(k))

    def z_recvs(q, k):
        return copies(number(from_z(k), y, core), q, z_s.at[q, k], z_r.at[q, k], peer_z(k))

    def y_copies(q, k, yy):
        return copies(number(from_z(k), yy, core), q, y_s.at[q, k], y_r.at[q, k], peer_y())

    def c_copies(q, k, far, cc):
        yy = (1 - y) if far else y
        slot = 4 * far + k
        return copies(number(from_z(k), yy, cc), q, c_s.at[q, slot], c_r.at[q, slot], peer_core())

    def start(list_of):
        for copy in list_of:
            copy.start()

    def first(q):
        for copy in x_copies(q):
            copy.wait()
        for k in (2, 1, 3):
            start(z_sends(q, k))
        start(y_copies(q, 0, y))
        start(c_copies(q, 0, 0, core))

    def second(q):
        for k in (1, 3, 2):
            for copy in z_recvs(q, k):
                copy.wait_recv()
            start(y_copies(q, k, y))
            start(c_copies(q, k, 0, core))

    def third(q):
        for k in range(4):
            for copy in y_copies(q, k, 1 - y):
                copy.wait_recv()
            start(c_copies(q, k, 1, core))

    def last(q):
        for k in range(4):
            for far in (0, 1):
                for copy in c_copies(q, k, far, 1 - core):
                    copy.wait_recv()

    def sent(q):
        for k in range(4):
            if k > 0:
                for copy in z_sends(q, k):
                    copy.wait_send()
            for copy in y_copies(q, k, y):
                copy.wait_send()
            for far in (0, 1):
                for copy in c_copies(q, k, far, core):
                    copy.wait_send()

    return first, second, third, last, sent, x_copies


def gather_semaphores(q):
    sem = pltpu.SemaphoreType.DMA
    return [sem((q, 2))] * 2 + [sem((q, 4, 2))] * 4 + [sem((q, 8, 2))] * 2


def hidden_views(arrays, dp, b):
    up, down = arrays
    n_up, n_down = up.shape[0] // PIECES, HIDDEN_BLOCK // PIECES
    return [
        up.at[pl.ds(pl.multiple_of(dp * n_up, n_up), n_up), pl.ds(b * HIDDEN_BLOCK, HIDDEN_BLOCK)],
        down.at[pl.ds(pl.multiple_of(b * HIDDEN_BLOCK + dp * n_down, n_down), n_down)],
    ]


def ahead_kernel(
    x_ref, par_ref, wqkv_ref, qvb_ref, seg_ref, wout_ref, wout_hbm, up_ref, down_ref, ub_ref,
    a1_ref, qkv_ref, mix_ref, mixt_ref, lse_ref, h_ref, woutt_ref, up_o, down_o, ub_o,
    mask_ref, a_send, a_recv, o_send, o_recv,
    *gather_sems_and_more,
):
    *gather_sems, b_s, b_r = gather_sems_and_more
    rows, width = x_ref.shape
    seq = 2 * rows
    local = wout_ref.shape[0]
    block = rows // 2
    piece = rows // 4
    z, y, core, side = place()
    partner = peer_x()
    own = pl.multiple_of(side * rows, rows)
    theirs = pl.multiple_of((1 - side) * rows, rows)
    greet()

    n_out = local // PIECES
    ours, others = (up_ref, down_ref), (up_o, down_o)

    def views(projection, feed, dp, q):
        if q == 0:
            return [projection.at[pl.ds(pl.multiple_of(dp * n_out, n_out), n_out)]]
        return hidden_views(feed, dp, q - 1)

    first, second, third, last, sent, x_copies = gather(
        lambda dp, q: views(wout_hbm, ours, dp, q), lambda dp, q: views(woutt_ref, others, dp, q), gather_sems
    )
    chunks = 1 + GATHERED_AHEAD

    def run(ticks):
        for stage, q in ticks:
            stage(q)

    early = [(third, 0), (first, 2), (second, 1)]
    middle = [(first, 3), (third, 1), (second, 2)]
    late = [(third, 2), (second, 3)]
    end = [(third, 3)]

    bias_copy = remote(ub_ref, ub_o, b_s, b_r, partner)
    for q in (0, 1):
        for copy in x_copies(q):
            copy.start()

    def a1_copy(base, b):
        part = a1_ref.at[pl.ds(pl.multiple_of(base + b * piece, piece), piece)]
        return remote(part, part, a_send.at[b], a_recv.at[b], partner)

    gain = par_ref[pl.ds(GAIN_1, 1)]
    shift = par_ref[pl.ds(SHIFT_1, 1)]
    for b in range(4):
        xhat, _ = norm_parts(x_ref[pl.ds(b * piece, piece)].astype(F32))
        at = pl.ds(pl.multiple_of(own + b * piece, piece), piece)
        a1_ref[at] = (xhat * gain + shift).astype(BF16)
        a1_copy(own, b).start()
        if b + 2 < chunks:
            for copy in x_copies(b + 2):
                copy.start()
    bias_copy.start()

    def project(base, count):
        at = pl.ds(pl.multiple_of(base, block), count)
        left = a1_ref[at]
        for part in range(3):
            cols = pl.ds(part * local, local)
            value = dot_nn(left, wqkv_ref[:, cols])
            if part != 1:
                value = value + qvb_ref[pl.ds(part // 2, 1)].astype(F32)
            qkv_ref[at, cols] = value.astype(BF16)

    project(own, rows)

    def mix_copy(j):
        at = pl.ds(pl.multiple_of(theirs + j * block, block), block)
        far = mixt_ref.at[pl.ds(j * block, block)]
        return remote(mix_ref.at[at], far, o_send.at[j], o_recv.at[j], partner)

    seg_row = seg_ref[...].astype(F32)
    seg_col = jnp.broadcast_to(seg_row, (8, seq)).T[:, :1]
    run([(first, 0), (first, 1)])

    @pl.when(side == 1)
    def _():
        run([(second, 0)])

    for i in range(4):
        lo = i * block
        keys = lo + block
        is_theirs = side == (1 if i < 2 else 0)
        at = pl.ds(lo, block)
        if i == 1:

            @pl.when(side == 0)
            def _():
                run([(second, 0)])

        @pl.when(is_theirs)
        def _():
            run(middle if i % 2 else early)
            for b in (2 * (i % 2), 2 * (i % 2) + 1):
                a1_copy(theirs, b).wait_recv()
            project(lo, block)

        same = seg_col[:keys] == seg_row[:, lo : lo + block]
        k_pos = lax.broadcasted_iota(jnp.int32, (keys, block), 0)
        q_pos = lo + lax.broadcasted_iota(jnp.int32, (keys, block), 1)
        mask_ref[pl.ds(0, keys)] = jnp.where(same & (q_pos >= k_pos), 0.0, -1e30)

        def pair(hp, _):
            base = pl.multiple_of(hp * 2 * HEAD_DIM, 2 * HEAD_DIM)
            cols = pl.ds(base, 2 * HEAD_DIM)
            q2 = qkv_ref[at, cols]
            k2 = qkv_ref[pl.ds(0, keys), pl.ds(pl.multiple_of(local + base, 128), 2 * HEAD_DIM)]
            v2 = qkv_ref[pl.ds(0, keys), pl.ds(pl.multiple_of(2 * local + base, 128), 2 * HEAD_DIM)]
            out = jnp.zeros((block, 2 * HEAD_DIM), F32)
            for h in range(2):
                scores = dot_nt(k2, only_head(q2, h)) * HEAD_DIM**-0.5 + mask_ref[pl.ds(0, keys)]
                top = jnp.max(scores, axis=0, keepdims=True)
                weights = jnp.exp(scores - top)
                total = total_of(weights)
                lse_ref[pl.ds(2 * hp + h, 1), at] = top + jnp.log(total)
                out += dot_tn((weights * (1.0 / total)).astype(BF16), only_head(v2, h))
            mix_ref[at, cols] = out.astype(BF16)
            return 0

        lax.fori_loop(0, local // (2 * HEAD_DIM), pair, 0)

        @pl.when(is_theirs)
        def _():
            mix_copy(i % 2).start()
            if i % 2:
                run(late)

    run(end)
    last(0)
    for j in range(2):
        at = pl.ds(j * block, block)
        mix_copy(j).wait_recv()
        h_ref[at] = (
            x_ref[at].astype(F32)
            + (dot_nn(mix_ref[pl.ds(pl.multiple_of(own + j * block, block), block)], wout_ref[...]) + dot_nn(mixt_ref[at], woutt_ref[...]))
            + par_ref[pl.ds(OUT_BIAS, 1)]
        )

    for j in range(2):
        mix_copy(j).wait_send()
    for b in range(4):
        a1_copy(own, b).wait_send()
    for q in range(1, chunks):
        last(q)
    for q in range(chunks):
        sent(q)
    bias_copy.wait()


def ahead_call(x, par, wqkv, qvb, seg, wout, up, down, ub):
    rows, width = x.shape
    local = wout.shape[0]
    seq = 2 * rows
    block = rows // 2
    vm = pl.BlockSpec(memory_space=pltpu.VMEM)
    hbm = pl.BlockSpec(memory_space=pltpu.HBM)
    sem = pltpu.SemaphoreType.DMA
    ahead = GATHERED_AHEAD * HIDDEN_BLOCK
    like = lambda a: jax.ShapeDtypeStruct(a.shape, a.dtype)
    return pl.pallas_call(
        ahead_kernel,
        out_shape=(
            jax.ShapeDtypeStruct((seq, width), BF16),
            jax.ShapeDtypeStruct((seq, 3 * local), BF16),
            jax.ShapeDtypeStruct((seq, local), BF16),
            jax.ShapeDtypeStruct((rows, local), BF16),
            jax.ShapeDtypeStruct((local // HEAD_DIM, seq), F32),
            jax.ShapeDtypeStruct((rows, width), F32),
            like(wout), jax.ShapeDtypeStruct((width, ahead), BF16), jax.ShapeDtypeStruct((ahead, width), BF16), like(ub),
        ),
        in_specs=[vm] * 6 + [hbm] * 3 + [vm],
        out_specs=(vm,) * 7 + (hbm,) * 2 + (vm,),
        scratch_shapes=[
            pltpu.VMEM((seq, block), F32),
            sem((4,)), sem((4,)), sem((2,)), sem((2,)),
            *gather_semaphores(1 + GATHERED_AHEAD), sem, sem,
        ],
        compiler_params=pltpu.CompilerParams(
            collective_id=0, has_side_effects=True, vmem_limit_bytes=VMEM_LIMIT
        ),
        name="attend_forward",
    )(x, par, wqkv, qvb, seg, wout, wout, up, down, ub)

CROSS_FIRST = 1
S_SLOTS = 6
VEC_ROWS = 8


def train_kernel(
    half, b_ticks, c_ticks,
    par_ref, ubo_ref, ubt_ref, seg_ref, h_hbm, g_hbm, up_own, down_own, up_oth, down_oth,
    x_hbm, qkv_hbm, mix_hbm, mixt_hbm, lse_ref, a1_hbm, wout_hbm, woutt_hbm, wqkv_hbm,
    out_ref, din_ref, mlp_ref, og_ref, qkvg_ref, vec_ref, up_last, down_last,
    dkv_ref, dm_ref, dsend_ref, send_ref, dq_ref, grad_ref, core_ref, sum_ref, ybuf, zbuf, xfirst, xsend, xbuf,
    vsum, vrecv,
    c_s, c_r, y_s, y_r, z_s, z_r, xf_s, xf_r, x_s, x_r, v_s, v_r, dm_s, dm_r, o_s, o_r, out_sem, free_sem, *gather_sems,
):
    rows, width = din_ref.shape
    seq = 2 * rows
    local = dm_ref.shape[1]
    block = rows // 2
    hb = HIDDEN_BLOCK
    nx = CROSS_FIRST
    n_mlp = 2 * half
    n_all = n_mlp + 4
    z, y, core, side = place()
    partner = peer_x()
    own = pl.multiple_of(side * rows, rows)
    scale = HEAD_DIM**-0.5

    def cols_of(p):
        return 2 * hb if p <= n_mlp else hb

    def hidden_of(p):
        mine = (p - (half - 1) + nx) % half
        if isinstance(p, int):
            return p if p < half - 1 else half - 1 if p == n_mlp - 1 else mine
        return jnp.where(p < half - 1, p, jnp.where(p == n_mlp - 1, half - 1, mine))

    def is_other(p):
        if isinstance(p, int):
            return p < half - 1 or p == n_mlp - 1
        return (p < half - 1) | (p == n_mlp - 1)

    def core_copy(p, cols):
        slot = p % 2
        lanes = pl.ds(0, cols)
        return remote(
            grad_ref.at[slot, :, 1 - core, :, lanes], core_ref.at[slot, :, :, lanes], c_s.at[slot], c_r.at[slot],
            peer_core(),
        )

    def place_of(p, cols):
        if isinstance(p, int) and p > n_mlp:
            n = p - n_mlp - 1
            return n_mlp + 1 - nx + n // 2, pl.ds(n % 2 * hb, hb)
        return p - nx, pl.ds(0, cols)

    def y_copy(p, cols):
        s, lanes = place_of(p, cols)
        src = sum_ref.at[p % S_SLOTS, :, 1 - y, :, pl.ds(0, cols)]
        return remote(src, ybuf.at[s, :, :, lanes], y_s.at[p - nx], y_r.at[p - nx], peer_y())

    def z_copy(p, k, cols):
        s, lanes = place_of(p, cols)
        src, dst = ybuf.at[s, (z + k) % 4, :, lanes], zbuf.at[s, k - 1, :, lanes]
        return remote(src, dst, z_s.at[p - nx, k - 1], z_r.at[p - nx, k - 1], peer_z(k))

    def xfirst_copy(p):
        return remote(sum_ref.at[p % S_SLOTS], xfirst.at[p], xf_s.at[p], xf_r.at[p], partner)

    def x_copy(n):
        lanes = pl.ds(0, 2 * hb if n < half - nx else hb)
        return remote(xsend.at[n, :, lanes], xbuf.at[n, :, lanes], x_s.at[n], x_r.at[n], partner)

    def produced(p, cols):
        @pl.when(p >= 2)
        def _():
            pl.semaphore_wait(free_sem, 1)

        core_copy(p, cols).start()

    def consume(p, cols):
        slot = p % 2
        lanes = pl.ds(0, cols)
        copy = core_copy(p, cols)
        copy.wait()
        if not isinstance(p, int):

            @pl.when(p == S_SLOTS)
            def _():
                sent(0)

        elif p >= S_SLOTS:
            sent(p - S_SLOTS)
        total = grad_ref[slot, :, core, :, lanes].astype(F32) + core_ref[slot, :, :, lanes].astype(F32)
        at = sum_ref.at[p % S_SLOTS, :, :, :, lanes]
        at[...] = total.astype(BF16).reshape(4, 2, 64, cols)

        @pl.when(p < n_all - 2)
        def _():
            pl.semaphore_signal(free_sem, inc=1, device_id=peer_core(), device_id_type=MESH)

    def sent(p):
        if p < nx:
            xfirst_copy(p).wait_send()
        else:
            y_copy(p, cols_of(p)).wait_send()

    def push(p, cols):
        if isinstance(p, int):
            if p < nx:
                xfirst_copy(p).start()
            else:
                y_copy(p, cols).start()
            return

        @pl.when(p < nx)
        def _():
            xfirst_copy(p).start()

        @pl.when(p >= nx)
        def _():
            @pl.when((p >= n_mlp - 1 - nx) & (p < n_mlp - 1))
            def _():
                add_first(p)

            y_copy(p, cols).start()

    def add_first(p):
        b = p - (n_mlp - 1 - nx)
        xfirst_copy(b).wait_recv()
        sum_ref[p % S_SLOTS] = (
            sum_ref[p % S_SLOTS].astype(F32) + xfirst[b].astype(F32)
        ).astype(BF16)

    def second(p):
        cols = cols_of(p)
        s, lanes = place_of(p, cols)
        y_copy(p, cols).wait_recv()
        ybuf[s, :, :, lanes] = (
            sum_ref[p % S_SLOTS, :, y, :, pl.ds(0, cols)].astype(F32) + ybuf[s, :, :, lanes].astype(F32)
        ).astype(BF16)
        for k in (2, 1, 3):
            z_copy(p, k, cols).start()

    def third(p):
        cols = cols_of(p)
        s, lanes = place_of(p, cols)
        for k in (1, 2, 3):
            z_copy(p, k, cols).wait_recv()
        total = ybuf[s, z, :, lanes].astype(F32)
        for k in (1, 2, 3):
            total = total + zbuf[s, k - 1, :, lanes].astype(F32)
        if p < n_mlp and is_other(p):
            n = hidden_of(p) - nx
            xsend[n] = total.astype(BF16)
            x_copy(n).start()
        elif p < n_mlp:
            mlp_ref[hidden_of(p)] = total
        elif p == n_mlp:
            og_ref[...] = total[:, :hb]
            xsend[half - nx, :, pl.ds(0, hb)] = total[:, hb:].astype(BF16)
            x_copy(half - nx).start()
        else:
            qkvg_ref[p - n_mlp - 1] = total

    def fourth(n):
        x_copy(n).wait_recv()
        if n < half - nx:
            mlp_ref[n + nx] += xbuf[n].astype(F32)
        else:
            og_ref[...] += xbuf[n, :, pl.ds(0, hb)].astype(F32)

    def run(names):
        for name, arg in names:
            stages[name](arg)

    def v_copy(w, n, peer, slot):
        return remote(vsum.at[w, n], vrecv.at[w, slot], v_s.at[w, slot], v_r.at[w, slot], peer)

    def z_vec(w, k, source):
        return remote(vsum.at[w, 2], vrecv.at[w, 2 + source], v_s.at[w, 2 + k], v_r.at[w, 2 + source], peer_z(k))

    def vectors(w, n):
        if n == 0:
            v_copy(w, 0, peer_core(), 0).start()
        elif n == 1:
            v_copy(w, 0, peer_core(), 0).wait()
            vsum[w, 1] = vsum[w, 0] + vrecv[w, 0]
            v_copy(w, 1, peer_y(), 1).start()
        elif n == 2:
            v_copy(w, 1, peer_y(), 1).wait()
            vsum[w, 2] = vsum[w, 1] + vrecv[w, 1]
            for k in (1, 2, 3):
                z_vec(w, k, z).start()
        elif n == 3:
            for k in (1, 2, 3):
                z_vec(w, k, z).wait_send()
                z_vec(w, k, (z + k) % 4).wait_recv()
            vrecv[w, 2 + z] = vsum[w, 2]
            vsum[w, 3] = (vrecv[w, 2] + vrecv[w, 3]) + (vrecv[w, 4] + vrecv[w, 5])
            v_copy(w, 3, partner, 6).start()
        elif n == 4:
            v_copy(w, 3, partner, 6).wait()
            vec_ref[pl.ds(w * VEC_ROWS, VEC_ROWS)] = vsum[w, 3] + vrecv[w, 6]

    g_first, g_second, g_third, g_last, g_sent, g_x = gather(
        lambda dp, q: hidden_views((up_own, down_own), dp, half - 1), lambda dp, q: hidden_views((up_last, down_last), dp, 0),
        gather_sems,
    )
    stages = dict(
        second=second, third=third, fourth=fourth, g_first=g_first, g_second=g_second, g_third=g_third, g_last=g_last
    )
    greet()
    for copy in g_x(0):
        copy.start()
    dm_own = dm_ref.at[pl.ds(own, rows)]

    def dm_copy(b):
        at = pl.ds(pl.multiple_of(own + b * block, block), block)
        return remote(dsend_ref.at[b], dm_ref.at[at], dm_s.at[b], dm_r.at[b], partner)

    def dm_from(b):
        at = pl.ds(pl.multiple_of((1 - side) * rows + b * block, block), block)
        return remote(dsend_ref.at[b], dm_ref.at[at], dm_s.at[b], dm_r.at[b], partner)

    def out_copy(j):
        return pltpu.make_async_copy(send_ref.at[j], out_ref.at[j], out_sem.at[j])

    def o_copy(j):
        return remote(send_ref.at[j], xfirst.at[0, pl.ds(2 * j, 2)], o_s.at[j], o_r.at[j], partner)

    def feed(h_ref, g_ref, a2_ref, a2t_ref, gt_ref, wu_ref, wd_ref, in_sem, w_sem):
        load_h = pltpu.make_async_copy(h_hbm, h_ref, in_sem.at[0])
        load_g = pltpu.make_async_copy(g_hbm, g_ref, in_sem.at[1])
        load_h.start()
        load_g.start()

        def fetch(b, up, down, slot):
            at = pl.ds(pl.multiple_of(b * hb, hb), hb)
            return (
                pltpu.make_async_copy(up.at[:, at], wu_ref.at[slot], w_sem.at[slot, 0]),
                pltpu.make_async_copy(down.at[at], wd_ref.at[slot], w_sem.at[slot, 1]),
            )

        def fetch_start(p, slot):
            @pl.when(p < half - 1)
            def _():
                for copy in fetch(hidden_of(p), up_oth, down_oth, slot):
                    copy.start()

            @pl.when((p >= half - 1) & (p < n_mlp - 1))
            def _():
                for copy in fetch(hidden_of(p), up_own, down_own, slot):
                    copy.start()

            @pl.when(p == n_mlp - 1)
            def _():
                g_last(0)
                for copy in fetch(0, up_last, down_last, slot):
                    copy.start()

        fetch_start(0, 0)
        load_h.wait()
        gain = par_ref[pl.ds(GAIN_2, 1)]
        xhat, _ = norm_parts(h_ref[...])
        a2 = (xhat * gain + par_ref[pl.ds(SHIFT_2, 1)]).astype(BF16)
        a2_ref[...] = a2
        a2t_ref[...] = a2.T
        load_g.wait()
        gt_ref[...] = g_ref[...].T
        dkv_ref[...] = jnp.zeros_like(dkv_ref)
        acc_ref = dkv_ref.at[pl.ds(0, rows)]
        da2_ref = dkv_ref.at[pl.ds(rows, rows)]

        def step(p, _):
            slot = p % 2
            for copy in fetch(0, up_own, down_own, slot):
                copy.wait()

            @pl.when(p + 1 < n_mlp)
            def _():
                fetch_start(p + 1, 1 - slot)

            b = hidden_of(p)
            wu, wd = wu_ref[slot], wd_ref[slot]
            u = dot_nn(a2_ref[...], wu) + jnp.where(is_other(p), ubt_ref[pl.ds(b, 1)], ubo_ref[pl.ds(b, 1)])
            tanh = jnp.tanh(0.7978845608028654 * (u + 0.044715 * u * u * u))
            hidden = (0.5 * u * (1.0 + tanh)).astype(BF16)
            slope = 0.5 * (1.0 + tanh) + 0.5 * u * (1.0 - tanh * tanh) * (
                0.7978845608028654 * (1.0 + 3.0 * 0.044715 * u * u)
            )
            acc_ref[...] += dot_nn(hidden, wd)
            du = (dot_nt(g_ref[...], wd) * slope).astype(BF16)
            where_side = jnp.where(is_other(p), 1 - side, side)
            lanes = pl.ds(pl.multiple_of((b % 2) * hb, hb), hb)
            vsum[0, 0, pl.ds(4 + where_side * (half // 2) + b // 2, 1), lanes] = total_of(du.astype(F32))
            da2_ref[...] += dot_nt(du, wu)
            grad_ref[slot, :, :, :, pl.ds(0, hb)] = dot_nn(a2t_ref[...], du).astype(BF16).reshape(8, 2, 64, hb)
            grad_ref[slot, :, :, :, pl.ds(hb, hb)] = dot_nn(gt_ref[...], hidden).astype(BF16).reshape(8, 2, 64, hb)
            produced(p, 2 * hb)

            @pl.when(p >= 1)
            def _():
                consume(p - 1, 2 * hb)
                push(p - 1, 2 * hb)

            for n, names in b_ticks.items():

                @pl.when(p == n)
                def _():
                    run(names)

            return 0

        vsum[0, 0] = jnp.zeros(vsum.shape[2:], F32)
        vsum[1, 0] = jnp.zeros(vsum.shape[2:], F32)
        lax.fori_loop(0, n_mlp, step, 0)

        piece = rows // 4
        sums = [jnp.zeros((1, width), F32) for _ in range(4)]
        for b in range(4):
            at = pl.ds(b * piece, piece)
            h = h_ref[at]
            g = g_ref[at].astype(F32)
            out = (h + acc_ref[at] + par_ref[pl.ds(DOWN_BIAS, 1)]).astype(BF16)
            send_ref[b // 2, b % 2] = out.reshape(2, 64, width)
            xhat, rstd = norm_parts(h)
            da2 = da2_ref[at]
            dh = g + norm_back(da2, gain, xhat, rstd)
            din_ref[at] = dh
            for n, term in enumerate((da2 * xhat, da2, dh.astype(BF16).astype(F32), g)):
                sums[n] = sums[n] + total_of(term)
        for n in range(4):
            vsum[0, 0, pl.ds(n, 1)] = sums[n]
        vectors(0, 0)
        for j in range(2):
            out_copy(j).start()

    vmem = pltpu.VMEM
    sem = pltpu.SemaphoreType.DMA
    pl.run_scoped(
        feed,
        vmem((rows, width), F32), vmem((rows, width), BF16), vmem((rows, width), BF16), vmem((width, rows), BF16),
        vmem((width, rows), BF16), vmem((2, width, hb), BF16), vmem((2, hb, width), BF16), sem((2,)), sem((2, 2)),
    )

    def attend(qkv_ref, mix_ref, mixt_ref, wout_ref, wqkv_ref, mask_ref, dhl_ref, in_sem):
        a1_ref, x_ref, dqkv_ref = wout_ref, dhl_ref, qkv_ref
        moves = [
            pltpu.make_async_copy(src, dst, in_sem.at[n])
            for n, (src, dst) in enumerate((
                (wout_hbm, wout_ref.at[pl.ds(0, local)]), (woutt_hbm, wout_ref.at[pl.ds(local, local)]),
                (mix_hbm, mix_ref), (mixt_hbm, mixt_ref), (qkv_hbm, qkv_ref), (wqkv_hbm, wqkv_ref),
                (x_hbm, x_ref), (a1_hbm, a1_ref),
            ))
        ]
        for move in moves[:6]:
            move.start()
        dhl_ref[...] = din_ref[...].astype(BF16)
        consume(n_mlp - 1, 2 * hb)
        push(n_mlp - 1, 2 * hb)
        moves[0].wait()
        moves[1].wait()
        for b in (1, 0):
            dsend_ref[b] = dot_nt(dhl_ref[pl.ds(b * block, block)], wout_ref[pl.ds(local, local)]).astype(BF16)
            dm_copy(b).start()
        dm_own[...] = dot_nt(dhl_ref[...], wout_ref[pl.ds(0, local)]).astype(BF16)
        moves[7].start()
        moves[2].wait()
        moves[3].wait()
        p = n_mlp
        for part in range(2):
            mixed = mixt_ref[...] if part else mix_ref[pl.ds(own, rows)]
            grad = dot_tn(dhl_ref[...], mixed).astype(BF16)
            grad_ref[p % 2, :, :, :, pl.ds(part * hb, hb)] = grad.reshape(8, 2, 64, hb)
        produced(p, 2 * hb)
        moves[6].start()
        dkv_ref[...] = jnp.zeros_like(dkv_ref)
        seg_row = seg_ref[...].astype(F32)
        seg_col = jnp.broadcast_to(seg_row, (8, seq)).T[:, :1]
        moves[4].wait()
        for j in range(2):
            out_copy(j).wait()

        def task(i, keys, stage="all", ticks=()):
            lo, start, count = i * block, keys[0], keys[1] - keys[0]
            at, among = pl.ds(lo, block), pl.ds(start, count)
            same = seg_col[start : start + count] == seg_row[:, lo : lo + block]
            k_pos = start + lax.broadcasted_iota(jnp.int32, (count, block), 0)
            q_pos = lo + lax.broadcasted_iota(jnp.int32, (count, block), 1)
            mask_ref[pl.ds(0, count)] = jnp.where(same & (q_pos >= k_pos), 0.0, -1e30)

            def pair(hp, _):
                base = pl.multiple_of(hp * 2 * HEAD_DIM, 2 * HEAD_DIM)
                cols = pl.ds(base, 2 * HEAD_DIM)
                v_cols = pl.ds(pl.multiple_of(local + base, 128), 2 * HEAD_DIM)
                q2 = qkv_ref[at, cols]
                k2 = qkv_ref[among, v_cols]
                v2 = qkv_ref[among, pl.ds(pl.multiple_of(2 * local + base, 128), 2 * HEAD_DIM)]
                g2 = dm_ref[at, cols]
                turned = (g2.astype(F32) * mix_ref[at, cols].astype(F32)).T
                dq = jnp.zeros((block, 2 * HEAD_DIM), F32)
                dk = jnp.zeros((count, 2 * HEAD_DIM), F32)
                dv = jnp.zeros((count, 2 * HEAD_DIM), F32)
                for h in range(2):
                    qh = only_head(q2, h)
                    gh = only_head(g2, h)
                    row_dot = total_of(turned[h * HEAD_DIM : (h + 1) * HEAD_DIM])
                    offset = mask_ref[pl.ds(0, count)] - lse_ref[pl.ds(2 * hp + h, 1), at]
                    probs = jnp.exp(dot_nt(k2, qh) * scale + offset)
                    dscore = (probs * (dot_nt(v2, gh) - row_dot)).astype(BF16)
                    dv += dot_nn(probs.astype(BF16), gh)
                    dk += dot_nn(dscore, qh)
                    dq += dot_tn(dscore, only_head(k2, h))
                if stage == "first":
                    dq_ref[i - 2, :, cols] = dq
                else:
                    if stage == "last":
                        dq = dq + dq_ref[i - 2, :, cols]
                    dqkv_ref[at, cols] = (dq * scale).astype(BF16)
                dkv_ref[among, cols] += dk
                dkv_ref[among, v_cols] += dv
                for n, names in ticks:

                    @pl.when(hp == n)
                    def _():
                        run(names)

                return 0

            lax.fori_loop(0, local // (2 * HEAD_DIM), pair, 0)

        def finish(i, send):
            at = pl.ds(i * block, block)
            dqkv_ref[at, pl.ds(local, local)] = (dkv_ref[at, pl.ds(0, local)] * scale).astype(BF16)
            dqkv_ref[at, pl.ds(2 * local, local)] = dkv_ref[at, pl.ds(local, local)].astype(BF16)
            product = dot_nt(dqkv_ref[at], wqkv_ref[...])
            if send:
                send_ref[i % 2] = product.astype(BF16).reshape(send_ref.shape[1:])
                o_copy(i % 2).start()
            else:
                dkv_ref[at] = product

        def second_block():
            consume(n_mlp, 2 * hb)
            push(n_mlp, 2 * hb)
            vectors(0, 1)
            moves[5].wait()

        @pl.when(side == 0)
        def _():
            dm_from(1).wait_recv()
            task(3, (0, 4 * block), ticks=c_ticks[0][0])
            second_block()
            finish(3, True)
            dm_from(0).wait_recv()
            task(2, (0, 3 * block), ticks=c_ticks[0][1])
            finish(2, True)
            task(1, (0, 2 * block), ticks=c_ticks[0][2])
            finish(1, False)
            task(0, (0, block), ticks=c_ticks[0][3])
            finish(0, False)

        @pl.when(side == 1)
        def _():
            task(3, (0, 2 * block), "first", ticks=c_ticks[1][0])
            task(2, (0, 2 * block), "first", ticks=c_ticks[1][1])
            second_block()
            dm_from(1).wait_recv()
            task(1, (0, 2 * block), ticks=c_ticks[1][2])
            finish(1, True)
            dm_from(0).wait_recv()
            task(0, (0, block), ticks=c_ticks[1][3])
            finish(0, True)
            task(3, (2 * block, 4 * block), "last", ticks=c_ticks[1][4])
            finish(3, False)
            task(2, (2 * block, 3 * block), "last", ticks=c_ticks[1][5])
            finish(2, False)

        moves[7].wait()
        for part in range(3):
            p = n_mlp + 1 + part
            grad = dot_tn(a1_ref[...], dqkv_ref[:, pl.ds(part * local, local)]).astype(BF16)
            grad_ref[p % 2, :, :, :, pl.ds(0, hb)] = grad.reshape(8, 2, 64, hb)
            produced(p, hb)
            if part == 1:
                consume(p - 1, hb)
                push(p - 1, hb)
        moves[6].wait()

        def finish_rows(j):
            at = pl.ds(j * block, block)
            o_copy(j).wait_recv()
            da1 = dkv_ref[pl.ds(pl.multiple_of(own + j * block, block), block)] + xfirst[0, pl.ds(2 * j, 2)].reshape(
                block, width
            ).astype(F32)
            xhat, rstd = norm_parts(x_ref[at].astype(F32))
            din_ref[at] += norm_back(da1, par_ref[pl.ds(GAIN_1, 1)], xhat, rstd)
            return total_of(da1 * xhat), total_of(da1)

        lanes = pl.ds(pl.multiple_of(side * local, local), local)
        vsum[1, 0, pl.ds(2, 1), lanes] = total_of(dqkv_ref[:, pl.ds(0, local)].astype(F32))
        vsum[1, 0, pl.ds(3, 1), lanes] = total_of(dqkv_ref[:, pl.ds(2 * local, local)].astype(F32))
        gain_1, shift_1 = finish_rows(1)
        consume(n_mlp + 2, hb)
        run(c_ticks["end"])
        consume(n_mlp + 3, hb)
        gain_0, shift_0 = finish_rows(0)
        vsum[1, 0, pl.ds(0, 1)] = gain_0 + gain_1
        vsum[1, 0, pl.ds(1, 1)] = shift_0 + shift_1
        vectors(1, 0)
        vectors(1, 1)
        push(n_mlp + 2, hb)
        push(n_mlp + 3, hb)

    pl.run_scoped(
        attend,
        vmem((seq, 3 * local), BF16), vmem((seq, local), BF16), vmem((rows, local), BF16),
        vmem((2 * local, width), BF16), vmem((width, 3 * local), BF16), vmem((seq, block), F32), vmem((rows, width), BF16),
        sem((8,)),
    )

    for name, arg in c_ticks["tail"]:
        if name == "vec":
            vectors(*arg)
        else:
            run([(name, arg)])

    g_sent(0)
    for j in range(2):
        dm_copy(j).wait_send()
        o_copy(j).wait_send()
    for p in range(n_all - S_SLOTS, n_all):
        sent(p)
    for p in range(nx, n_all):
        for k in (1, 2, 3):
            z_copy(p, k, cols_of(p)).wait_send()
    for n in range(half - nx + 1):
        x_copy(n).wait_send()


def train_call(par, ubo, ubt, seg, h, g, up_own, down_own, up_oth, down_oth, x, qkv, mix, mixt, lse, a1, wout, woutt, wqkv):
    rows, width = h.shape
    local = wout.shape[0]
    seq = 2 * rows
    block = rows // 2
    hb = HIDDEN_BLOCK
    half = up_own.shape[1] // hb
    nx = CROSS_FIRST
    n_mlp, n_all = 2 * half, 2 * half + 4
    height = width // PIECES
    vm = pl.BlockSpec(memory_space=pltpu.VMEM)
    hbm = pl.BlockSpec(memory_space=pltpu.HBM)
    sem = pltpu.SemaphoreType.DMA
    ny = n_all - nx
    nxl = half - nx + 1
    b_ticks, c_ticks = schedule(half)
    return pl.pallas_call(
        functools.partial(train_kernel, half, b_ticks, c_ticks),
        out_shape=(
            jax.ShapeDtypeStruct((2, 2, 2, height, width), BF16),
            jax.ShapeDtypeStruct((rows, width), F32),
            jax.ShapeDtypeStruct((half, height, 2 * hb), F32),
            jax.ShapeDtypeStruct((height, local), F32),
            jax.ShapeDtypeStruct((3, height, local), F32),
            jax.ShapeDtypeStruct((2 * VEC_ROWS, width), F32),
            jax.ShapeDtypeStruct((width, hb), BF16),
            jax.ShapeDtypeStruct((hb, width), BF16),
        ),
        in_specs=[vm] * 4 + [hbm] * 10 + [vm] + [hbm] * 4,
        out_specs=(hbm,) + (vm,) * 5 + (hbm,) * 2,
        scratch_shapes=[
            pltpu.VMEM((seq, width), F32),
            pltpu.VMEM((seq, local), BF16),
            pltpu.VMEM((2, block, local), BF16),
            pltpu.VMEM((2, 2, 2, height, width), BF16),
            pltpu.VMEM((2, block, local), F32),
            pltpu.VMEM((2, 8, 2, height, 2 * hb), BF16),
            pltpu.VMEM((2, 8, height, 2 * hb), BF16),
            pltpu.VMEM((S_SLOTS, 4, 2, height, 2 * hb), BF16),
            pltpu.VMEM((ny - 1, 4, height, 2 * hb), BF16),
            pltpu.VMEM((ny - 1, 3, height, 2 * hb), BF16),
            pltpu.VMEM((max(nx, 1), 4, 2, height, 2 * hb), BF16),
            pltpu.VMEM((nxl, height, 2 * hb), BF16),
            pltpu.VMEM((nxl, height, 2 * hb), BF16),
            pltpu.VMEM((2, 4, VEC_ROWS, width), F32),
            pltpu.VMEM((2, 7, VEC_ROWS, width), F32),
            sem((2,)), sem((2,)), sem((ny,)), sem((ny,)), sem((ny, 3)), sem((ny, 3)),
            sem((max(nx, 1),)), sem((max(nx, 1),)), sem((nxl,)), sem((nxl,)), sem((2, 7)), sem((2, 7)),
            sem((2,)), sem((2,)), sem((2,)), sem((2,)), sem((2,)), pltpu.SemaphoreType.REGULAR,
            *gather_semaphores(1),
        ],
        compiler_params=pltpu.CompilerParams(
            collective_id=1, has_side_effects=True, vmem_limit_bytes=VMEM_LIMIT
        ),
        name="train_step",
    )(par, ubo, ubt, seg, h, g, up_own, down_own, up_oth, down_oth, x, qkv, mix, mixt, lse, a1, wout, woutt, wqkv)


def schedule(half):
    nx = CROSS_FIRST
    n_mlp = 2 * half
    n_all = n_mlp + 4
    todo = []
    for p in range(nx, n_all + 1):
        if p < n_all:
            todo.append(("second", p))
        if p - 1 >= nx:
            todo.append(("third", p - 1))
    b_ticks = {0: [("g_first", 0)], 2: [("g_second", 0)], 4: [("g_third", 0)], n_mlp - 3: [todo.pop(0)]}
    a, b, c, d, e = [todo.pop(0) for _ in range(5)]
    c_ticks = {
        0: [[(1, [a]), (3, [b])], [(1, [c]), (3, [d])], [(2, [e])], []],
        1: [[(1, [a])], [(0, [b]), (2, [c])], [(1, [d])], [], [(0, [e])], []],
        "end": [todo.pop(0), todo.pop(0)],
    }
    after = {
        ("second", n_mlp): (0, 2), ("third", n_mlp): (0, 3), ("second", n_mlp + 1): (1, 2), ("third", n_mlp + 1): (1, 3)
    }
    tail = []
    for item in todo:
        tail.append(item)
        if item in after:
            tail.append(("vec", after[item]))
    tail += [("fourth", n) for n in range(half - nx + 1)]
    c_ticks["tail"] = tail + [("vec", (0, 4)), ("vec", (1, 4))]
    return b_ticks, c_ticks


def on_device_pair(
    inputs, segment_ids, first_gain, first_shift, qkv_weight, qv_bias, out_weight, out_bias,
    second_gain, second_shift, up_weight, up_bias, down_weight, down_bias, cotangent,
):
    rows, _, width = inputs.shape
    seq = segment_ids.shape[0]
    local = out_weight.shape[0]
    hidden = up_weight.shape[1]
    side = lax.axis_index("tensor")
    x = inputs.reshape(rows, width)
    g = cotangent.reshape(rows, width)
    seg = segment_ids.reshape(1, seq)
    wqkv = qkv_weight.reshape(width, 3 * local)
    par = jnp.stack([first_gain, first_shift, out_bias, second_gain, second_shift, down_bias]).astype(F32)
    half = hidden // HIDDEN_BLOCK
    ubo = jnp.pad(up_bias.astype(F32).reshape(half, HIDDEN_BLOCK), ((0, 8 - half), (0, 0)))
    a1, qkv, mix, mixt, lse, h, woutt, up_oth, down_oth, ubt = ahead_call(
        x, par, wqkv, qv_bias, seg, out_weight, up_weight, down_weight, ubo
    )
    layer_output, input_grad, mlp, out_g, qkv_g, total, _, _ = train_call(
        par, ubo, ubt, seg, h, g, up_weight, down_weight, up_oth, down_oth, x, qkv, mix, mixt, lse, a1,
        out_weight, woutt, wqkv,
    )
    height = width // PIECES
    up_share = jnp.transpose(mlp[:, :, :HIDDEN_BLOCK], (1, 0, 2)).reshape(height, hidden)
    down_share = jnp.transpose(mlp[:, :, HIDDEN_BLOCK:], (0, 2, 1)).reshape(hidden, height)
    qkv_share = jnp.transpose(qkv_g, (1, 0, 2))
    out_share = out_g.T
    qv_share = lax.dynamic_slice_in_dim(total[10:12], side * local, local, 1)
    up_bias_share = lax.dynamic_slice_in_dim(total[4:8].reshape(2 * hidden), side * hidden, hidden, 0)
    return (
        layer_output.reshape(rows, 1, width),
        input_grad.reshape(rows, 1, width),
        total[8],
        total[9],
        qkv_share,
        qv_share,
        out_share,
        total[2],
        total[0],
        total[1],
        up_share,
        up_bias_share,
        down_share,
        total[3],
    )


def solution(mesh):
    in_specs = (
        P("tensor", "dp", None),
        P(None, "dp"),
        P(),
        P(),
        P(None, None, "tensor"),
        P(None, "tensor"),
        P("tensor", None),
        P(),
        P(),
        P(),
        P(None, "tensor"),
        P("tensor"),
        P("tensor", None),
        P(),
        P("tensor", "dp", None),
    )
    out_specs = (
        P("tensor", "dp", None),
        P("tensor", "dp", None),
        P(),
        P(),
        P("dp", None, "tensor"),
        P(None, "tensor"),
        P("tensor", "dp"),
        P(),
        P(),
        P(),
        P("dp", "tensor"),
        P("tensor"),
        P("tensor", "dp"),
        P(),
    )
    pair = mesh.shape["tensor"] == 2 and mesh.shape["dp"] == Z_SIZE * Y_SIZE * CORES
    return jax.shard_map(
        on_device_pair if pair else on_device, mesh=mesh, in_specs=in_specs, out_specs=out_specs, check_vma=False
    )
```

```python
import functools

import jax
import jax.numpy as jnp
from jax import lax
from jax.experimental import pallas as pl
from jax.experimental.pallas import tpu as pltpu
from jax.sharding import PartitionSpec as P

HEAD_DIM = 64
MESH = pl.DeviceIdType.MESH
F32 = jnp.float32
BF16 = jnp.bfloat16
VMEM_LIMIT = 63 << 20


norm_eps = 1e-05


def layer_norm(value, gain, shift):
    row_mean = jnp.mean(value, axis=-1, keepdims=True)
    centred = value - row_mean
    variance = jnp.mean(centred * centred, axis=-1, keepdims=True)
    return centred * lax.rsqrt(variance + norm_eps) * gain + shift


def gelu_tanh(value):
    return (
        0.5
        * value
        * (1.0 + jnp.tanh(0.7978845608028654 * (value + 0.044715 * value * value * value)))
    )


def masked_scores(query_block, keys_all, seg_block, seg_all, row_start, block_rows, score_scale):
    scores = (
        jnp.einsum("qhd,khd->hqk", query_block, keys_all, preferred_element_type=jnp.float32)
        * score_scale
    )
    key_pos = jnp.arange(keys_all.shape[0], dtype=jnp.int32)
    query_pos = row_start + jnp.arange(block_rows, dtype=jnp.int32)
    allowed = (seg_block[:, None] == seg_all[None, :]) & (query_pos[:, None] >= key_pos[None, :])
    return jnp.where(allowed[None], scores, -1e30)


def attend_forward(queries, keys_all, values_all, seg_all, score_scale):
    seq_len = queries.shape[0]
    block_rows = min(512, seq_len)

    def one_block(block_index):
        row_start = block_index * block_rows
        query_block = lax.dynamic_slice_in_dim(queries, row_start, block_rows, 0)
        seg_block = lax.dynamic_slice_in_dim(seg_all, row_start, block_rows, 0)
        scores = masked_scores(
            query_block, keys_all, seg_block, seg_all, row_start, block_rows, score_scale
        )
        row_top = jnp.max(scores, axis=-1, keepdims=True)
        weights = jnp.exp(scores - row_top)
        row_total = jnp.sum(weights, axis=-1, keepdims=True)
        probs_low = (weights / row_total).astype(jnp.bfloat16)
        mixed = jnp.einsum(
            "hqk,khd->qhd", probs_low, values_all, preferred_element_type=jnp.float32
        )
        return (mixed, row_top + jnp.log(row_total))

    mixed, log_total = lax.map(one_block, jnp.arange(seq_len // block_rows, dtype=jnp.int32))
    return (mixed.reshape(seq_len, -1), log_total)


def attend_backward(queries, keys_all, values_all, seg_all, log_total, out_grad, score_scale):
    seq_len = queries.shape[0]
    block_rows = min(512, seq_len)

    def one_block(carry, block_index):
        key_grad, value_grad = carry
        row_start = block_index * block_rows
        query_block = lax.dynamic_slice_in_dim(queries, row_start, block_rows, 0)
        seg_block = lax.dynamic_slice_in_dim(seg_all, row_start, block_rows, 0)
        grad_block = lax.dynamic_slice_in_dim(out_grad, row_start, block_rows, 0)
        scores = masked_scores(
            query_block, keys_all, seg_block, seg_all, row_start, block_rows, score_scale
        )
        probs = jnp.exp(scores - log_total[block_index])
        probs_low = probs.astype(jnp.bfloat16)
        value_grad = value_grad + jnp.einsum(
            "hqk,qhd->khd", probs_low, grad_block, preferred_element_type=jnp.float32
        )
        prob_grad = jnp.einsum(
            "qhd,khd->hqk", grad_block, values_all, preferred_element_type=jnp.float32
        )
        row_dot = jnp.sum(probs * prob_grad, axis=-1, keepdims=True)
        score_grad = (probs * (prob_grad - row_dot)).astype(jnp.bfloat16)
        query_grad = (
            jnp.einsum("hqk,khd->qhd", score_grad, keys_all, preferred_element_type=jnp.float32)
            * score_scale
        )
        key_grad = (
            key_grad
            + jnp.einsum(
                "hqk,qhd->khd", score_grad, query_block, preferred_element_type=jnp.float32
            )
            * score_scale
        )
        return ((key_grad, value_grad), query_grad)

    zero_grads = jnp.zeros(keys_all.shape, jnp.float32)
    (key_grad, value_grad), query_grad = lax.scan(
        one_block, (zero_grads, zero_grads), jnp.arange(seq_len // block_rows, dtype=jnp.int32)
    )
    return (
        query_grad.reshape(seq_len, -1),
        key_grad.reshape(seq_len, -1),
        value_grad.reshape(seq_len, -1),
    )


def row_product(left, right, contract):
    return lax.dot_general(
        left, right, (((1,), (contract,)), ((), ())), preferred_element_type=jnp.float32
    )


def rows_contract(left, right):
    return lax.dot_general(
        left, right, (((0,), (0,)), ((), ())), preferred_element_type=jnp.float32
    )


def on_device(
    inputs,
    segment_ids,
    first_gain,
    first_shift,
    qkv_weight,
    qv_bias,
    out_weight,
    out_bias,
    second_gain,
    second_shift,
    up_weight,
    up_bias,
    down_weight,
    down_bias,
    cotangent,
):
    rows_dev, seq_count, model_width = inputs.shape
    tensor_count = lax.axis_size("tensor")
    tensor_rank = lax.axis_index("tensor")
    seq_len = rows_dev * tensor_count
    local_width = out_weight.shape[0]
    heads_dev = local_width // HEAD_DIM
    hidden_dev = up_weight.shape[1]
    local_rows = rows_dev * seq_count
    score_scale = HEAD_DIM ** (-0.5)
    residual_in = inputs.reshape(local_rows, model_width).astype(jnp.float32)
    gain_one = first_gain.astype(jnp.float32)
    shift_one = first_shift.astype(jnp.float32)
    gain_two = second_gain.astype(jnp.float32)
    shift_two = second_shift.astype(jnp.float32)
    normed_one, pull_one = jax.vjp(layer_norm, residual_in, gain_one, shift_one)
    first_local = normed_one.astype(jnp.bfloat16)
    first_rows = lax.all_gather(first_local, "tensor", axis=0, tiled=True)
    qkv_flat = qkv_weight.reshape(model_width, 3 * local_width)
    qkv_bias = jnp.concatenate(
        [
            qv_bias[0].astype(jnp.float32),
            jnp.zeros((local_width,), jnp.float32),
            qv_bias[1].astype(jnp.float32),
        ]
    )
    qkv_low = (jnp.dot(first_rows, qkv_flat, preferred_element_type=jnp.float32) + qkv_bias).astype(
        jnp.bfloat16
    )
    qkv_split = qkv_low.reshape(seq_len, seq_count, 3, heads_dev, HEAD_DIM)
    seq_index = 0
    mixed_one, log_one = attend_forward(
        qkv_split[:, seq_index, 0],
        qkv_split[:, seq_index, 1],
        qkv_split[:, seq_index, 2],
        segment_ids[:, seq_index],
        score_scale,
    )
    mixed_list = [mixed_one]
    log_list = [log_one]
    mixed_low = (
        jnp.stack(mixed_list, axis=1).reshape(seq_len * seq_count, local_width).astype(jnp.bfloat16)
    )
    attn_local = lax.psum_scatter(
        row_product(mixed_low, out_weight, 0), "tensor", scatter_dimension=0, tiled=True
    )
    residual_mid = residual_in + attn_local + out_bias.astype(jnp.float32)
    normed_two, pull_two = jax.vjp(layer_norm, residual_mid, gain_two, shift_two)
    second_local = normed_two.astype(jnp.bfloat16)
    second_rows = lax.all_gather(second_local, "tensor", axis=0, tiled=True)
    hidden_pre = jnp.dot(
        second_rows, up_weight, preferred_element_type=jnp.float32
    ) + up_bias.astype(jnp.float32)
    activated, pull_gelu = jax.vjp(gelu_tanh, hidden_pre)
    hidden_low = activated.astype(jnp.bfloat16)
    mlp_local = lax.psum_scatter(
        row_product(hidden_low, down_weight, 0).astype(jnp.bfloat16),
        "tensor",
        scatter_dimension=0,
        tiled=True,
    ).astype(jnp.float32)
    layer_output = (residual_mid + mlp_local + down_bias.astype(jnp.float32)).astype(jnp.bfloat16)
    layer_output = layer_output.reshape(rows_dev, seq_count, model_width)
    grad_local = cotangent.reshape(local_rows, model_width)
    grad_rows = lax.all_gather(grad_local, "tensor", axis=0, tiled=True)
    down_grad = rows_contract(hidden_low, grad_rows)
    hidden_grad = lax.dot_general(
        grad_rows, down_weight, (((1,), (1,)), ((), ())), preferred_element_type=jnp.float32
    )
    (pre_grad,) = pull_gelu(hidden_grad)
    pre_low = pre_grad.astype(jnp.bfloat16)
    up_sums = jnp.sum(pre_low, axis=0, dtype=jnp.float32)
    second_back = lax.all_gather(second_local, "tensor", axis=0, tiled=True)
    up_grad = rows_contract(second_back, pre_low)
    second_norm_grad = lax.psum_scatter(
        row_product(pre_low, up_weight, 1), "tensor", scatter_dimension=0, tiled=True
    )
    mid_from_norm, gain_two_grad, shift_two_grad = pull_two(second_norm_grad)
    residual_grad = grad_local.astype(jnp.float32) + mid_from_norm
    residual_low = residual_grad.astype(jnp.bfloat16)
    residual_rows = lax.all_gather(residual_low, "tensor", axis=0, tiled=True)
    out_grad_weight = rows_contract(mixed_low, residual_rows)
    mixed_grad = lax.dot_general(
        residual_rows, out_weight, (((1,), (1,)), ((), ())), preferred_element_type=jnp.float32
    ).astype(jnp.bfloat16)
    mixed_grad = mixed_grad.reshape(seq_len, seq_count, heads_dev, HEAD_DIM)
    seq_index = 0
    query_grad, key_grad, value_grad = attend_backward(
        qkv_split[:, seq_index, 0],
        qkv_split[:, seq_index, 1],
        qkv_split[:, seq_index, 2],
        segment_ids[:, seq_index],
        log_list[seq_index],
        mixed_grad[:, seq_index],
        score_scale,
    )
    query_list = [query_grad]
    key_list = [key_grad]
    value_list = [value_grad]
    qkv_grad = jnp.concatenate(
        [jnp.stack(query_list, axis=1), jnp.stack(key_list, axis=1), jnp.stack(value_list, axis=1)],
        axis=-1,
    )
    qkv_grad_low = qkv_grad.reshape(seq_len * seq_count, 3 * local_width).astype(jnp.bfloat16)
    qkv_sums = jnp.sum(qkv_grad_low, axis=0, dtype=jnp.float32)
    qv_sums = jnp.stack([qkv_sums[:local_width], qkv_sums[2 * local_width :]], axis=0)
    first_back = lax.all_gather(first_local, "tensor", axis=0, tiled=True)
    qkv_grad_weight = rows_contract(first_back, qkv_grad_low).reshape(model_width, 3, local_width)
    first_norm_grad = lax.psum_scatter(
        row_product(qkv_grad_low, qkv_flat, 1), "tensor", scatter_dimension=0, tiled=True
    )
    in_from_norm, gain_one_grad, shift_one_grad = pull_one(first_norm_grad)
    input_grad = (residual_grad + in_from_norm).reshape(rows_dev, seq_count, model_width)
    qkv_share, out_share, up_share, down_share = (
        lax.psum_scatter(qkv_grad_weight, "dp", scatter_dimension=0, tiled=True),
        lax.psum_scatter(out_grad_weight, "dp", scatter_dimension=1, tiled=True),
        lax.psum_scatter(up_grad, "dp", scatter_dimension=0, tiled=True),
        lax.psum_scatter(down_grad, "dp", scatter_dimension=1, tiled=True),
    )
    out_bias_part = jnp.sum(residual_low, axis=0, dtype=jnp.float32)
    down_bias_part = jnp.sum(grad_local, axis=0, dtype=jnp.float32)
    stacked = jnp.stack(
        [
            gain_one_grad,
            shift_one_grad,
            gain_two_grad,
            shift_two_grad,
            out_bias_part,
            down_bias_part,
        ],
        axis=0,
    )
    qv_full = lax.dynamic_update_slice(
        jnp.zeros((2, model_width), jnp.float32), qv_sums, (jnp.int32(0), tensor_rank * local_width)
    )
    up_full = lax.dynamic_update_slice(
        jnp.zeros((hidden_dev * tensor_count,), jnp.float32), up_sums, (tensor_rank * hidden_dev,)
    )
    stacked, qv_total, up_total = lax.psum((stacked, qv_full, up_full), ("dp", "tensor"))
    qv_share = lax.dynamic_slice_in_dim(qv_total, tensor_rank * local_width, local_width, 1)
    up_bias_share = lax.dynamic_slice_in_dim(up_total, tensor_rank * hidden_dev, hidden_dev, 0)
    return (
        layer_output,
        input_grad,
        stacked[0],
        stacked[1],
        qkv_share,
        qv_share,
        out_share,
        stacked[4],
        stacked[2],
        stacked[3],
        up_share,
        up_bias_share,
        down_share,
        stacked[5],
    )


Z_SIZE, Y_SIZE, CORES = 4, 2, 2


def place():
    dp = lax.axis_index("dp")
    side = lax.axis_index("tensor")
    return dp // 4, (dp // 2) % 2, dp % 2, side


def dev(z, y, core, side):
    return (z * 4 + y * 2 + core, side)


def peer_x():
    z, y, core, side = place()
    return dev(z, y, core, 1 - side)


def peer_y():
    z, y, core, side = place()
    return dev(z, 1 - y, core, side)


def peer_core():
    z, y, core, side = place()
    return dev(z, y, 1 - core, side)


def peer_z(step):
    z, y, core, side = place()
    return dev((z + step) % 4, y, core, side)


def greet():
    peers = [peer_x(), peer_y(), peer_core()] + [peer_z(k) for k in (1, 2, 3)]
    barrier = pltpu.get_barrier_semaphore()
    for peer in peers:
        pl.semaphore_signal(barrier, inc=1, device_id=peer, device_id_type=MESH)
    pl.semaphore_wait(barrier, len(peers))


def remote(src, dst, send_sem, recv_sem, peer):
    return pltpu.make_async_remote_copy(
        src_ref=src, dst_ref=dst, send_sem=send_sem, recv_sem=recv_sem, device_id=peer, device_id_type=MESH
    )


def dot_nn(a, b):
    return lax.dot_general(a, b, (((1,), (0,)), ((), ())), preferred_element_type=F32)


def dot_nt(a, b):
    return lax.dot_general(a, b, (((1,), (1,)), ((), ())), preferred_element_type=F32)


def dot_tn(a, b):
    return lax.dot_general(a, b, (((0,), (0,)), ((), ())), preferred_element_type=F32)


def norm_parts(value):
    mean = jnp.mean(value, axis=-1, keepdims=True)
    centred = value - mean
    rstd = lax.rsqrt(jnp.mean(centred * centred, axis=-1, keepdims=True) + norm_eps)
    return centred * rstd, rstd


def norm_back(grad, gain, xhat, rstd):
    e = grad * gain
    return rstd * (e - jnp.mean(e, axis=-1, keepdims=True) - xhat * jnp.mean(e * xhat, axis=-1, keepdims=True))


def head_lanes(h):
    lane = lax.broadcasted_iota(jnp.int32, (1, 2 * HEAD_DIM), 1)
    return (lane // HEAD_DIM) == h


def only_head(value, h):
    return jnp.where(head_lanes(h), value, jnp.zeros_like(value))


def total_of(row):
    return jnp.sum(row, axis=0, keepdims=True)


GAIN_1, SHIFT_1, OUT_BIAS, GAIN_2, SHIFT_2, DOWN_BIAS = range(6)
PIECES = 16
HIDDEN_BLOCK = 512


def gather(source, target, sems):
    x_s, x_r, z_s, z_r, y_s, y_r, c_s, c_r = sems
    z, y, core, side = place()

    def copies(dp, q, send, recv, peer, views=target):
        pairs = zip(views(dp, q), target(dp, q))
        return [remote(s, d, send.at[a], recv.at[a], peer) for a, (s, d) in enumerate(pairs)]

    def number(zz, yy, cc):
        return zz * 4 + yy * 2 + cc

    def from_z(k):
        return (z + 4 - k) % 4

    def x_copies(q):
        return copies(number(z, y, core), q, x_s.at[q], x_r.at[q], peer_x(), source)

    def z_sends(q, k):
        return copies(number(z, y, core), q, z_s.at[q, k], z_r.at[q, k], peer_z(k))

    def z_recvs(q, k):
        return copies(number(from_z(k), y, core), q, z_s.at[q, k], z_r.at[q, k], peer_z(k))

    def y_copies(q, k, yy):
        return copies(number(from_z(k), yy, core), q, y_s.at[q, k], y_r.at[q, k], peer_y())

    def c_copies(q, k, far, cc):
        yy = (1 - y) if far else y
        slot = 4 * far + k
        return copies(number(from_z(k), yy, cc), q, c_s.at[q, slot], c_r.at[q, slot], peer_core())

    def start(list_of):
        for copy in list_of:
            copy.start()

    def first(q):
        for copy in x_copies(q):
            copy.wait()
        for k in (2, 1, 3):
            start(z_sends(q, k))
        start(y_copies(q, 0, y))
        start(c_copies(q, 0, 0, core))

    def second(q):
        for k in (1, 3, 2):
            for copy in z_recvs(q, k):
                copy.wait_recv()
            start(y_copies(q, k, y))
            start(c_copies(q, k, 0, core))

    def third(q):
        for k in range(4):
            for copy in y_copies(q, k, 1 - y):
                copy.wait_recv()
            start(c_copies(q, k, 1, core))

    def last(q):
        for k in range(4):
            for far in (0, 1):
                for copy in c_copies(q, k, far, 1 - core):
                    copy.wait_recv()

    def sent(q):
        for k in range(4):
            if k > 0:
                for copy in z_sends(q, k):
                    copy.wait_send()
            for copy in y_copies(q, k, y):
                copy.wait_send()
            for far in (0, 1):
                for copy in c_copies(q, k, far, core):
                    copy.wait_send()

    return first, second, third, last, sent, x_copies


def gather_semaphores(q):
    sem = pltpu.SemaphoreType.DMA
    return [sem((q, 2))] * 2 + [sem((q, 4, 2))] * 4 + [sem((q, 8, 2))] * 2


def hidden_views(arrays, dp, b):
    up, down = arrays
    n_up, n_down = up.shape[0] // PIECES, HIDDEN_BLOCK // PIECES
    return [
        up.at[pl.ds(pl.multiple_of(dp * n_up, n_up), n_up), pl.ds(b * HIDDEN_BLOCK, HIDDEN_BLOCK)],
        down.at[pl.ds(pl.multiple_of(b * HIDDEN_BLOCK + dp * n_down, n_down), n_down)],
    ]


CROSS_FIRST = 2
ORDER = (("t", 0), ("t", 1), ("o", 2), ("o", 3), ("t", 2), ("t", 3), ("o", 0), ("o", 1))
SLOT = (0, 1, 2, 3, 4, 5, 6, 0, 2, 3, 4, 5)
S_SLOTS = 7
HALF = len(ORDER) // 2
N_MLP = 2 * HALF
N_ALL = N_MLP + 4
VEC_ROWS = 8
B_TICKS = {1: [("g_third", 4)], 6: [("second", 2)]}
C_TICKS = {
    0: (
        [("second", 3), ("second", 4), ("third", 2)],
        [(1, [("second", 5)])], [(1, [("third", 3)]), (3, [("second", 6)])], [(1, [("third", 4)])], [],
    ),
    1: (
        [],
        [(0, [("second", 3)])], [(1, [("third", 2)]), (3, [("second", 4)])], [(3, [("second", 5)])], [],
        [(1, [("third", 3)])], [(1, [("third", 4)]), (3, [("second", 6)])],
    ),
}
END_TICKS = [("third", 5)]
TAIL = [
    ("second", 8), ("vec", (0, 2)), ("third", 6), ("second", 7), ("vec", (0, 3)), ("third", 8), ("second", 9),
    ("vec", (1, 2)), ("third", 7), ("second", 10), ("vec", (1, 3)), ("third", 9), ("second", 11), ("third", 10),
    ("third", 11), ("fourth", 0), ("fourth", 1), ("fourth", 2), ("vec", (0, 4)), ("vec", (1, 4)),
]


def lookup(table, p):
    if isinstance(p, int):
        return table[p]
    value = jnp.int32(table[0])
    for n in range(1, len(table)):
        value = jnp.where(p == n, jnp.int32(table[n]), value)
    return value


def hidden_of(p):
    return lookup([b for _, b in ORDER], p)


def is_other(p):
    if isinstance(p, int):
        return ORDER[p][0] == "t"
    return lookup([int(s == "t") for s, _ in ORDER], p) == 1


def step_kernel(
    par_ref, qvb_ref, seg_ref, ubo_ref, x_hbm, g_hbm, wqkv_hbm, wout_hbm, up_own, down_own,
    out_ref, din_ref, mlp_ref, og_ref, qkvg_ref, vec_ref, a1_hbm, qkv_hbm, mix_hbm, up_oth, down_oth,
    wout_ref, mixt_ref, lse_ref, ubt_ref,
    dkv_ref, dm_ref, dsend_ref, send_ref, dq_ref, grad_ref, core_ref, sum_ref, ybuf, zbuf, xfirst, xsend, xbuf,
    vsum, vrecv,
    a_s, a_r, m_s, m_r, b_s, b_r, l_sem,
    c_s, c_r, y_s, y_r, z_s, z_r, xf_s, xf_r, x_s, x_r, v_s, v_r, dm_s, dm_r, o_s, o_r, out_sem, free_sem, *gather_sems,
):
    rows, width = din_ref.shape
    seq = 2 * rows
    local = dm_ref.shape[1]
    block = rows // 2
    piece = rows // 4
    hb = HIDDEN_BLOCK
    nx = CROSS_FIRST
    half, n_mlp, n_all = HALF, N_MLP, N_ALL
    z, y, core, side = place()
    partner = peer_x()
    own = pl.multiple_of(side * rows, rows)
    theirs = pl.multiple_of((1 - side) * rows, rows)
    scale = HEAD_DIM**-0.5
    vmem = pltpu.VMEM
    sem = pltpu.SemaphoreType.DMA

    def out_views(ref, dp):
        return [ref.at[dp // 4, dp // 2 % 2, pl.ds(dp % 2 * 32, 32)]]

    def gather_source(dp, q):
        return out_views(wout_hbm, dp) if q == 0 else hidden_views((up_own, down_own), dp, q - 1)

    def gather_target(dp, q):
        return out_views(wout_ref.at[1], dp) if q == 0 else hidden_views((up_oth, down_oth), dp, q - 1)

    g_first, g_second, g_third, g_last, g_sent, g_x = gather(gather_source, gather_target, gather_sems)

    def g_start(q):
        for copy in g_x(q):
            copy.start()

    def cols_of(p):
        return 2 * hb if p <= n_mlp else hb

    def slot_of(p):
        return lookup(SLOT, p)

    def core_copy(p, cols):
        slot = p % 2
        lanes = pl.ds(0, cols)
        return remote(
            grad_ref.at[slot, :, 1 - core, :, lanes], core_ref.at[slot, :, :, lanes], c_s.at[slot], c_r.at[slot],
            peer_core(),
        )

    def place_of(p, cols):
        if isinstance(p, int) and p > n_mlp:
            n = p - n_mlp - 1
            return n_mlp + 1 - nx + n // 2, pl.ds(n % 2 * hb, hb)
        return p - nx, pl.ds(0, cols)

    def y_copy(p, cols):
        s, lanes = place_of(p, cols)
        src = sum_ref.at[slot_of(p), :, 1 - y, :, pl.ds(0, cols)]
        return remote(src, ybuf.at[s, :, :, lanes], y_s.at[p - nx], y_r.at[p - nx], peer_y())

    def z_copy(p, k, cols):
        s, lanes = place_of(p, cols)
        src, dst = ybuf.at[s, (z + k) % 4, :, lanes], zbuf.at[s, k - 1, :, lanes]
        return remote(src, dst, z_s.at[p - nx, k - 1], z_r.at[p - nx, k - 1], peer_z(k))

    def xfirst_copy(p):
        return remote(sum_ref.at[slot_of(p)], xfirst.at[p], xf_s.at[p], xf_r.at[p], partner)

    def x_copy(n):
        lanes = pl.ds(0, 2 * hb if n < half - nx else hb)
        return remote(xsend.at[n, :, lanes], xbuf.at[n, :, lanes], x_s.at[n], x_r.at[n], partner)

    def produced(p, cols):
        @pl.when(p >= 2)
        def _():
            pl.semaphore_wait(free_sem, 1)

        core_copy(p, cols).start()

    def consume(p, cols):
        slot = p % 2
        lanes = pl.ds(0, cols)
        copy = core_copy(p, cols)
        copy.wait()
        if isinstance(p, int) and p > SLOT.index(SLOT[p]):
            sent(SLOT.index(SLOT[p]))
        total = grad_ref[slot, :, core, :, lanes].astype(F32) + core_ref[slot, :, :, lanes].astype(F32)
        at = sum_ref.at[slot_of(p), :, :, :, lanes]
        at[...] = total.astype(BF16).reshape(4, 2, 64, cols)

        @pl.when(p < n_all - 2)
        def _():
            pl.semaphore_signal(free_sem, inc=1, device_id=peer_core(), device_id_type=MESH)

    def sent(p):
        if p < nx:
            xfirst_copy(p).wait_send()
        else:
            y_copy(p, cols_of(p)).wait_send()

    def push(p, cols):
        if isinstance(p, int):
            if p < n_mlp and not is_other(p) and hidden_of(p) < nx:
                add_first(p)
            y_copy(p, cols).start()
            return

        @pl.when(p < nx)
        def _():
            xfirst_copy(p).start()

        @pl.when(p >= nx)
        def _():
            @pl.when(jnp.logical_not(is_other(p)) & (hidden_of(p) < nx))
            def _():
                add_first(p)

            y_copy(p, cols).start()

    def add_first(p):
        b = hidden_of(p)
        xfirst_copy(b).wait_recv()
        sum_ref[slot_of(p)] = (
            sum_ref[slot_of(p)].astype(F32) + xfirst[b].astype(F32)
        ).astype(BF16)

    def second(p):
        cols = cols_of(p)
        s, lanes = place_of(p, cols)
        y_copy(p, cols).wait_recv()
        ybuf[s, :, :, lanes] = (
            sum_ref[slot_of(p), :, y, :, pl.ds(0, cols)].astype(F32) + ybuf[s, :, :, lanes].astype(F32)
        ).astype(BF16)
        for k in (2, 1, 3):
            z_copy(p, k, cols).start()

    def third(p):
        cols = cols_of(p)
        s, lanes = place_of(p, cols)
        for k in (1, 2, 3):
            z_copy(p, k, cols).wait_recv()
        total = ybuf[s, z, :, lanes].astype(F32)
        for k in (1, 2, 3):
            total = total + zbuf[s, k - 1, :, lanes].astype(F32)
        if p < n_mlp and is_other(p):
            n = hidden_of(p) - nx
            xsend[n] = total.astype(BF16)
            x_copy(n).start()
        elif p < n_mlp:
            mlp_ref[hidden_of(p)] = total
        elif p == n_mlp:
            og_ref[...] = total[:, :hb]
            xsend[half - nx, :, pl.ds(0, hb)] = total[:, hb:].astype(BF16)
            x_copy(half - nx).start()
        else:
            qkvg_ref[p - n_mlp - 1] = total

    def fourth(n):
        x_copy(n).wait_recv()
        if n < half - nx:
            mlp_ref[n + nx] += xbuf[n].astype(F32)
        else:
            og_ref[...] += xbuf[n, :, pl.ds(0, hb)].astype(F32)

    def v_copy(w, n, peer, slot):
        return remote(vsum.at[w, n], vrecv.at[w, slot], v_s.at[w, slot], v_r.at[w, slot], peer)

    def z_vec(w, k, source):
        return remote(vsum.at[w, 2], vrecv.at[w, 2 + source], v_s.at[w, 2 + k], v_r.at[w, 2 + source], peer_z(k))

    def vectors(w, n):
        if n == 0:
            v_copy(w, 0, peer_core(), 0).start()
        elif n == 1:
            v_copy(w, 0, peer_core(), 0).wait()
            vsum[w, 1] = vsum[w, 0] + vrecv[w, 0]
            v_copy(w, 1, peer_y(), 1).start()
        elif n == 2:
            v_copy(w, 1, peer_y(), 1).wait()
            vsum[w, 2] = vsum[w, 1] + vrecv[w, 1]
            for k in (1, 2, 3):
                z_vec(w, k, z).start()
        elif n == 3:
            for k in (1, 2, 3):
                z_vec(w, k, z).wait_send()
                z_vec(w, k, (z + k) % 4).wait_recv()
            vrecv[w, 2 + z] = vsum[w, 2]
            vsum[w, 3] = (vrecv[w, 2] + vrecv[w, 3]) + (vrecv[w, 4] + vrecv[w, 5])
            v_copy(w, 3, partner, 6).start()
        elif n == 4:
            v_copy(w, 3, partner, 6).wait()
            vec_ref[pl.ds(w * VEC_ROWS, VEC_ROWS)] = vsum[w, 3] + vrecv[w, 6]

    stages = dict(
        second=second, third=third, fourth=fourth, g_first=g_first, g_second=g_second, g_third=g_third, g_last=g_last
    )

    def run(names):
        for name, arg in names:
            if name == "vec":
                vectors(*arg)
            else:
                stages[name](arg)

    dm_own = dm_ref.at[pl.ds(own, rows)]

    def dm_copy(b):
        at = pl.ds(pl.multiple_of(own + b * block, block), block)
        return remote(dsend_ref.at[b], dm_ref.at[at], dm_s.at[b], dm_r.at[b], partner)

    def dm_from(b):
        at = pl.ds(pl.multiple_of((1 - side) * rows + b * block, block), block)
        return remote(dsend_ref.at[b], dm_ref.at[at], dm_s.at[b], dm_r.at[b], partner)

    def out_copy(j):
        return pltpu.make_async_copy(send_ref.at[j], out_ref.at[j], out_sem.at[j])

    def o_copy(j):
        return remote(send_ref.at[j], xfirst.at[0, pl.ds(2 * j, 2)], o_s.at[j], o_r.at[j], partner)

    greet()
    bias_copy = remote(ubo_ref, ubt_ref, b_s, b_r, partner)
    a1_ref = sum_ref

    def a1_copy(which, b):
        return remote(a1_ref.at[which, b], a1_ref.at[which, b], a_s.at[b], a_r.at[b], partner)

    def wout_own():
        return wout_ref[0].reshape(local, width)

    def wout_other():
        return wout_ref[1].reshape(local, width)

    def ahead(x_ref, wqkv_ref, qkv_ref, mix_ref, mask_ref):
        loads = [
            pltpu.make_async_copy(src, dst, l_sem.at[n])
            for n, (src, dst) in enumerate(((x_hbm, x_ref), (wqkv_hbm, wqkv_ref), (wout_hbm, wout_ref.at[0])))
        ]
        for load in loads:
            load.start()
        g_start(0)
        g_start(1)
        gain = par_ref[pl.ds(GAIN_1, 1)]
        shift = par_ref[pl.ds(SHIFT_1, 1)]
        loads[0].wait()
        for b in range(4):
            xhat, _ = norm_parts(x_ref[pl.ds(b * piece, piece)].astype(F32))
            a1_ref[side, b] = (xhat * gain + shift).astype(BF16).reshape(2, 64, width)
            a1_copy(side, b).start()
            if b < 2:
                g_start(2 + b)
        bias_copy.start()
        g_start(4)

        def project(left, base, count):
            at = pl.ds(pl.multiple_of(base, block), count)
            for part in range(3):
                cols = pl.ds(part * local, local)
                value = dot_nn(left, wqkv_ref[:, cols])
                if part != 1:
                    value = value + qvb_ref[pl.ds(part // 2, 1)].astype(F32)
                qkv_ref[at, cols] = value.astype(BF16)

        loads[1].wait()
        project(a1_ref[side].reshape(rows, width), own, rows)

        def mix_copy(j):
            at = pl.ds(pl.multiple_of(theirs + j * block, block), block)
            far = mixt_ref.at[pl.ds(j * block, block)]
            return remote(mix_ref.at[at], far, m_s.at[j], m_r.at[j], partner)

        seg_row = seg_ref[...].astype(F32)
        seg_col = jnp.broadcast_to(seg_row, (8, seq)).T[:, :1]
        run([("g_first", 0), ("g_first", 1)])

        @pl.when(side == 1)
        def _():
            run([("g_second", 0)])

        for i in range(4):
            lo = i * block
            keys = lo + block
            is_theirs = side == (1 if i < 2 else 0)
            at = pl.ds(lo, block)
            if i == 1:

                @pl.when(side == 0)
                def _():
                    run([("g_second", 0)])

            @pl.when(is_theirs)
            def _():
                j = i % 2
                run([("g_first", 3), ("g_third", 1), ("g_second", 2)] if j else [("g_third", 0), ("g_first", 2), ("g_second", 1)])
                for b in (2 * j, 2 * j + 1):
                    a1_copy(1 - side, b).wait_recv()
                project(a1_ref[1 - side, pl.ds(2 * j, 2)].reshape(block, width), lo, block)

            same = seg_col[:keys] == seg_row[:, lo : lo + block]
            k_pos = lax.broadcasted_iota(jnp.int32, (keys, block), 0)
            q_pos = lo + lax.broadcasted_iota(jnp.int32, (keys, block), 1)
            mask_ref[pl.ds(0, keys)] = jnp.where(same & (q_pos >= k_pos), 0.0, -1e30)

            def pair(hp, _):
                base = pl.multiple_of(hp * 2 * HEAD_DIM, 2 * HEAD_DIM)
                cols = pl.ds(base, 2 * HEAD_DIM)
                q2 = qkv_ref[at, cols]
                k2 = qkv_ref[pl.ds(0, keys), pl.ds(pl.multiple_of(local + base, 128), 2 * HEAD_DIM)]
                v2 = qkv_ref[pl.ds(0, keys), pl.ds(pl.multiple_of(2 * local + base, 128), 2 * HEAD_DIM)]
                out = jnp.zeros((block, 2 * HEAD_DIM), F32)
                for h in range(2):
                    scores = dot_nt(k2, only_head(q2, h)) * scale + mask_ref[pl.ds(0, keys)]
                    top = jnp.max(scores, axis=0, keepdims=True)
                    weights = jnp.exp(scores - top)
                    total = total_of(weights)
                    lse_ref[pl.ds(2 * hp + h, 1), at] = top + jnp.log(total)
                    out += dot_tn((weights * (1.0 / total)).astype(BF16), only_head(v2, h))
                mix_ref[at, cols] = out.astype(BF16)
                return 0

            lax.fori_loop(0, local // (2 * HEAD_DIM), pair, 0)

            @pl.when(is_theirs)
            def _():
                mix_copy(i % 2).start()
                if i % 2:
                    run([("g_first", 4), ("g_third", 2), ("g_second", 3)])

        saves = [
            pltpu.make_async_copy(src, dst, l_sem.at[n])
            for n, (src, dst) in enumerate(((qkv_ref, qkv_hbm), (mix_ref, mix_hbm), (a1_ref.at[pl.ds(0, 2)], a1_hbm)), start=3)
        ]
        for save in saves:
            save.start()
        loads[2].wait()
        run([("g_third", 3), ("g_last", 0), ("g_second", 4)])
        for j in range(2):
            at = pl.ds(j * block, block)
            mix_copy(j).wait_recv()
            mine = dot_nn(mix_ref[pl.ds(pl.multiple_of(own + j * block, block), block)], wout_own())
            din_ref[at] = (
                x_ref[at].astype(F32) + (mine + dot_nn(mixt_ref[at], wout_other())) + par_ref[pl.ds(OUT_BIAS, 1)]
            )
        for save in saves:
            save.wait()
        for j in range(2):
            mix_copy(j).wait_send()
        for b in range(4):
            a1_copy(side, b).wait_send()
        bias_copy.wait()

    pl.run_scoped(
        ahead,
        vmem((rows, width), BF16), vmem((width, 3 * local), BF16), vmem((seq, 3 * local), BF16), vmem((seq, local), BF16),
        vmem((seq, block), F32),
    )

    h_ref = din_ref

    def feed(g_ref, a2_ref, a2t_ref, gt_ref, wu_ref, wd_ref, in_sem, w_sem):
        load_g = pltpu.make_async_copy(g_hbm, g_ref, in_sem)
        load_g.start()

        def fetch(b, up, down, slot):
            at = pl.ds(pl.multiple_of(b * hb, hb), hb)
            return (
                pltpu.make_async_copy(up.at[:, at], wu_ref.at[slot], w_sem.at[slot, 0]),
                pltpu.make_async_copy(down.at[at], wd_ref.at[slot], w_sem.at[slot, 1]),
            )

        def fetch_start(p, slot):
            for n in range(n_mlp):
                if is_other(n):

                    @pl.when(p == n)
                    def _():
                        g_last(1 + hidden_of(n))

            @pl.when(is_other(p))
            def _():
                for copy in fetch(hidden_of(p), up_oth, down_oth, slot):
                    copy.start()

            @pl.when(jnp.logical_not(is_other(p)))
            def _():
                for copy in fetch(hidden_of(p), up_own, down_own, slot):
                    copy.start()

        fetch_start(jnp.int32(0), 0)
        gain = par_ref[pl.ds(GAIN_2, 1)]
        xhat, _ = norm_parts(h_ref[...])
        a2 = (xhat * gain + par_ref[pl.ds(SHIFT_2, 1)]).astype(BF16)
        a2_ref[...] = a2
        a2t_ref[...] = a2.T
        load_g.wait()
        gt_ref[...] = g_ref[...].T
        dkv_ref[...] = jnp.zeros_like(dkv_ref)
        acc_ref = dkv_ref.at[pl.ds(0, rows)]
        da2_ref = dkv_ref.at[pl.ds(rows, rows)]

        def step(p, _):
            slot = p % 2
            for copy in fetch(0, up_own, down_own, slot):
                copy.wait()

            @pl.when(p + 1 < n_mlp)
            def _():
                fetch_start(p + 1, 1 - slot)

            b = hidden_of(p)
            wu, wd = wu_ref[slot], wd_ref[slot]
            u = dot_nn(a2_ref[...], wu) + jnp.where(is_other(p), ubt_ref[pl.ds(b, 1)], ubo_ref[pl.ds(b, 1)])
            tanh = jnp.tanh(0.7978845608028654 * (u + 0.044715 * u * u * u))
            hidden = (0.5 * u * (1.0 + tanh)).astype(BF16)
            slope = 0.5 * (1.0 + tanh) + 0.5 * u * (1.0 - tanh * tanh) * (
                0.7978845608028654 * (1.0 + 3.0 * 0.044715 * u * u)
            )
            acc_ref[...] += dot_nn(hidden, wd)
            du = (dot_nt(g_ref[...], wd) * slope).astype(BF16)
            where_side = jnp.where(is_other(p), 1 - side, side)
            lanes = pl.ds(pl.multiple_of((b % 2) * hb, hb), hb)
            vsum[0, 0, pl.ds(4 + where_side * (half // 2) + b // 2, 1), lanes] = total_of(du.astype(F32))
            da2_ref[...] += dot_nt(du, wu)
            grad_ref[slot, :, :, :, pl.ds(0, hb)] = dot_nn(a2t_ref[...], du).astype(BF16).reshape(8, 2, 64, hb)
            grad_ref[slot, :, :, :, pl.ds(hb, hb)] = dot_nn(gt_ref[...], hidden).astype(BF16).reshape(8, 2, 64, hb)
            produced(p, 2 * hb)

            for n, names in B_TICKS.items():

                @pl.when(p == n)
                def _():
                    run(names)

            @pl.when(p >= 1)
            def _():
                consume(p - 1, 2 * hb)
                push(p - 1, 2 * hb)

            return 0

        vsum[0, 0] = jnp.zeros(vsum.shape[2:], F32)
        vsum[1, 0] = jnp.zeros(vsum.shape[2:], F32)
        lax.fori_loop(0, n_mlp, step, 0)

        piece = rows // 4
        sums = [jnp.zeros((1, width), F32) for _ in range(4)]
        for b in range(4):
            at = pl.ds(b * piece, piece)
            h = h_ref[at]
            g = g_ref[at].astype(F32)
            out = (h + acc_ref[at] + par_ref[pl.ds(DOWN_BIAS, 1)]).astype(BF16)
            send_ref[b // 2, b % 2] = out.reshape(2, 64, width)
            xhat, rstd = norm_parts(h)
            da2 = da2_ref[at]
            dh = g + norm_back(da2, gain, xhat, rstd)
            din_ref[at] = dh
            for n, term in enumerate((da2 * xhat, da2, dh.astype(BF16).astype(F32), g)):
                sums[n] = sums[n] + total_of(term)
        for n in range(4):
            vsum[0, 0, pl.ds(n, 1)] = sums[n]
        vectors(0, 0)
        for j in range(2):
            out_copy(j).start()

    pl.run_scoped(
        feed,
        vmem((rows, width), BF16), vmem((rows, width), BF16), vmem((width, rows), BF16),
        vmem((width, rows), BF16), vmem((2, width, hb), BF16), vmem((2, hb, width), BF16), sem, sem((2, 2)),
    )

    def attend(qkv_ref, mix_ref, wqkv_ref, mask_ref, dhl_ref, in_sem):
        x_ref, dqkv_ref = dhl_ref, qkv_ref
        moves = [
            pltpu.make_async_copy(src, dst, in_sem.at[n])
            for n, (src, dst) in enumerate((
                (mix_hbm, mix_ref), (qkv_hbm, qkv_ref), (wqkv_hbm, wqkv_ref), (x_hbm, x_ref), (a1_hbm, wout_ref),
            ))
        ]
        for move in moves[:3]:
            move.start()
        dhl_ref[...] = din_ref[...].astype(BF16)
        consume(n_mlp - 1, 2 * hb)
        for b in (1, 0):
            dsend_ref[b] = dot_nt(dhl_ref[pl.ds(b * block, block)], wout_other()).astype(BF16)
            dm_copy(b).start()
        dm_own[...] = dot_nt(dhl_ref[...], wout_own()).astype(BF16)
        g_sent(0)
        moves[4].start()
        moves[0].wait()
        p = n_mlp
        for part in range(2):
            mixed = mixt_ref[...] if part else mix_ref[pl.ds(own, rows)]
            grad = dot_tn(dhl_ref[...], mixed).astype(BF16)
            grad_ref[p % 2, :, :, :, pl.ds(part * hb, hb)] = grad.reshape(8, 2, 64, hb)
        produced(p, 2 * hb)
        moves[3].start()
        dkv_ref[...] = jnp.zeros_like(dkv_ref)
        seg_row = seg_ref[...].astype(F32)
        seg_col = jnp.broadcast_to(seg_row, (8, seq)).T[:, :1]
        moves[1].wait()
        for j in range(2):
            out_copy(j).wait()

        def task(i, keys, stage="all", ticks=()):
            lo, start, count = i * block, keys[0], keys[1] - keys[0]
            at, among = pl.ds(lo, block), pl.ds(start, count)
            same = seg_col[start : start + count] == seg_row[:, lo : lo + block]
            k_pos = start + lax.broadcasted_iota(jnp.int32, (count, block), 0)
            q_pos = lo + lax.broadcasted_iota(jnp.int32, (count, block), 1)
            mask_ref[pl.ds(0, count)] = jnp.where(same & (q_pos >= k_pos), 0.0, -1e30)

            def pair(hp, _):
                base = pl.multiple_of(hp * 2 * HEAD_DIM, 2 * HEAD_DIM)
                cols = pl.ds(base, 2 * HEAD_DIM)
                v_cols = pl.ds(pl.multiple_of(local + base, 128), 2 * HEAD_DIM)
                q2 = qkv_ref[at, cols]
                k2 = qkv_ref[among, v_cols]
                v2 = qkv_ref[among, pl.ds(pl.multiple_of(2 * local + base, 128), 2 * HEAD_DIM)]
                g2 = dm_ref[at, cols]
                turned = (g2.astype(F32) * mix_ref[at, cols].astype(F32)).T
                dq = jnp.zeros((block, 2 * HEAD_DIM), F32)
                dk = jnp.zeros((count, 2 * HEAD_DIM), F32)
                dv = jnp.zeros((count, 2 * HEAD_DIM), F32)
                for h in range(2):
                    qh = only_head(q2, h)
                    gh = only_head(g2, h)
                    row_dot = total_of(turned[h * HEAD_DIM : (h + 1) * HEAD_DIM])
                    offset = mask_ref[pl.ds(0, count)] - lse_ref[pl.ds(2 * hp + h, 1), at]
                    probs = jnp.exp(dot_nt(k2, qh) * scale + offset)
                    dscore = (probs * (dot_nt(v2, gh) - row_dot)).astype(BF16)
                    dv += dot_nn(probs.astype(BF16), gh)
                    dk += dot_nn(dscore, qh)
                    dq += dot_tn(dscore, only_head(k2, h))
                if stage == "first":
                    dq_ref[i - 2, :, cols] = dq
                else:
                    if stage == "last":
                        dq = dq + dq_ref[i - 2, :, cols]
                    dqkv_ref[at, cols] = (dq * scale).astype(BF16)
                dkv_ref[among, cols] += dk
                dkv_ref[among, v_cols] += dv
                for n, names in ticks:

                    @pl.when(hp == n)
                    def _():
                        run(names)

                return 0

            lax.fori_loop(0, local // (2 * HEAD_DIM), pair, 0)

        def finish(i, send):
            at = pl.ds(i * block, block)
            dqkv_ref[at, pl.ds(local, local)] = (dkv_ref[at, pl.ds(0, local)] * scale).astype(BF16)
            dqkv_ref[at, pl.ds(2 * local, local)] = dkv_ref[at, pl.ds(local, local)].astype(BF16)
            product = dot_nt(dqkv_ref[at], wqkv_ref[...])
            if send:
                send_ref[i % 2] = product.astype(BF16).reshape(send_ref.shape[1:])
                o_copy(i % 2).start()
            else:
                dkv_ref[at] = product

        def second_block():
            consume(n_mlp, 2 * hb)
            push(n_mlp, 2 * hb)
            push(n_mlp - 1, 2 * hb)
            vectors(0, 1)
            moves[2].wait()

        @pl.when(side == 0)
        def _():
            run(C_TICKS[0][0])
            dm_from(1).wait_recv()
            task(3, (0, 4 * block), ticks=C_TICKS[0][1])
            second_block()
            finish(3, True)
            dm_from(0).wait_recv()
            task(2, (0, 3 * block), ticks=C_TICKS[0][2])
            finish(2, True)
            task(1, (0, 2 * block), ticks=C_TICKS[0][3])
            finish(1, False)
            task(0, (0, block), ticks=C_TICKS[0][4])
            finish(0, False)

        @pl.when(side == 1)
        def _():
            task(3, (0, 2 * block), "first", ticks=C_TICKS[1][1])
            task(2, (0, 2 * block), "first", ticks=C_TICKS[1][2])
            second_block()
            dm_from(1).wait_recv()
            task(1, (0, 2 * block), ticks=C_TICKS[1][3])
            finish(1, True)
            dm_from(0).wait_recv()
            task(0, (0, block), ticks=C_TICKS[1][4])
            finish(0, True)
            task(3, (2 * block, 4 * block), "last", ticks=C_TICKS[1][5])
            finish(3, False)
            task(2, (2 * block, 3 * block), "last", ticks=C_TICKS[1][6])
            finish(2, False)

        moves[4].wait()
        for part in range(3):
            p = n_mlp + 1 + part
            grad = dot_tn(wout_ref[...].reshape(seq, width), dqkv_ref[:, pl.ds(part * local, local)]).astype(BF16)
            grad_ref[p % 2, :, :, :, pl.ds(0, hb)] = grad.reshape(8, 2, 64, hb)
            produced(p, hb)
            if part == 1:
                consume(p - 1, hb)
                push(p - 1, hb)
        moves[3].wait()

        def finish_rows(j):
            at = pl.ds(j * block, block)
            o_copy(j).wait_recv()
            da1 = dkv_ref[pl.ds(pl.multiple_of(own + j * block, block), block)] + xfirst[0, pl.ds(2 * j, 2)].reshape(
                block, width
            ).astype(F32)
            xhat, rstd = norm_parts(x_ref[at].astype(F32))
            din_ref[at] += norm_back(da1, par_ref[pl.ds(GAIN_1, 1)], xhat, rstd)
            return total_of(da1 * xhat), total_of(da1)

        lanes = pl.ds(pl.multiple_of(side * local, local), local)
        vsum[1, 0, pl.ds(2, 1), lanes] = total_of(dqkv_ref[:, pl.ds(0, local)].astype(F32))
        vsum[1, 0, pl.ds(3, 1), lanes] = total_of(dqkv_ref[:, pl.ds(2 * local, local)].astype(F32))
        gain_1, shift_1 = finish_rows(1)
        consume(n_mlp + 2, hb)
        run(END_TICKS)
        consume(n_mlp + 3, hb)
        gain_0, shift_0 = finish_rows(0)
        vsum[1, 0, pl.ds(0, 1)] = gain_0 + gain_1
        vsum[1, 0, pl.ds(1, 1)] = shift_0 + shift_1
        vectors(1, 0)
        vectors(1, 1)
        push(n_mlp + 2, hb)
        push(n_mlp + 3, hb)

    pl.run_scoped(
        attend,
        vmem((seq, 3 * local), BF16), vmem((seq, local), BF16), vmem((width, 3 * local), BF16), vmem((seq, block), F32),
        vmem((rows, width), BF16), sem((5,)),
    )

    run(TAIL)
    for q in range(1, half + 1):
        g_sent(q)
    for j in range(2):
        dm_copy(j).wait_send()
        o_copy(j).wait_send()
    for p in range(n_all):
        if p in (1, *range(6, n_all)):
            sent(p)
    for p in range(nx, n_all):
        for k in (1, 2, 3):
            z_copy(p, k, cols_of(p)).wait_send()
    for n in range(half - nx + 1):
        x_copy(n).wait_send()


def step_call(par, qvb, seg, ubo, x, g, wqkv, wout, up, down):
    rows, width = x.shape
    local = wout.size // width
    seq = 2 * rows
    block = rows // 2
    hb = HIDDEN_BLOCK
    nx = CROSS_FIRST
    height = width // PIECES
    vm = pl.BlockSpec(memory_space=pltpu.VMEM)
    hbm = pl.BlockSpec(memory_space=pltpu.HBM)
    sem = pltpu.SemaphoreType.DMA
    ny = N_ALL - nx
    nxl = HALF - nx + 1
    shape = jax.ShapeDtypeStruct
    return pl.pallas_call(
        step_kernel,
        out_shape=(
            shape((2, 2, 2, height, width), BF16),
            shape((rows, width), F32),
            shape((HALF, height, 2 * hb), F32),
            shape((height, local), F32),
            shape((3, height, local), F32),
            shape((2 * VEC_ROWS, width), F32),
            shape((2, 4, 2, height, width), BF16),
            shape((seq, 3 * local), BF16),
            shape((seq, local), BF16),
            shape(up.shape, BF16),
            shape(down.shape, BF16),
        ),
        in_specs=[vm] * 4 + [hbm] * 6,
        out_specs=(hbm,) + (vm,) * 5 + (hbm,) * 5,
        scratch_shapes=[
            pltpu.VMEM((2, 4, 2, height, width), BF16),
            pltpu.VMEM((rows, local), BF16),
            pltpu.VMEM((local // HEAD_DIM, seq), F32),
            pltpu.VMEM(ubo.shape, F32),
            pltpu.VMEM((seq, width), F32),
            pltpu.VMEM((seq, local), BF16),
            pltpu.VMEM((2, block, local), BF16),
            pltpu.VMEM((2, 2, 2, height, width), BF16),
            pltpu.VMEM((2, block, local), F32),
            pltpu.VMEM((2, 8, 2, height, 2 * hb), BF16),
            pltpu.VMEM((2, 8, height, 2 * hb), BF16),
            pltpu.VMEM((S_SLOTS, 4, 2, height, 2 * hb), BF16),
            pltpu.VMEM((ny - 1, 4, height, 2 * hb), BF16),
            pltpu.VMEM((ny - 1, 3, height, 2 * hb), BF16),
            pltpu.VMEM((nx, 4, 2, height, 2 * hb), BF16),
            pltpu.VMEM((nxl, height, 2 * hb), BF16),
            pltpu.VMEM((nxl, height, 2 * hb), BF16),
            pltpu.VMEM((2, 4, VEC_ROWS, width), F32),
            pltpu.VMEM((2, 7, VEC_ROWS, width), F32),
            sem((4,)), sem((4,)), sem((2,)), sem((2,)), sem, sem, sem((6,)),
            sem((2,)), sem((2,)), sem((ny,)), sem((ny,)), sem((ny, 3)), sem((ny, 3)),
            sem((nx,)), sem((nx,)), sem((nxl,)), sem((nxl,)), sem((2, 7)), sem((2, 7)),
            sem((2,)), sem((2,)), sem((2,)), sem((2,)), sem((2,)), pltpu.SemaphoreType.REGULAR,
            *gather_semaphores(1 + HALF),
        ],
        compiler_params=pltpu.CompilerParams(
            collective_id=0, has_side_effects=True, vmem_limit_bytes=VMEM_LIMIT
        ),
        name="train_step",
    )(par, qvb, seg, ubo, x, g, wqkv, wout, up, down)


def on_device_pair(
    inputs, segment_ids, first_gain, first_shift, qkv_weight, qv_bias, out_weight, out_bias,
    second_gain, second_shift, up_weight, up_bias, down_weight, down_bias, cotangent,
):
    rows, _, width = inputs.shape
    seq = segment_ids.shape[0]
    local = out_weight.shape[0]
    hidden = up_weight.shape[1]
    side = lax.axis_index("tensor")
    x = inputs.reshape(rows, width)
    g = cotangent.reshape(rows, width)
    seg = segment_ids.reshape(1, seq)
    wqkv = qkv_weight.reshape(width, 3 * local)
    par = jnp.stack([first_gain, first_shift, out_bias, second_gain, second_shift, down_bias]).astype(F32)
    half = hidden // HIDDEN_BLOCK
    ubo = jnp.pad(up_bias.astype(F32).reshape(half, HIDDEN_BLOCK), ((0, 8 - half), (0, 0)))
    height = width // PIECES
    wout = out_weight.reshape(4, 2, height, width)
    layer_output, input_grad, mlp, out_g, qkv_g, total = step_call(
        par, qv_bias, seg, ubo, x, g, wqkv, wout, up_weight, down_weight
    )[:6]
    up_share = jnp.transpose(mlp[:, :, :HIDDEN_BLOCK], (1, 0, 2)).reshape(height, hidden)
    down_share = jnp.transpose(mlp[:, :, HIDDEN_BLOCK:], (0, 2, 1)).reshape(hidden, height)
    qkv_share = jnp.transpose(qkv_g, (1, 0, 2))
    out_share = out_g.T
    qv_share = lax.dynamic_slice_in_dim(total[10:12], side * local, local, 1)
    up_bias_share = lax.dynamic_slice_in_dim(total[4:8].reshape(2 * hidden), side * hidden, hidden, 0)
    return (
        layer_output.reshape(rows, 1, width),
        input_grad.reshape(rows, 1, width),
        total[8],
        total[9],
        qkv_share,
        qv_share,
        out_share,
        total[2],
        total[0],
        total[1],
        up_share,
        up_bias_share,
        down_share,
        total[3],
    )


def solution(mesh):
    in_specs = (
        P("tensor", "dp", None),
        P(None, "dp"),
        P(),
        P(),
        P(None, None, "tensor"),
        P(None, "tensor"),
        P("tensor", None),
        P(),
        P(),
        P(),
        P(None, "tensor"),
        P("tensor"),
        P("tensor", None),
        P(),
        P("tensor", "dp", None),
    )
    out_specs = (
        P("tensor", "dp", None),
        P("tensor", "dp", None),
        P(),
        P(),
        P("dp", None, "tensor"),
        P(None, "tensor"),
        P("tensor", "dp"),
        P(),
        P(),
        P(),
        P("dp", "tensor"),
        P("tensor"),
        P("tensor", "dp"),
        P(),
    )
    pair = mesh.shape["tensor"] == 2 and mesh.shape["dp"] == Z_SIZE * Y_SIZE * CORES
    return jax.shard_map(
        on_device_pair if pair else on_device, mesh=mesh, in_specs=in_specs, out_specs=out_specs, check_vma=False
    )
```

```python
import functools

import jax
import jax.numpy as jnp
from jax import lax
from jax.experimental import pallas as pl
from jax.experimental.pallas import tpu as pltpu
from jax.sharding import PartitionSpec as P

HEAD_DIM = 64
MESH = pl.DeviceIdType.MESH
F32 = jnp.float32
BF16 = jnp.bfloat16
VMEM_LIMIT = 63 << 20


norm_eps = 1e-05


def layer_norm(value, gain, shift):
    row_mean = jnp.mean(value, axis=-1, keepdims=True)
    centred = value - row_mean
    variance = jnp.mean(centred * centred, axis=-1, keepdims=True)
    return centred * lax.rsqrt(variance + norm_eps) * gain + shift


def gelu_tanh(value):
    return (
        0.5
        * value
        * (1.0 + jnp.tanh(0.7978845608028654 * (value + 0.044715 * value * value * value)))
    )


def masked_scores(query_block, keys_all, seg_block, seg_all, row_start, block_rows, score_scale):
    scores = (
        jnp.einsum("qhd,khd->hqk", query_block, keys_all, preferred_element_type=jnp.float32)
        * score_scale
    )
    key_pos = jnp.arange(keys_all.shape[0], dtype=jnp.int32)
    query_pos = row_start + jnp.arange(block_rows, dtype=jnp.int32)
    allowed = (seg_block[:, None] == seg_all[None, :]) & (query_pos[:, None] >= key_pos[None, :])
    return jnp.where(allowed[None], scores, -1e30)


def attend_forward(queries, keys_all, values_all, seg_all, score_scale):
    seq_len = queries.shape[0]
    block_rows = min(512, seq_len)

    def one_block(block_index):
        row_start = block_index * block_rows
        query_block = lax.dynamic_slice_in_dim(queries, row_start, block_rows, 0)
        seg_block = lax.dynamic_slice_in_dim(seg_all, row_start, block_rows, 0)
        scores = masked_scores(
            query_block, keys_all, seg_block, seg_all, row_start, block_rows, score_scale
        )
        row_top = jnp.max(scores, axis=-1, keepdims=True)
        weights = jnp.exp(scores - row_top)
        row_total = jnp.sum(weights, axis=-1, keepdims=True)
        probs_low = (weights / row_total).astype(jnp.bfloat16)
        mixed = jnp.einsum(
            "hqk,khd->qhd", probs_low, values_all, preferred_element_type=jnp.float32
        )
        return (mixed, row_top + jnp.log(row_total))

    mixed, log_total = lax.map(one_block, jnp.arange(seq_len // block_rows, dtype=jnp.int32))
    return (mixed.reshape(seq_len, -1), log_total)


def attend_backward(queries, keys_all, values_all, seg_all, log_total, out_grad, score_scale):
    seq_len = queries.shape[0]
    block_rows = min(512, seq_len)

    def one_block(carry, block_index):
        key_grad, value_grad = carry
        row_start = block_index * block_rows
        query_block = lax.dynamic_slice_in_dim(queries, row_start, block_rows, 0)
        seg_block = lax.dynamic_slice_in_dim(seg_all, row_start, block_rows, 0)
        grad_block = lax.dynamic_slice_in_dim(out_grad, row_start, block_rows, 0)
        scores = masked_scores(
            query_block, keys_all, seg_block, seg_all, row_start, block_rows, score_scale
        )
        probs = jnp.exp(scores - log_total[block_index])
        probs_low = probs.astype(jnp.bfloat16)
        value_grad = value_grad + jnp.einsum(
            "hqk,qhd->khd", probs_low, grad_block, preferred_element_type=jnp.float32
        )
        prob_grad = jnp.einsum(
            "qhd,khd->hqk", grad_block, values_all, preferred_element_type=jnp.float32
        )
        row_dot = jnp.sum(probs * prob_grad, axis=-1, keepdims=True)
        score_grad = (probs * (prob_grad - row_dot)).astype(jnp.bfloat16)
        query_grad = (
            jnp.einsum("hqk,khd->qhd", score_grad, keys_all, preferred_element_type=jnp.float32)
            * score_scale
        )
        key_grad = (
            key_grad
            + jnp.einsum(
                "hqk,qhd->khd", score_grad, query_block, preferred_element_type=jnp.float32
            )
            * score_scale
        )
        return ((key_grad, value_grad), query_grad)

    zero_grads = jnp.zeros(keys_all.shape, jnp.float32)
    (key_grad, value_grad), query_grad = lax.scan(
        one_block, (zero_grads, zero_grads), jnp.arange(seq_len // block_rows, dtype=jnp.int32)
    )
    return (
        query_grad.reshape(seq_len, -1),
        key_grad.reshape(seq_len, -1),
        value_grad.reshape(seq_len, -1),
    )


def row_product(left, right, contract):
    return lax.dot_general(
        left, right, (((1,), (contract,)), ((), ())), preferred_element_type=jnp.float32
    )


def rows_contract(left, right):
    return lax.dot_general(
        left, right, (((0,), (0,)), ((), ())), preferred_element_type=jnp.float32
    )


def on_device(
    inputs,
    segment_ids,
    first_gain,
    first_shift,
    qkv_weight,
    qv_bias,
    out_weight,
    out_bias,
    second_gain,
    second_shift,
    up_weight,
    up_bias,
    down_weight,
    down_bias,
    cotangent,
):
    rows_dev, seq_count, model_width = inputs.shape
    tensor_count = lax.axis_size("tensor")
    tensor_rank = lax.axis_index("tensor")
    seq_len = rows_dev * tensor_count
    local_width = out_weight.shape[0]
    heads_dev = local_width // HEAD_DIM
    hidden_dev = up_weight.shape[1]
    local_rows = rows_dev * seq_count
    score_scale = HEAD_DIM ** (-0.5)
    residual_in = inputs.reshape(local_rows, model_width).astype(jnp.float32)
    gain_one = first_gain.astype(jnp.float32)
    shift_one = first_shift.astype(jnp.float32)
    gain_two = second_gain.astype(jnp.float32)
    shift_two = second_shift.astype(jnp.float32)
    normed_one, pull_one = jax.vjp(layer_norm, residual_in, gain_one, shift_one)
    first_local = normed_one.astype(jnp.bfloat16)
    first_rows = lax.all_gather(first_local, "tensor", axis=0, tiled=True)
    qkv_flat = qkv_weight.reshape(model_width, 3 * local_width)
    qkv_bias = jnp.concatenate(
        [
            qv_bias[0].astype(jnp.float32),
            jnp.zeros((local_width,), jnp.float32),
            qv_bias[1].astype(jnp.float32),
        ]
    )
    qkv_low = (jnp.dot(first_rows, qkv_flat, preferred_element_type=jnp.float32) + qkv_bias).astype(
        jnp.bfloat16
    )
    qkv_split = qkv_low.reshape(seq_len, seq_count, 3, heads_dev, HEAD_DIM)
    seq_index = 0
    mixed_one, log_one = attend_forward(
        qkv_split[:, seq_index, 0],
        qkv_split[:, seq_index, 1],
        qkv_split[:, seq_index, 2],
        segment_ids[:, seq_index],
        score_scale,
    )
    mixed_list = [mixed_one]
    log_list = [log_one]
    mixed_low = (
        jnp.stack(mixed_list, axis=1).reshape(seq_len * seq_count, local_width).astype(jnp.bfloat16)
    )
    attn_local = lax.psum_scatter(
        row_product(mixed_low, out_weight, 0), "tensor", scatter_dimension=0, tiled=True
    )
    residual_mid = residual_in + attn_local + out_bias.astype(jnp.float32)
    normed_two, pull_two = jax.vjp(layer_norm, residual_mid, gain_two, shift_two)
    second_local = normed_two.astype(jnp.bfloat16)
    second_rows = lax.all_gather(second_local, "tensor", axis=0, tiled=True)
    hidden_pre = jnp.dot(
        second_rows, up_weight, preferred_element_type=jnp.float32
    ) + up_bias.astype(jnp.float32)
    activated, pull_gelu = jax.vjp(gelu_tanh, hidden_pre)
    hidden_low = activated.astype(jnp.bfloat16)
    mlp_local = lax.psum_scatter(
        row_product(hidden_low, down_weight, 0).astype(jnp.bfloat16),
        "tensor",
        scatter_dimension=0,
        tiled=True,
    ).astype(jnp.float32)
    layer_output = (residual_mid + mlp_local + down_bias.astype(jnp.float32)).astype(jnp.bfloat16)
    layer_output = layer_output.reshape(rows_dev, seq_count, model_width)
    grad_local = cotangent.reshape(local_rows, model_width)
    grad_rows = lax.all_gather(grad_local, "tensor", axis=0, tiled=True)
    down_grad = rows_contract(hidden_low, grad_rows)
    hidden_grad = lax.dot_general(
        grad_rows, down_weight, (((1,), (1,)), ((), ())), preferred_element_type=jnp.float32
    )
    (pre_grad,) = pull_gelu(hidden_grad)
    pre_low = pre_grad.astype(jnp.bfloat16)
    up_sums = jnp.sum(pre_low, axis=0, dtype=jnp.float32)
    second_back = lax.all_gather(second_local, "tensor", axis=0, tiled=True)
    up_grad = rows_contract(second_back, pre_low)
    second_norm_grad = lax.psum_scatter(
        row_product(pre_low, up_weight, 1), "tensor", scatter_dimension=0, tiled=True
    )
    mid_from_norm, gain_two_grad, shift_two_grad = pull_two(second_norm_grad)
    residual_grad = grad_local.astype(jnp.float32) + mid_from_norm
    residual_low = residual_grad.astype(jnp.bfloat16)
    residual_rows = lax.all_gather(residual_low, "tensor", axis=0, tiled=True)
    out_grad_weight = rows_contract(mixed_low, residual_rows)
    mixed_grad = lax.dot_general(
        residual_rows, out_weight, (((1,), (1,)), ((), ())), preferred_element_type=jnp.float32
    ).astype(jnp.bfloat16)
    mixed_grad = mixed_grad.reshape(seq_len, seq_count, heads_dev, HEAD_DIM)
    seq_index = 0
    query_grad, key_grad, value_grad = attend_backward(
        qkv_split[:, seq_index, 0],
        qkv_split[:, seq_index, 1],
        qkv_split[:, seq_index, 2],
        segment_ids[:, seq_index],
        log_list[seq_index],
        mixed_grad[:, seq_index],
        score_scale,
    )
    query_list = [query_grad]
    key_list = [key_grad]
    value_list = [value_grad]
    qkv_grad = jnp.concatenate(
        [jnp.stack(query_list, axis=1), jnp.stack(key_list, axis=1), jnp.stack(value_list, axis=1)],
        axis=-1,
    )
    qkv_grad_low = qkv_grad.reshape(seq_len * seq_count, 3 * local_width).astype(jnp.bfloat16)
    qkv_sums = jnp.sum(qkv_grad_low, axis=0, dtype=jnp.float32)
    qv_sums = jnp.stack([qkv_sums[:local_width], qkv_sums[2 * local_width :]], axis=0)
    first_back = lax.all_gather(first_local, "tensor", axis=0, tiled=True)
    qkv_grad_weight = rows_contract(first_back, qkv_grad_low).reshape(model_width, 3, local_width)
    first_norm_grad = lax.psum_scatter(
        row_product(qkv_grad_low, qkv_flat, 1), "tensor", scatter_dimension=0, tiled=True
    )
    in_from_norm, gain_one_grad, shift_one_grad = pull_one(first_norm_grad)
    input_grad = (residual_grad + in_from_norm).reshape(rows_dev, seq_count, model_width)
    qkv_share, out_share, up_share, down_share = (
        lax.psum_scatter(qkv_grad_weight, "dp", scatter_dimension=0, tiled=True),
        lax.psum_scatter(out_grad_weight, "dp", scatter_dimension=1, tiled=True),
        lax.psum_scatter(up_grad, "dp", scatter_dimension=0, tiled=True),
        lax.psum_scatter(down_grad, "dp", scatter_dimension=1, tiled=True),
    )
    out_bias_part = jnp.sum(residual_low, axis=0, dtype=jnp.float32)
    down_bias_part = jnp.sum(grad_local, axis=0, dtype=jnp.float32)
    stacked = jnp.stack(
        [
            gain_one_grad,
            shift_one_grad,
            gain_two_grad,
            shift_two_grad,
            out_bias_part,
            down_bias_part,
        ],
        axis=0,
    )
    qv_full = lax.dynamic_update_slice(
        jnp.zeros((2, model_width), jnp.float32), qv_sums, (jnp.int32(0), tensor_rank * local_width)
    )
    up_full = lax.dynamic_update_slice(
        jnp.zeros((hidden_dev * tensor_count,), jnp.float32), up_sums, (tensor_rank * hidden_dev,)
    )
    stacked, qv_total, up_total = lax.psum((stacked, qv_full, up_full), ("dp", "tensor"))
    qv_share = lax.dynamic_slice_in_dim(qv_total, tensor_rank * local_width, local_width, 1)
    up_bias_share = lax.dynamic_slice_in_dim(up_total, tensor_rank * hidden_dev, hidden_dev, 0)
    return (
        layer_output,
        input_grad,
        stacked[0],
        stacked[1],
        qkv_share,
        qv_share,
        out_share,
        stacked[4],
        stacked[2],
        stacked[3],
        up_share,
        up_bias_share,
        down_share,
        stacked[5],
    )


Z_SIZE, Y_SIZE, CORES = 4, 2, 2


def place():
    dp = lax.axis_index("dp")
    side = lax.axis_index("tensor")
    return dp // 4, (dp // 2) % 2, dp % 2, side


def dev(z, y, core, side):
    return (z * 4 + y * 2 + core, side)


def peer_x():
    z, y, core, side = place()
    return dev(z, y, core, 1 - side)


def peer_y():
    z, y, core, side = place()
    return dev(z, 1 - y, core, side)


def peer_core():
    z, y, core, side = place()
    return dev(z, y, 1 - core, side)


def peer_z(step):
    z, y, core, side = place()
    return dev((z + step) % 4, y, core, side)


def greet():
    peers = [peer_x(), peer_y(), peer_core()] + [peer_z(k) for k in (1, 2, 3)]
    barrier = pltpu.get_barrier_semaphore()
    for peer in peers:
        pl.semaphore_signal(barrier, inc=1, device_id=peer, device_id_type=MESH)
    pl.semaphore_wait(barrier, len(peers))


def remote(src, dst, send_sem, recv_sem, peer):
    return pltpu.make_async_remote_copy(
        src_ref=src, dst_ref=dst, send_sem=send_sem, recv_sem=recv_sem, device_id=peer, device_id_type=MESH
    )


def dot_nn(a, b):
    return lax.dot_general(a, b, (((1,), (0,)), ((), ())), preferred_element_type=F32)


def dot_nt(a, b):
    return lax.dot_general(a, b, (((1,), (1,)), ((), ())), preferred_element_type=F32)


def dot_tn(a, b):
    return lax.dot_general(a, b, (((0,), (0,)), ((), ())), preferred_element_type=F32)


def norm_parts(value):
    mean = jnp.mean(value, axis=-1, keepdims=True)
    centred = value - mean
    rstd = lax.rsqrt(jnp.mean(centred * centred, axis=-1, keepdims=True) + norm_eps)
    return centred * rstd, rstd


def norm_back(grad, gain, xhat, rstd):
    e = grad * gain
    return rstd * (e - jnp.mean(e, axis=-1, keepdims=True) - xhat * jnp.mean(e * xhat, axis=-1, keepdims=True))


def head_lanes(h):
    lane = lax.broadcasted_iota(jnp.int32, (1, 2 * HEAD_DIM), 1)
    return (lane // HEAD_DIM) == h


def only_head(value, h):
    return jnp.where(head_lanes(h), value, jnp.zeros_like(value))


def total_of(row):
    return jnp.sum(row, axis=0, keepdims=True)


GAIN_1, SHIFT_1, OUT_BIAS, GAIN_2, SHIFT_2, DOWN_BIAS = range(6)
PIECES = 16
HIDDEN_BLOCK = 512


def gather(source, target, sems):
    x_s, x_r, z_s, z_r, y_s, y_r, c_s, c_r = sems
    z, y, core, side = place()

    def copies(dp, q, send, recv, peer, views=target):
        pairs = zip(views(dp, q), target(dp, q))
        return [remote(s, d, send.at[a], recv.at[a], peer) for a, (s, d) in enumerate(pairs)]

    def number(zz, yy, cc):
        return zz * 4 + yy * 2 + cc

    def from_z(k):
        return (z + 4 - k) % 4

    def x_copies(q):
        return copies(number(z, y, core), q, x_s.at[q], x_r.at[q], peer_x(), source)

    def z_sends(q, k):
        return copies(number(z, y, core), q, z_s.at[q, k], z_r.at[q, k], peer_z(k))

    def z_recvs(q, k):
        return copies(number(from_z(k), y, core), q, z_s.at[q, k], z_r.at[q, k], peer_z(k))

    def y_copies(q, k, yy):
        return copies(number(from_z(k), yy, core), q, y_s.at[q, k], y_r.at[q, k], peer_y())

    def c_copies(q, k, far, cc):
        yy = (1 - y) if far else y
        slot = 4 * far + k
        return copies(number(from_z(k), yy, cc), q, c_s.at[q, slot], c_r.at[q, slot], peer_core())

    def start(list_of):
        for copy in list_of:
            copy.start()

    def first(q):
        for copy in x_copies(q):
            copy.wait()
        for k in (2, 1, 3):
            start(z_sends(q, k))
        start(y_copies(q, 0, y))
        start(c_copies(q, 0, 0, core))

    def second(q):
        for k in (1, 3, 2):
            for copy in z_recvs(q, k):
                copy.wait_recv()
            start(y_copies(q, k, y))
            start(c_copies(q, k, 0, core))

    def third(q):
        for k in range(4):
            for copy in y_copies(q, k, 1 - y):
                copy.wait_recv()
            start(c_copies(q, k, 1, core))

    def last(q):
        for k in range(4):
            for far in (0, 1):
                for copy in c_copies(q, k, far, 1 - core):
                    copy.wait_recv()

    def sent(q):
        for k in range(4):
            if k > 0:
                for copy in z_sends(q, k):
                    copy.wait_send()
            for copy in y_copies(q, k, y):
                copy.wait_send()
            for far in (0, 1):
                for copy in c_copies(q, k, far, core):
                    copy.wait_send()

    return first, second, third, last, sent, x_copies


def gather_semaphores(q):
    sem = pltpu.SemaphoreType.DMA
    return [sem((q, 2))] * 2 + [sem((q, 4, 2))] * 4 + [sem((q, 8, 2))] * 2


def hidden_views(arrays, dp, b):
    up, down = arrays
    n_up, n_down = up.shape[0] // PIECES, HIDDEN_BLOCK // PIECES
    return [
        up.at[pl.ds(pl.multiple_of(dp * n_up, n_up), n_up), pl.ds(b * HIDDEN_BLOCK, HIDDEN_BLOCK)],
        down.at[pl.ds(pl.multiple_of(b * HIDDEN_BLOCK + dp * n_down, n_down), n_down)],
    ]


CROSS_FIRST = 2
ORDER = (("t", 0), ("t", 1), ("o", 2), ("o", 3), ("t", 2), ("o", 0), ("o", 1), ("t", 3))
SLOT = (0, 1, 2, 3, 4, 5, 0, 2, 3, 4, 5, 1)
S_SLOTS = 6
DELAYED = 6
HALF = len(ORDER) // 2
N_MLP = 2 * HALF
N_ALL = N_MLP + 4
VEC_ROWS = 8
A_TICKS = {
    "start": [("g_first", 0)],
    "block": [("g_second", 0)],
    "early": [("g_first", 1), ("g_third", 0)],
    "middle": [("g_first", 2), ("g_second", 1)],
    "late": [("g_first", 3), ("g_third", 1), ("g_second", 2)],
    "end": [("g_third", 2)],
}
B_START = [("g_first", 4), ("g_second", 3)]
B_TICKS = {1: [("g_third", 3)], 2: [("g_second", 4)], 4: [("g_third", 4)], 7: [("second", 2)]}
C_START = []
C_TICKS = {
    0: ([("second", 3)], [(2, [("third", 2)])], [(2, [("second", 4)])], [(1, [("third", 3)])], [(3, [("second", 5)])]),
    1: (
        [], [], [(0, [("second", 3)])], [(2, [("third", 2)])], [(2, [("second", 4)])], [(2, [("third", 3)])],
        [(3, [("second", 5)])],
    ),
}
END_TICKS = [("third", 4)]
MORE_TICKS = ([("second", 7), ("third", 5)], [("second", 8), ("vec", (0, 2))])
TAIL = [
    ("third", 7), ("second", 9), ("vec", (1, 1)), ("third", 8), ("second", 6), ("third", 9), ("vec", (0, 3)), ("second", 10),
    ("third", 6), ("second", 11), ("vec", (1, 2)), ("third", 10), ("third", 11), ("vec", (1, 3)), ("fourth", 0),
    ("fourth", 1), ("fourth", 2), ("vec", (0, 4)), ("vec", (1, 4)),
]


def lookup(table, p):
    if isinstance(p, int):
        return table[p]
    value = jnp.int32(table[0])
    for n in range(1, len(table)):
        value = jnp.where(p == n, jnp.int32(table[n]), value)
    return value


def before(p):
    return max((n for n in range(p) if SLOT[n] == SLOT[p]), default=None)


def hidden_of(p):
    return lookup([b for _, b in ORDER], p)


def is_other(p):
    if isinstance(p, int):
        return ORDER[p][0] == "t"
    return lookup([int(s == "t") for s, _ in ORDER], p) == 1


def step_kernel(
    g1_ref, s1_ref, ob_ref, g2_ref, s2_ref, db_ref, ub_ref, qvb_ref, seg_ref,
    x_hbm, g_hbm, wqkv_hbm, wout_hbm, up_own, down_own,
    out_ref, dinr_ref, upg_ref, downg_ref, og_ref, qkvg_ref, vec_ref, qvg_ref, ubg_ref,
    a1_hbm, qkv_hbm, mix_hbm, up_oth, down_oth,
    wout_ref, mixt_ref, lse_ref, par_ref, ubo_ref, ubt_ref, din_ref, stage_ref,
    dkv_ref, dm_ref, dsend_ref, send_ref, dq_ref, grad_ref, core_ref, sum_ref, ybuf, zbuf, xfirst, xsend, xbuf,
    vsum, vrecv,
    a_s, a_r, m_s, m_r, b_s, b_r, l_sem,
    c_s, c_r, y_s, y_r, z_s, z_r, xf_s, xf_r, x_s, x_r, v_s, v_r, dm_s, dm_r, o_s, o_r, out_sem, free_sem, *gather_sems,
):
    rows, width = din_ref.shape
    seq = 2 * rows
    local = dm_ref.shape[1]
    block = rows // 2
    piece = rows // 4
    hb = HIDDEN_BLOCK
    nx = CROSS_FIRST
    half, n_mlp, n_all = HALF, N_MLP, N_ALL
    z, y, core, side = place()
    partner = peer_x()
    own = pl.multiple_of(side * rows, rows)
    theirs = pl.multiple_of((1 - side) * rows, rows)
    scale = HEAD_DIM**-0.5
    vmem = pltpu.VMEM
    sem = pltpu.SemaphoreType.DMA

    def out_views(ref, dp):
        return [ref.at[dp // 4, dp // 2 % 2, pl.ds(dp % 2 * 32, 32)]]

    def gather_source(dp, q):
        return out_views(wout_hbm, dp) if q == 0 else hidden_views((up_own, down_own), dp, q - 1)

    def gather_target(dp, q):
        return out_views(wout_ref.at[1], dp) if q == 0 else hidden_views((up_oth, down_oth), dp, q - 1)

    g_first, g_second, g_third, g_last, g_sent, g_x = gather(gather_source, gather_target, gather_sems)

    def g_start(q):
        for copy in g_x(q):
            copy.start()

    def cols_of(p):
        return 2 * hb if p <= n_mlp else hb

    def slot_of(p):
        return lookup(SLOT, p)

    def core_copy(p, cols):
        slot = p % 2
        lanes = pl.ds(0, cols)
        return remote(
            grad_ref.at[slot, :, 1 - core, :, lanes], core_ref.at[slot, :, :, lanes], c_s.at[slot], c_r.at[slot],
            peer_core(),
        )

    def place_of(p, cols):
        if isinstance(p, int) and p > n_mlp:
            n = p - n_mlp - 1
            return n_mlp + 1 - nx + n // 2, pl.ds(n % 2 * hb, hb)
        return p - nx, pl.ds(0, cols)

    def y_copy(p, cols):
        s, lanes = place_of(p, cols)
        src = sum_ref.at[slot_of(p), :, 1 - y, :, pl.ds(0, cols)]
        return remote(src, ybuf.at[s, :, :, lanes], y_s.at[p - nx], y_r.at[p - nx], peer_y())

    def z_copy(p, k, cols):
        s, lanes = place_of(p, cols)
        src, dst = ybuf.at[s, (z + k) % 4, :, lanes], zbuf.at[s, k - 1, :, lanes]
        return remote(src, dst, z_s.at[p - nx, k - 1], z_r.at[p - nx, k - 1], peer_z(k))

    def xfirst_copy(p):
        return remote(sum_ref.at[slot_of(p)], xfirst.at[p], xf_s.at[p], xf_r.at[p], partner)

    def x_copy(n):
        lanes = pl.ds(0, 2 * hb if n < half - nx else hb)
        return remote(xsend.at[n, :, lanes], xbuf.at[n, :, lanes], x_s.at[n], x_r.at[n], partner)

    def produced(p, cols):
        @pl.when(p >= 2)
        def _():
            pl.semaphore_wait(free_sem, 1)

        core_copy(p, cols).start()

    def consume(p, cols):
        slot = p % 2
        lanes = pl.ds(0, cols)
        copy = core_copy(p, cols)
        copy.wait()
        for n in range(n_all) if not isinstance(p, int) else (p,):
            if before(n) is not None and n < n_mlp - 1 and not isinstance(p, int):

                @pl.when(p == n)
                def _():
                    sent(before(n))

            elif before(n) is not None and isinstance(p, int):
                sent(before(n))
        total = grad_ref[slot, :, core, :, lanes].astype(F32) + core_ref[slot, :, :, lanes].astype(F32)
        at = sum_ref.at[slot_of(p), :, :, :, lanes]
        at[...] = total.astype(BF16).reshape(4, 2, 64, cols)

        @pl.when(p < n_all - 2)
        def _():
            pl.semaphore_signal(free_sem, inc=1, device_id=peer_core(), device_id_type=MESH)

    def sent(p):
        if p < nx:
            xfirst_copy(p).wait_send()
        else:
            y_copy(p, cols_of(p)).wait_send()

    def push(p, cols):
        if isinstance(p, int):
            if p < n_mlp and not is_other(p) and hidden_of(p) < nx:
                add_first(p)
            y_copy(p, cols).start()
            return

        @pl.when(p == 0)
        def _():
            xfirst_copy(p).start()

        @pl.when((p >= nx) & (p != DELAYED))
        def _():
            @pl.when(jnp.logical_not(is_other(p)) & (hidden_of(p) < nx))
            def _():
                add_first(p)

            y_copy(p, cols).start()

    def add_first(p):
        b = hidden_of(p)
        xfirst_copy(b).wait_recv()
        sum_ref[slot_of(p)] = (
            sum_ref[slot_of(p)].astype(F32) + xfirst[b].astype(F32)
        ).astype(BF16)

    def second(p):
        cols = cols_of(p)
        s, lanes = place_of(p, cols)
        y_copy(p, cols).wait_recv()
        ybuf[s, :, :, lanes] = (
            sum_ref[slot_of(p), :, y, :, pl.ds(0, cols)].astype(F32) + ybuf[s, :, :, lanes].astype(F32)
        ).astype(BF16)
        for k in (2, 1, 3):
            z_copy(p, k, cols).start()

    def mlp_write(b, total, more=False):
        cols = pl.ds(b * hb, hb)
        for ref, part in ((upg_ref, total[:, :hb]), (downg_ref, total[:, hb:])):
            ref[:, cols] = ref[:, cols] + part if more else part

    def third(p):
        cols = cols_of(p)
        s, lanes = place_of(p, cols)
        for k in (1, 2, 3):
            z_copy(p, k, cols).wait_recv()
        total = ybuf[s, z, :, lanes].astype(F32)
        for k in (1, 2, 3):
            total = total + zbuf[s, k - 1, :, lanes].astype(F32)
        if p < n_mlp and is_other(p):
            n = hidden_of(p) - nx
            xsend[n] = total.astype(BF16)
            x_copy(n).start()
        elif p < n_mlp:
            mlp_write(hidden_of(p), total)
        elif p == n_mlp:
            og_ref[...] = total[:, :hb]
            xsend[half - nx, :, pl.ds(0, hb)] = total[:, hb:].astype(BF16)
            x_copy(half - nx).start()
        else:
            qkvg_ref[p - n_mlp - 1] = total

    def fourth(n):
        x_copy(n).wait_recv()
        if n < half - nx:
            mlp_write(n + nx, xbuf[n].astype(F32), more=True)
        else:
            og_ref[...] += xbuf[n, :, pl.ds(0, hb)].astype(F32)

    def v_copy(w, n, peer, slot):
        return remote(vsum.at[w, n], vrecv.at[w, slot], v_s.at[w, slot], v_r.at[w, slot], peer)

    def z_vec(w, k, source):
        return remote(vsum.at[w, 2], vrecv.at[w, 2 + source], v_s.at[w, 2 + k], v_r.at[w, 2 + source], peer_z(k))

    def vectors(w, n):
        if n == 0:
            v_copy(w, 0, peer_core(), 0).start()
        elif n == 1:
            v_copy(w, 0, peer_core(), 0).wait()
            vsum[w, 1] = vsum[w, 0] + vrecv[w, 0]
            v_copy(w, 1, peer_y(), 1).start()
        elif n == 2:
            v_copy(w, 1, peer_y(), 1).wait()
            vsum[w, 2] = vsum[w, 1] + vrecv[w, 1]
            for k in (1, 2, 3):
                z_vec(w, k, z).start()
        elif n == 3:
            for k in (1, 2, 3):
                z_vec(w, k, z).wait_send()
                z_vec(w, k, (z + k) % 4).wait_recv()
            vrecv[w, 2 + z] = vsum[w, 2]
            vsum[w, 3] = (vrecv[w, 2] + vrecv[w, 3]) + (vrecv[w, 4] + vrecv[w, 5])
            v_copy(w, 3, partner, 6).start()
        elif n == 4:
            v_copy(w, 3, partner, 6).wait()
            vec_ref[pl.ds(w * VEC_ROWS, VEC_ROWS)] = vsum[w, 3] + vrecv[w, 6]

    stages = dict(
        second=second, third=third, fourth=fourth, g_first=g_first, g_second=g_second, g_third=g_third, g_last=g_last
    )

    def run(names):
        for name, arg in names:
            if name == "vec":
                vectors(*arg)
            else:
                stages[name](arg)

    dm_own = dm_ref.at[pl.ds(own, rows)]

    def dm_copy(b):
        at = pl.ds(pl.multiple_of(own + b * block, block), block)
        return remote(dsend_ref.at[b], dm_ref.at[at], dm_s.at[b], dm_r.at[b], partner)

    def dm_from(b):
        at = pl.ds(pl.multiple_of((1 - side) * rows + b * block, block), block)
        return remote(dsend_ref.at[b], dm_ref.at[at], dm_s.at[b], dm_r.at[b], partner)

    def out_copy(j):
        return pltpu.make_async_copy(send_ref.at[j], out_ref.at[j], out_sem.at[j])

    def o_copy(j):
        return remote(send_ref.at[j], xfirst.at[0, pl.ds(2 * j, 2)], o_s.at[j], o_r.at[j], partner)

    greet()
    for n, vector in enumerate((g1_ref, s1_ref, ob_ref, g2_ref, s2_ref, db_ref)):
        par_ref[pl.ds(n, 1)] = vector[...].astype(F32).reshape(1, width)
    for n in range(half):
        ubo_ref[pl.ds(n, 1)] = ub_ref[pl.ds(n * hb, hb)].astype(F32).reshape(1, hb)
    bias_copy = remote(ubo_ref, ubt_ref, b_s, b_r, partner)
    a1_ref = sum_ref

    def a1_copy(which, b):
        return remote(a1_ref.at[which, b], a1_ref.at[which, b], a_s.at[b], a_r.at[b], partner)

    def wqkv_parts(ref):
        return [(wqkv_hbm.at[n], ref.at[:, pl.ds(n * local, local)]) for n in range(3)]

    def wout_own():
        return wout_ref[0].reshape(local, width)

    def wout_other():
        return wout_ref[1].reshape(local, width)

    def ahead(x_ref, wqkv_ref, qkv_ref, mix_ref, mask_ref):
        loads = [
            pltpu.make_async_copy(src, dst, l_sem.at[n])
            for n, (src, dst) in enumerate(((x_hbm, x_ref), (wout_hbm, wout_ref.at[0]), *wqkv_parts(wqkv_ref)))
        ]
        for load in loads:
            load.start()
        g_start(0)
        gain = par_ref[pl.ds(GAIN_1, 1)]
        shift = par_ref[pl.ds(SHIFT_1, 1)]
        loads[0].wait()
        for b in range(4):
            xhat, _ = norm_parts(x_ref[pl.ds(b * piece, piece)].astype(F32))
            a1_ref[side, b] = (xhat * gain + shift).astype(BF16).reshape(2, 64, width)
            a1_copy(side, b).start()
            if b < 2:
                g_start(1 + b)
        bias_copy.start()
        g_start(3)

        def project(left, base, count):
            at = pl.ds(pl.multiple_of(base, block), count)
            for part in range(3):
                cols = pl.ds(part * local, local)
                value = dot_nn(left, wqkv_ref[:, cols])
                if part != 1:
                    value = value + qvb_ref[pl.ds(part // 2, 1)].astype(F32)
                qkv_ref[at, cols] = value.astype(BF16)

        for load in loads[2:]:
            load.wait()
        project(a1_ref[side].reshape(rows, width), own, rows)

        def mix_copy(j):
            at = pl.ds(pl.multiple_of(theirs + j * block, block), block)
            far = mixt_ref.at[pl.ds(j * block, block)]
            return remote(mix_ref.at[at], far, m_s.at[j], m_r.at[j], partner)

        seg_row = seg_ref[...].astype(F32)
        seg_col = jnp.broadcast_to(seg_row, (8, seq)).T[:, :1]
        run(A_TICKS["start"])

        @pl.when(side == 1)
        def _():
            run(A_TICKS["block"])

        for i in range(4):
            lo = i * block
            keys = lo + block
            is_theirs = side == (1 if i < 2 else 0)
            at = pl.ds(lo, block)
            if i == 1:

                @pl.when(side == 0)
                def _():
                    run(A_TICKS["block"])

            @pl.when(is_theirs)
            def _():
                j = i % 2
                run(A_TICKS["middle" if j else "early"])
                for b in (2 * j, 2 * j + 1):
                    a1_copy(1 - side, b).wait_recv()
                project(a1_ref[1 - side, pl.ds(2 * j, 2)].reshape(block, width), lo, block)

            same = seg_col[:keys] == seg_row[:, lo : lo + block]
            k_pos = lax.broadcasted_iota(jnp.int32, (keys, block), 0)
            q_pos = lo + lax.broadcasted_iota(jnp.int32, (keys, block), 1)
            mask_ref[pl.ds(0, keys)] = jnp.where(same & (q_pos >= k_pos), 0.0, -1e30)

            def pair(hp, _):
                base = pl.multiple_of(hp * 2 * HEAD_DIM, 2 * HEAD_DIM)
                cols = pl.ds(base, 2 * HEAD_DIM)
                q2 = qkv_ref[at, cols]
                k2 = qkv_ref[pl.ds(0, keys), pl.ds(pl.multiple_of(local + base, 128), 2 * HEAD_DIM)]
                v2 = qkv_ref[pl.ds(0, keys), pl.ds(pl.multiple_of(2 * local + base, 128), 2 * HEAD_DIM)]
                out = jnp.zeros((block, 2 * HEAD_DIM), F32)
                for h in range(2):
                    scores = dot_nt(k2, only_head(q2, h)) * scale + mask_ref[pl.ds(0, keys)]
                    top = jnp.max(scores, axis=0, keepdims=True)
                    weights = jnp.exp(scores - top)
                    total = total_of(weights)
                    lse_ref[pl.ds(2 * hp + h, 1), at] = top + jnp.log(total)
                    out += dot_tn((weights * (1.0 / total)).astype(BF16), only_head(v2, h))
                mix_ref[at, cols] = out.astype(BF16)
                return 0

            lax.fori_loop(0, local // (2 * HEAD_DIM), pair, 0)

            @pl.when(is_theirs)
            def _():
                mix_copy(i % 2).start()
                if i % 2:
                    g_start(4)
                    run(A_TICKS["late"])

        saves = [
            pltpu.make_async_copy(src, dst, l_sem.at[n])
            for n, (src, dst) in enumerate(((qkv_ref, qkv_hbm), (mix_ref, mix_hbm), (a1_ref.at[pl.ds(0, 2)], a1_hbm)), start=5)
        ]
        for save in saves:
            save.start()
        loads[1].wait()
        g_last(0)
        for j in range(2):
            at = pl.ds(j * block, block)
            mix_copy(j).wait_recv()
            mine = dot_nn(mix_ref[pl.ds(pl.multiple_of(own + j * block, block), block)], wout_own())
            din_ref[at] = (
                x_ref[at].astype(F32) + (mine + dot_nn(mixt_ref[at], wout_other())) + par_ref[pl.ds(OUT_BIAS, 1)]
            )
        run(A_TICKS["end"])
        for save in saves:
            save.wait()
        for j in range(2):
            mix_copy(j).wait_send()
        for b in range(4):
            a1_copy(side, b).wait_send()
        bias_copy.wait()

    pl.run_scoped(
        ahead,
        vmem((rows, width), BF16), vmem((width, 3 * local), BF16), vmem((seq, 3 * local), BF16), vmem((seq, local), BF16),
        vmem((seq, block), F32),
    )

    h_ref = din_ref

    def feed(g_ref, a2_ref, a2t_ref, gt_ref, wu_ref, wd_ref, in_sem, w_sem):
        load_g = pltpu.make_async_copy(g_hbm, g_ref, in_sem)
        load_g.start()

        def fetch(b, up, down, slot):
            at = pl.ds(pl.multiple_of(b * hb, hb), hb)
            return (
                pltpu.make_async_copy(up.at[:, at], wu_ref.at[slot], w_sem.at[slot, 0]),
                pltpu.make_async_copy(down.at[at], wd_ref.at[slot], w_sem.at[slot, 1]),
            )

        def fetch_start(p, slot):
            for n in range(n_mlp):
                if is_other(n):

                    @pl.when(p == n)
                    def _():
                        g_last(1 + hidden_of(n))

            @pl.when(is_other(p))
            def _():
                for copy in fetch(hidden_of(p), up_oth, down_oth, slot):
                    copy.start()

            @pl.when(jnp.logical_not(is_other(p)))
            def _():
                for copy in fetch(hidden_of(p), up_own, down_own, slot):
                    copy.start()

        fetch_start(jnp.int32(0), 0)
        gain = par_ref[pl.ds(GAIN_2, 1)]
        xhat, _ = norm_parts(h_ref[...])
        a2 = (xhat * gain + par_ref[pl.ds(SHIFT_2, 1)]).astype(BF16)
        a2_ref[...] = a2
        a2t_ref[...] = a2.T
        load_g.wait()
        gt_ref[...] = g_ref[...].T
        dkv_ref[...] = jnp.zeros_like(dkv_ref)
        acc_ref = dkv_ref.at[pl.ds(0, rows)]
        da2_ref = dkv_ref.at[pl.ds(rows, rows)]

        def step(p, _):
            slot = p % 2
            for copy in fetch(0, up_own, down_own, slot):
                copy.wait()

            @pl.when(p + 1 < n_mlp)
            def _():
                fetch_start(p + 1, 1 - slot)

            b = hidden_of(p)
            wu, wd = wu_ref[slot], wd_ref[slot]
            u = dot_nn(a2_ref[...], wu) + jnp.where(is_other(p), ubt_ref[pl.ds(b, 1)], ubo_ref[pl.ds(b, 1)])
            tanh = jnp.tanh(0.7978845608028654 * (u + 0.044715 * u * u * u))
            hidden = (0.5 * u * (1.0 + tanh)).astype(BF16)
            slope = 0.5 * (1.0 + tanh) + 0.5 * u * (1.0 - tanh * tanh) * (
                0.7978845608028654 * (1.0 + 3.0 * 0.044715 * u * u)
            )
            acc_ref[...] += dot_nn(hidden, wd)
            du = (dot_nt(g_ref[...], wd) * slope).astype(BF16)
            where_side = jnp.where(is_other(p), 1 - side, side)
            lanes = pl.ds(pl.multiple_of((b % 2) * hb, hb), hb)
            vsum[0, 0, pl.ds(4 + where_side * (half // 2) + b // 2, 1), lanes] = total_of(du.astype(F32))
            da2_ref[...] += dot_nt(du, wu)
            grad_ref[slot, :, :, :, pl.ds(0, hb)] = dot_nn(a2t_ref[...], du).astype(BF16).reshape(8, 2, 64, hb)
            grad_ref[slot, :, :, :, pl.ds(hb, hb)] = dot_nn(gt_ref[...], hidden).astype(BF16).reshape(8, 2, 64, hb)
            produced(p, 2 * hb)

            for n, names in B_TICKS.items():

                @pl.when(p == n)
                def _():
                    run(names)

            @pl.when(p >= 1)
            def _():
                consume(p - 1, 2 * hb)
                push(p - 1, 2 * hb)

            return 0

        vsum[0, 0] = jnp.zeros(vsum.shape[2:], F32)
        vsum[1, 0] = jnp.zeros(vsum.shape[2:], F32)
        run(B_START)
        lax.fori_loop(0, n_mlp, step, 0)

        piece = rows // 4
        sums = [jnp.zeros((1, width), F32) for _ in range(4)]
        for b in range(4):
            at = pl.ds(b * piece, piece)
            h = h_ref[at]
            g = g_ref[at].astype(F32)
            out = (h + acc_ref[at] + par_ref[pl.ds(DOWN_BIAS, 1)]).astype(BF16)
            send_ref[b // 2, b % 2] = out.reshape(2, 64, width)
            xhat, rstd = norm_parts(h)
            da2 = da2_ref[at]
            dh = g + norm_back(da2, gain, xhat, rstd)
            din_ref[at] = dh
            for n, term in enumerate((da2 * xhat, da2, dh.astype(BF16).astype(F32), g)):
                sums[n] = sums[n] + total_of(term)
        for n in range(4):
            vsum[0, 0, pl.ds(n, 1)] = sums[n]
        vectors(0, 0)
        for j in range(2):
            out_copy(j).start()

    pl.run_scoped(
        feed,
        vmem((rows, width), BF16), vmem((rows, width), BF16), vmem((width, rows), BF16),
        vmem((width, rows), BF16), vmem((2, width, hb), BF16), vmem((2, hb, width), BF16), sem, sem((2, 2)),
    )

    def attend(qkv_ref, mix_ref, wqkv_ref, mask_ref, dhl_ref, in_sem):
        x_ref, dqkv_ref = dhl_ref, qkv_ref
        moves = [
            pltpu.make_async_copy(src, dst, in_sem.at[n])
            for n, (src, dst) in enumerate((
                (mix_hbm, mix_ref), (qkv_hbm, qkv_ref), (x_hbm, x_ref), (a1_hbm, wout_ref), *wqkv_parts(wqkv_ref),
            ))
        ]
        for n in (0, 1, 4, 5, 6):
            moves[n].start()
        dhl_ref[...] = din_ref[...].astype(BF16)
        consume(n_mlp - 1, 2 * hb)
        push(n_mlp - 1, 2 * hb)
        for b in (1, 0):
            dsend_ref[b] = dot_nt(dhl_ref[pl.ds(b * block, block)], wout_other()).astype(BF16)
            dm_copy(b).start()
        for b in range(1, nx):
            xfirst_copy(b).start()
        run(C_START)
        dm_own[...] = dot_nt(dhl_ref[...], wout_own()).astype(BF16)
        g_sent(0)
        moves[3].start()
        moves[0].wait()
        p = n_mlp
        for part in range(2):
            mixed = mixt_ref[...] if part else mix_ref[pl.ds(own, rows)]
            grad = dot_tn(dhl_ref[...], mixed).astype(BF16)
            grad_ref[p % 2, :, :, :, pl.ds(part * hb, hb)] = grad.reshape(8, 2, 64, hb)
        produced(p, 2 * hb)
        moves[2].start()
        dkv_ref[...] = jnp.zeros_like(dkv_ref)
        seg_row = seg_ref[...].astype(F32)
        seg_col = jnp.broadcast_to(seg_row, (8, seq)).T[:, :1]
        moves[1].wait()
        for j in range(2):
            out_copy(j).wait()

        def task(i, keys, stage="all", ticks=()):
            lo, start, count = i * block, keys[0], keys[1] - keys[0]
            at, among = pl.ds(lo, block), pl.ds(start, count)
            same = seg_col[start : start + count] == seg_row[:, lo : lo + block]
            k_pos = start + lax.broadcasted_iota(jnp.int32, (count, block), 0)
            q_pos = lo + lax.broadcasted_iota(jnp.int32, (count, block), 1)
            mask_ref[pl.ds(0, count)] = jnp.where(same & (q_pos >= k_pos), 0.0, -1e30)

            def pair(hp, _):
                base = pl.multiple_of(hp * 2 * HEAD_DIM, 2 * HEAD_DIM)
                cols = pl.ds(base, 2 * HEAD_DIM)
                v_cols = pl.ds(pl.multiple_of(local + base, 128), 2 * HEAD_DIM)
                q2 = qkv_ref[at, cols]
                k2 = qkv_ref[among, v_cols]
                v2 = qkv_ref[among, pl.ds(pl.multiple_of(2 * local + base, 128), 2 * HEAD_DIM)]
                g2 = dm_ref[at, cols]
                turned = (g2.astype(F32) * mix_ref[at, cols].astype(F32)).T
                dq = jnp.zeros((block, 2 * HEAD_DIM), F32)
                dk = jnp.zeros((count, 2 * HEAD_DIM), F32)
                dv = jnp.zeros((count, 2 * HEAD_DIM), F32)
                for h in range(2):
                    qh = only_head(q2, h)
                    gh = only_head(g2, h)
                    row_dot = total_of(turned[h * HEAD_DIM : (h + 1) * HEAD_DIM])
                    offset = mask_ref[pl.ds(0, count)] - lse_ref[pl.ds(2 * hp + h, 1), at]
                    probs = jnp.exp(dot_nt(k2, qh) * scale + offset)
                    dscore = (probs * (dot_nt(v2, gh) - row_dot)).astype(BF16)
                    dv += dot_nn(probs.astype(BF16), gh)
                    dk += dot_nn(dscore, qh)
                    dq += dot_tn(dscore, only_head(k2, h))
                if stage == "first":
                    dq_ref[i - 2, :, cols] = dq
                else:
                    if stage == "last":
                        dq = dq + dq_ref[i - 2, :, cols]
                    dqkv_ref[at, cols] = (dq * scale).astype(BF16)
                dkv_ref[among, cols] += dk
                dkv_ref[among, v_cols] += dv
                for n, names in ticks:

                    @pl.when(hp == n)
                    def _():
                        run(names)

                return 0

            lax.fori_loop(0, local // (2 * HEAD_DIM), pair, 0)

        def finish(i, send):
            at = pl.ds(i * block, block)
            dqkv_ref[at, pl.ds(local, local)] = (dkv_ref[at, pl.ds(0, local)] * scale).astype(BF16)
            dqkv_ref[at, pl.ds(2 * local, local)] = dkv_ref[at, pl.ds(local, local)].astype(BF16)
            product = dot_nt(dqkv_ref[at], wqkv_ref[...])
            if send:
                send_ref[i % 2] = product.astype(BF16).reshape(send_ref.shape[1:])
                o_copy(i % 2).start()
            else:
                dkv_ref[at] = product

        def second_block():
            consume(n_mlp, 2 * hb)
            push(n_mlp, 2 * hb)
            vectors(0, 1)
            for move in moves[4:]:
                move.wait()

        @pl.when(side == 0)
        def _():
            run(C_TICKS[0][0])
            dm_from(1).wait_recv()
            task(3, (0, 4 * block), ticks=C_TICKS[0][1])
            second_block()
            finish(3, True)
            dm_from(0).wait_recv()
            task(2, (0, 3 * block), ticks=C_TICKS[0][2])
            finish(2, True)
            task(1, (0, 2 * block), ticks=C_TICKS[0][3])
            finish(1, False)
            task(0, (0, block), ticks=C_TICKS[0][4])
            finish(0, False)

        @pl.when(side == 1)
        def _():
            task(3, (0, 2 * block), "first", ticks=C_TICKS[1][1])
            task(2, (0, 2 * block), "first", ticks=C_TICKS[1][2])
            second_block()
            dm_from(1).wait_recv()
            task(1, (0, 2 * block), ticks=C_TICKS[1][3])
            finish(1, True)
            dm_from(0).wait_recv()
            task(0, (0, block), ticks=C_TICKS[1][4])
            finish(0, True)
            task(3, (2 * block, 4 * block), "last", ticks=C_TICKS[1][5])
            finish(3, False)
            task(2, (2 * block, 3 * block), "last", ticks=C_TICKS[1][6])
            finish(2, False)

        moves[3].wait()
        for part in range(3):
            p = n_mlp + 1 + part
            grad = dot_tn(wout_ref[...].reshape(seq, width), dqkv_ref[:, pl.ds(part * local, local)]).astype(BF16)
            grad_ref[p % 2, :, :, :, pl.ds(0, hb)] = grad.reshape(8, 2, 64, hb)
            produced(p, hb)
            if part == 1:
                consume(p - 1, hb)
                push(p - 1, hb)
        moves[2].wait()

        def din_copy(j):
            return pltpu.make_async_copy(stage_ref, dinr_ref.at[pl.ds(j * block, block)], in_sem.at[j])

        def finish_rows(j):
            at = pl.ds(j * block, block)
            o_copy(j).wait_recv()
            da1 = dkv_ref[pl.ds(pl.multiple_of(own + j * block, block), block)] + xfirst[0, pl.ds(2 * j, 2)].reshape(
                block, width
            ).astype(F32)
            xhat, rstd = norm_parts(x_ref[at].astype(F32))
            grad = din_ref[at] + norm_back(da1, par_ref[pl.ds(GAIN_1, 1)], xhat, rstd)
            if j == 0:
                din_copy(1).wait()
            stage_ref[...] = grad.reshape(block, 8, width // 8)
            din_copy(j).start()
            return total_of(da1 * xhat), total_of(da1)

        lanes = pl.ds(pl.multiple_of(side * local, local), local)
        vsum[1, 0, pl.ds(2, 1), lanes] = total_of(dqkv_ref[:, pl.ds(0, local)].astype(F32))
        vsum[1, 0, pl.ds(3, 1), lanes] = total_of(dqkv_ref[:, pl.ds(2 * local, local)].astype(F32))
        push(DELAYED, 2 * hb)
        consume(n_mlp + 2, hb)
        push(n_mlp + 2, hb)
        run(END_TICKS)
        consume(n_mlp + 3, hb)
        push(n_mlp + 3, hb)
        run(MORE_TICKS[0])
        gain_1, shift_1 = finish_rows(1)
        run(MORE_TICKS[1])
        gain_0, shift_0 = finish_rows(0)
        vsum[1, 0, pl.ds(0, 1)] = gain_0 + gain_1
        vsum[1, 0, pl.ds(1, 1)] = shift_0 + shift_1
        vectors(1, 0)
        din_copy(0).wait()

    pl.run_scoped(
        attend,
        vmem((seq, 3 * local), BF16), vmem((seq, local), BF16), vmem((width, 3 * local), BF16), vmem((seq, block), F32),
        vmem((rows, width), BF16), sem((7,)),
    )

    run(TAIL)
    qvg_ref[...] = vec_ref[pl.ds(VEC_ROWS + 2, 2), pl.ds(pl.multiple_of(side * local, local), local)]
    for n in range(2):
        ubg_ref[pl.ds(n, 1)] = vec_ref[pl.ds(4 + side * 2 + n, 1)]
    for q in range(1, half + 1):
        g_sent(q)
    for j in range(2):
        dm_copy(j).wait_send()
        o_copy(j).wait_send()
    for p in range(n_all):
        if all(before(n) != p for n in range(n_all)):
            sent(p)
    for p in range(nx, n_all):
        for k in (1, 2, 3):
            z_copy(p, k, cols_of(p)).wait_send()
    for n in range(half - nx + 1):
        x_copy(n).wait_send()


def step_call(vectors, ub, qvb, seg, x, g, wqkv, wout, up, down):
    rows, width = x.shape
    local = wout.size // width
    seq = 2 * rows
    block = rows // 2
    hb = HIDDEN_BLOCK
    nx = CROSS_FIRST
    height = width // PIECES
    vm = pl.BlockSpec(memory_space=pltpu.VMEM)
    hbm = pl.BlockSpec(memory_space=pltpu.HBM)
    sem = pltpu.SemaphoreType.DMA
    ny = N_ALL - nx
    nxl = HALF - nx + 1
    shape = jax.ShapeDtypeStruct
    return pl.pallas_call(
        step_kernel,
        out_shape=(
            shape((2, 2, 2, height, width), BF16),
            shape((rows, 8, width // 8), F32),
            shape((height, HALF * hb), F32),
            shape((height, HALF * hb), F32),
            shape((height, local), F32),
            shape((3, height, local), F32),
            shape((2 * VEC_ROWS, width), F32),
            shape((2, local), F32),
            shape((2, width), F32),
            shape((2, 4, 2, height, width), BF16),
            shape((seq, 3 * local), BF16),
            shape((seq, local), BF16),
            shape(up.shape, BF16),
            shape(down.shape, BF16),
        ),
        in_specs=[vm] * 9 + [hbm] * 6,
        out_specs=(hbm,) * 2 + (vm,) * 7 + (hbm,) * 5,
        scratch_shapes=[
            pltpu.VMEM((2, 4, 2, height, width), BF16),
            pltpu.VMEM((rows, local), BF16),
            pltpu.VMEM((local // HEAD_DIM, seq), F32),
            pltpu.VMEM((8, width), F32),
            pltpu.VMEM((8, hb), F32),
            pltpu.VMEM((8, hb), F32),
            pltpu.VMEM((rows, width), F32),
            pltpu.VMEM((block, 8, width // 8), F32),
            pltpu.VMEM((seq, width), F32),
            pltpu.VMEM((seq, local), BF16),
            pltpu.VMEM((2, block, local), BF16),
            pltpu.VMEM((2, 2, 2, height, width), BF16),
            pltpu.VMEM((2, block, local), F32),
            pltpu.VMEM((2, 8, 2, height, 2 * hb), BF16),
            pltpu.VMEM((2, 8, height, 2 * hb), BF16),
            pltpu.VMEM((S_SLOTS, 4, 2, height, 2 * hb), BF16),
            pltpu.VMEM((ny - 1, 4, height, 2 * hb), BF16),
            pltpu.VMEM((ny - 1, 3, height, 2 * hb), BF16),
            pltpu.VMEM((nx, 4, 2, height, 2 * hb), BF16),
            pltpu.VMEM((nxl, height, 2 * hb), BF16),
            pltpu.VMEM((nxl, height, 2 * hb), BF16),
            pltpu.VMEM((2, 4, VEC_ROWS, width), F32),
            pltpu.VMEM((2, 7, VEC_ROWS, width), F32),
            sem((4,)), sem((4,)), sem((2,)), sem((2,)), sem, sem, sem((8,)),
            sem((2,)), sem((2,)), sem((ny,)), sem((ny,)), sem((ny, 3)), sem((ny, 3)),
            sem((nx,)), sem((nx,)), sem((nxl,)), sem((nxl,)), sem((2, 7)), sem((2, 7)),
            sem((2,)), sem((2,)), sem((2,)), sem((2,)), sem((2,)), pltpu.SemaphoreType.REGULAR,
            *gather_semaphores(1 + HALF),
        ],
        compiler_params=pltpu.CompilerParams(
            collective_id=0, has_side_effects=True, vmem_limit_bytes=VMEM_LIMIT
        ),
        name="train_step",
    )(*vectors, ub, qvb, seg, x, g, wqkv, wout, up, down)


def on_device_pair(
    inputs, segment_ids, first_gain, first_shift, qkv_weight, qv_bias, out_weight, out_bias,
    second_gain, second_shift, up_weight, up_bias, down_weight, down_bias, cotangent,
):
    rows, _, width = inputs.shape
    seq = segment_ids.shape[0]
    local = out_weight.shape[0]
    x = inputs.reshape(rows, width)
    g = cotangent.reshape(rows, width)
    seg = segment_ids.reshape(1, seq)
    height = width // PIECES
    wout = out_weight.reshape(4, 2, height, width)
    vectors = (first_gain, first_shift, out_bias, second_gain, second_shift, down_bias)
    wqkv = jnp.transpose(qkv_weight, (1, 0, 2))
    layer_output, input_grad, up_g, down_g, out_g, qkv_g, total, qv_g, up_bias_g = step_call(
        vectors, up_bias, qv_bias, seg, x, g, wqkv, wout, up_weight, down_weight
    )[:9]
    return (
        layer_output.reshape(rows, 1, width),
        input_grad.reshape(rows, 1, width),
        total[VEC_ROWS],
        total[VEC_ROWS + 1],
        jnp.transpose(qkv_g, (1, 0, 2)),
        qv_g,
        out_g.T,
        total[2],
        total[0],
        total[1],
        up_g,
        up_bias_g.reshape(-1),
        down_g.T,
        total[3],
    )


def solution(mesh):
    in_specs = (
        P("tensor", "dp", None),
        P(None, "dp"),
        P(),
        P(),
        P(None, None, "tensor"),
        P(None, "tensor"),
        P("tensor", None),
        P(),
        P(),
        P(),
        P(None, "tensor"),
        P("tensor"),
        P("tensor", None),
        P(),
        P("tensor", "dp", None),
    )
    out_specs = (
        P("tensor", "dp", None),
        P("tensor", "dp", None),
        P(),
        P(),
        P("dp", None, "tensor"),
        P(None, "tensor"),
        P("tensor", "dp"),
        P(),
        P(),
        P(),
        P("dp", "tensor"),
        P("tensor"),
        P("tensor", "dp"),
        P(),
    )
    pair = mesh.shape["tensor"] == 2 and mesh.shape["dp"] == Z_SIZE * Y_SIZE * CORES
    return jax.shard_map(
        on_device_pair if pair else on_device, mesh=mesh, in_specs=in_specs, out_specs=out_specs, check_vma=False
    )
```

```python
import functools

import jax
import jax.numpy as jnp
from jax import lax
from jax.experimental import pallas as pl
from jax.experimental.pallas import tpu as pltpu
from jax.sharding import PartitionSpec as P

HEAD_DIM = 64
MESH = pl.DeviceIdType.MESH
F32 = jnp.float32
BF16 = jnp.bfloat16
VMEM_LIMIT = 63 << 20


norm_eps = 1e-05


def layer_norm(value, gain, shift):
    row_mean = jnp.mean(value, axis=-1, keepdims=True)
    centred = value - row_mean
    variance = jnp.mean(centred * centred, axis=-1, keepdims=True)
    return centred * lax.rsqrt(variance + norm_eps) * gain + shift


def gelu_tanh(value):
    return (
        0.5
        * value
        * (1.0 + jnp.tanh(0.7978845608028654 * (value + 0.044715 * value * value * value)))
    )


def masked_scores(query_block, keys_all, seg_block, seg_all, row_start, block_rows, score_scale):
    scores = (
        jnp.einsum("qhd,khd->hqk", query_block, keys_all, preferred_element_type=jnp.float32)
        * score_scale
    )
    key_pos = jnp.arange(keys_all.shape[0], dtype=jnp.int32)
    query_pos = row_start + jnp.arange(block_rows, dtype=jnp.int32)
    allowed = (seg_block[:, None] == seg_all[None, :]) & (query_pos[:, None] >= key_pos[None, :])
    return jnp.where(allowed[None], scores, -1e30)


def attend_forward(queries, keys_all, values_all, seg_all, score_scale):
    seq_len = queries.shape[0]
    block_rows = min(512, seq_len)

    def one_block(block_index):
        row_start = block_index * block_rows
        query_block = lax.dynamic_slice_in_dim(queries, row_start, block_rows, 0)
        seg_block = lax.dynamic_slice_in_dim(seg_all, row_start, block_rows, 0)
        scores = masked_scores(
            query_block, keys_all, seg_block, seg_all, row_start, block_rows, score_scale
        )
        row_top = jnp.max(scores, axis=-1, keepdims=True)
        weights = jnp.exp(scores - row_top)
        row_total = jnp.sum(weights, axis=-1, keepdims=True)
        probs_low = (weights / row_total).astype(jnp.bfloat16)
        mixed = jnp.einsum(
            "hqk,khd->qhd", probs_low, values_all, preferred_element_type=jnp.float32
        )
        return (mixed, row_top + jnp.log(row_total))

    mixed, log_total = lax.map(one_block, jnp.arange(seq_len // block_rows, dtype=jnp.int32))
    return (mixed.reshape(seq_len, -1), log_total)


def attend_backward(queries, keys_all, values_all, seg_all, log_total, out_grad, score_scale):
    seq_len = queries.shape[0]
    block_rows = min(512, seq_len)

    def one_block(carry, block_index):
        key_grad, value_grad = carry
        row_start = block_index * block_rows
        query_block = lax.dynamic_slice_in_dim(queries, row_start, block_rows, 0)
        seg_block = lax.dynamic_slice_in_dim(seg_all, row_start, block_rows, 0)
        grad_block = lax.dynamic_slice_in_dim(out_grad, row_start, block_rows, 0)
        scores = masked_scores(
            query_block, keys_all, seg_block, seg_all, row_start, block_rows, score_scale
        )
        probs = jnp.exp(scores - log_total[block_index])
        probs_low = probs.astype(jnp.bfloat16)
        value_grad = value_grad + jnp.einsum(
            "hqk,qhd->khd", probs_low, grad_block, preferred_element_type=jnp.float32
        )
        prob_grad = jnp.einsum(
            "qhd,khd->hqk", grad_block, values_all, preferred_element_type=jnp.float32
        )
        row_dot = jnp.sum(probs * prob_grad, axis=-1, keepdims=True)
        score_grad = (probs * (prob_grad - row_dot)).astype(jnp.bfloat16)
        query_grad = (
            jnp.einsum("hqk,khd->qhd", score_grad, keys_all, preferred_element_type=jnp.float32)
            * score_scale
        )
        key_grad = (
            key_grad
            + jnp.einsum(
                "hqk,qhd->khd", score_grad, query_block, preferred_element_type=jnp.float32
            )
            * score_scale
        )
        return ((key_grad, value_grad), query_grad)

    zero_grads = jnp.zeros(keys_all.shape, jnp.float32)
    (key_grad, value_grad), query_grad = lax.scan(
        one_block, (zero_grads, zero_grads), jnp.arange(seq_len // block_rows, dtype=jnp.int32)
    )
    return (
        query_grad.reshape(seq_len, -1),
        key_grad.reshape(seq_len, -1),
        value_grad.reshape(seq_len, -1),
    )


def row_product(left, right, contract):
    return lax.dot_general(
        left, right, (((1,), (contract,)), ((), ())), preferred_element_type=jnp.float32
    )


def rows_contract(left, right):
    return lax.dot_general(
        left, right, (((0,), (0,)), ((), ())), preferred_element_type=jnp.float32
    )


def on_device(
    inputs,
    segment_ids,
    first_gain,
    first_shift,
    qkv_weight,
    qv_bias,
    out_weight,
    out_bias,
    second_gain,
    second_shift,
    up_weight,
    up_bias,
    down_weight,
    down_bias,
    cotangent,
):
    rows_dev, seq_count, model_width = inputs.shape
    tensor_count = lax.axis_size("tensor")
    tensor_rank = lax.axis_index("tensor")
    seq_len = rows_dev * tensor_count
    local_width = out_weight.shape[0]
    heads_dev = local_width // HEAD_DIM
    hidden_dev = up_weight.shape[1]
    local_rows = rows_dev * seq_count
    score_scale = HEAD_DIM ** (-0.5)
    residual_in = inputs.reshape(local_rows, model_width).astype(jnp.float32)
    gain_one = first_gain.astype(jnp.float32)
    shift_one = first_shift.astype(jnp.float32)
    gain_two = second_gain.astype(jnp.float32)
    shift_two = second_shift.astype(jnp.float32)
    normed_one, pull_one = jax.vjp(layer_norm, residual_in, gain_one, shift_one)
    first_local = normed_one.astype(jnp.bfloat16)
    first_rows = lax.all_gather(first_local, "tensor", axis=0, tiled=True)
    qkv_flat = qkv_weight.reshape(model_width, 3 * local_width)
    qkv_bias = jnp.concatenate(
        [
            qv_bias[0].astype(jnp.float32),
            jnp.zeros((local_width,), jnp.float32),
            qv_bias[1].astype(jnp.float32),
        ]
    )
    qkv_low = (jnp.dot(first_rows, qkv_flat, preferred_element_type=jnp.float32) + qkv_bias).astype(
        jnp.bfloat16
    )
    qkv_split = qkv_low.reshape(seq_len, seq_count, 3, heads_dev, HEAD_DIM)
    seq_index = 0
    mixed_one, log_one = attend_forward(
        qkv_split[:, seq_index, 0],
        qkv_split[:, seq_index, 1],
        qkv_split[:, seq_index, 2],
        segment_ids[:, seq_index],
        score_scale,
    )
    mixed_list = [mixed_one]
    log_list = [log_one]
    mixed_low = (
        jnp.stack(mixed_list, axis=1).reshape(seq_len * seq_count, local_width).astype(jnp.bfloat16)
    )
    attn_local = lax.psum_scatter(
        row_product(mixed_low, out_weight, 0), "tensor", scatter_dimension=0, tiled=True
    )
    residual_mid = residual_in + attn_local + out_bias.astype(jnp.float32)
    normed_two, pull_two = jax.vjp(layer_norm, residual_mid, gain_two, shift_two)
    second_local = normed_two.astype(jnp.bfloat16)
    second_rows = lax.all_gather(second_local, "tensor", axis=0, tiled=True)
    hidden_pre = jnp.dot(
        second_rows, up_weight, preferred_element_type=jnp.float32
    ) + up_bias.astype(jnp.float32)
    activated, pull_gelu = jax.vjp(gelu_tanh, hidden_pre)
    hidden_low = activated.astype(jnp.bfloat16)
    mlp_local = lax.psum_scatter(
        row_product(hidden_low, down_weight, 0).astype(jnp.bfloat16),
        "tensor",
        scatter_dimension=0,
        tiled=True,
    ).astype(jnp.float32)
    layer_output = (residual_mid + mlp_local + down_bias.astype(jnp.float32)).astype(jnp.bfloat16)
    layer_output = layer_output.reshape(rows_dev, seq_count, model_width)
    grad_local = cotangent.reshape(local_rows, model_width)
    grad_rows = lax.all_gather(grad_local, "tensor", axis=0, tiled=True)
    down_grad = rows_contract(hidden_low, grad_rows)
    hidden_grad = lax.dot_general(
        grad_rows, down_weight, (((1,), (1,)), ((), ())), preferred_element_type=jnp.float32
    )
    (pre_grad,) = pull_gelu(hidden_grad)
    pre_low = pre_grad.astype(jnp.bfloat16)
    up_sums = jnp.sum(pre_low, axis=0, dtype=jnp.float32)
    second_back = lax.all_gather(second_local, "tensor", axis=0, tiled=True)
    up_grad = rows_contract(second_back, pre_low)
    second_norm_grad = lax.psum_scatter(
        row_product(pre_low, up_weight, 1), "tensor", scatter_dimension=0, tiled=True
    )
    mid_from_norm, gain_two_grad, shift_two_grad = pull_two(second_norm_grad)
    residual_grad = grad_local.astype(jnp.float32) + mid_from_norm
    residual_low = residual_grad.astype(jnp.bfloat16)
    residual_rows = lax.all_gather(residual_low, "tensor", axis=0, tiled=True)
    out_grad_weight = rows_contract(mixed_low, residual_rows)
    mixed_grad = lax.dot_general(
        residual_rows, out_weight, (((1,), (1,)), ((), ())), preferred_element_type=jnp.float32
    ).astype(jnp.bfloat16)
    mixed_grad = mixed_grad.reshape(seq_len, seq_count, heads_dev, HEAD_DIM)
    seq_index = 0
    query_grad, key_grad, value_grad = attend_backward(
        qkv_split[:, seq_index, 0],
        qkv_split[:, seq_index, 1],
        qkv_split[:, seq_index, 2],
        segment_ids[:, seq_index],
        log_list[seq_index],
        mixed_grad[:, seq_index],
        score_scale,
    )
    query_list = [query_grad]
    key_list = [key_grad]
    value_list = [value_grad]
    qkv_grad = jnp.concatenate(
        [jnp.stack(query_list, axis=1), jnp.stack(key_list, axis=1), jnp.stack(value_list, axis=1)],
        axis=-1,
    )
    qkv_grad_low = qkv_grad.reshape(seq_len * seq_count, 3 * local_width).astype(jnp.bfloat16)
    qkv_sums = jnp.sum(qkv_grad_low, axis=0, dtype=jnp.float32)
    qv_sums = jnp.stack([qkv_sums[:local_width], qkv_sums[2 * local_width :]], axis=0)
    first_back = lax.all_gather(first_local, "tensor", axis=0, tiled=True)
    qkv_grad_weight = rows_contract(first_back, qkv_grad_low).reshape(model_width, 3, local_width)
    first_norm_grad = lax.psum_scatter(
        row_product(qkv_grad_low, qkv_flat, 1), "tensor", scatter_dimension=0, tiled=True
    )
    in_from_norm, gain_one_grad, shift_one_grad = pull_one(first_norm_grad)
    input_grad = (residual_grad + in_from_norm).reshape(rows_dev, seq_count, model_width)
    qkv_share, out_share, up_share, down_share = (
        lax.psum_scatter(qkv_grad_weight, "dp", scatter_dimension=0, tiled=True),
        lax.psum_scatter(out_grad_weight, "dp", scatter_dimension=1, tiled=True),
        lax.psum_scatter(up_grad, "dp", scatter_dimension=0, tiled=True),
        lax.psum_scatter(down_grad, "dp", scatter_dimension=1, tiled=True),
    )
    out_bias_part = jnp.sum(residual_low, axis=0, dtype=jnp.float32)
    down_bias_part = jnp.sum(grad_local, axis=0, dtype=jnp.float32)
    stacked = jnp.stack(
        [
            gain_one_grad,
            shift_one_grad,
            gain_two_grad,
            shift_two_grad,
            out_bias_part,
            down_bias_part,
        ],
        axis=0,
    )
    qv_full = lax.dynamic_update_slice(
        jnp.zeros((2, model_width), jnp.float32), qv_sums, (jnp.int32(0), tensor_rank * local_width)
    )
    up_full = lax.dynamic_update_slice(
        jnp.zeros((hidden_dev * tensor_count,), jnp.float32), up_sums, (tensor_rank * hidden_dev,)
    )
    stacked, qv_total, up_total = lax.psum((stacked, qv_full, up_full), ("dp", "tensor"))
    qv_share = lax.dynamic_slice_in_dim(qv_total, tensor_rank * local_width, local_width, 1)
    up_bias_share = lax.dynamic_slice_in_dim(up_total, tensor_rank * hidden_dev, hidden_dev, 0)
    return (
        layer_output,
        input_grad,
        stacked[0],
        stacked[1],
        qkv_share,
        qv_share,
        out_share,
        stacked[4],
        stacked[2],
        stacked[3],
        up_share,
        up_bias_share,
        down_share,
        stacked[5],
    )


Z_SIZE, Y_SIZE, CORES = 4, 2, 2


def place():
    dp = lax.axis_index("dp")
    side = lax.axis_index("tensor")
    return dp // 4, (dp // 2) % 2, dp % 2, side


def dev(z, y, core, side):
    return (z * 4 + y * 2 + core, side)


def peer_x():
    z, y, core, side = place()
    return dev(z, y, core, 1 - side)


def peer_y():
    z, y, core, side = place()
    return dev(z, 1 - y, core, side)


def peer_core():
    z, y, core, side = place()
    return dev(z, y, 1 - core, side)


def peer_z(step):
    z, y, core, side = place()
    return dev((z + step) % 4, y, core, side)


def greet():
    peers = [peer_x(), peer_y(), peer_core()] + [peer_z(k) for k in (1, 2, 3)]
    barrier = pltpu.get_barrier_semaphore()
    for peer in peers:
        pl.semaphore_signal(barrier, inc=1, device_id=peer, device_id_type=MESH)
    return lambda: pl.semaphore_wait(barrier, len(peers))


def remote(src, dst, send_sem, recv_sem, peer):
    return pltpu.make_async_remote_copy(
        src_ref=src, dst_ref=dst, send_sem=send_sem, recv_sem=recv_sem, device_id=peer, device_id_type=MESH
    )


def dot_nn(a, b):
    return lax.dot_general(a, b, (((1,), (0,)), ((), ())), preferred_element_type=F32)


def dot_nt(a, b):
    return lax.dot_general(a, b, (((1,), (1,)), ((), ())), preferred_element_type=F32)


def dot_tn(a, b):
    return lax.dot_general(a, b, (((0,), (0,)), ((), ())), preferred_element_type=F32)


def norm_parts(value):
    mean = jnp.mean(value, axis=-1, keepdims=True)
    centred = value - mean
    rstd = lax.rsqrt(jnp.mean(centred * centred, axis=-1, keepdims=True) + norm_eps)
    return centred * rstd, rstd


def norm_back(grad, gain, xhat, rstd):
    e = grad * gain
    return rstd * (e - jnp.mean(e, axis=-1, keepdims=True) - xhat * jnp.mean(e * xhat, axis=-1, keepdims=True))


def head_lanes(h):
    lane = lax.broadcasted_iota(jnp.int32, (1, 2 * HEAD_DIM), 1)
    return (lane // HEAD_DIM) == h


def only_head(value, h):
    return jnp.where(head_lanes(h), value, jnp.zeros_like(value))


def total_of(row):
    return jnp.sum(row, axis=0, keepdims=True)


GAIN_1, SHIFT_1, OUT_BIAS, GAIN_2, SHIFT_2, DOWN_BIAS = range(6)
PIECES = 16
HIDDEN_BLOCK = 512


def gather(source, target, sems):
    x_s, x_r, z_s, z_r, y_s, y_r, c_s, c_r = sems
    z, y, core, side = place()

    def copies(dp, q, send, recv, peer, views=target):
        pairs = zip(views(dp, q), target(dp, q))
        return [remote(s, d, send.at[a], recv.at[a], peer) for a, (s, d) in enumerate(pairs)]

    def number(zz, yy, cc):
        return zz * 4 + yy * 2 + cc

    def from_z(k):
        return (z + 4 - k) % 4

    def x_copies(q):
        return copies(number(z, y, core), q, x_s.at[q], x_r.at[q], peer_x(), source)

    def z_sends(q, k):
        return copies(number(z, y, core), q, z_s.at[q, k], z_r.at[q, k], peer_z(k))

    def z_recvs(q, k):
        return copies(number(from_z(k), y, core), q, z_s.at[q, k], z_r.at[q, k], peer_z(k))

    def y_copies(q, k, yy):
        return copies(number(from_z(k), yy, core), q, y_s.at[q, k], y_r.at[q, k], peer_y())

    def c_copies(q, k, far, cc):
        yy = (1 - y) if far else y
        slot = 4 * far + k
        return copies(number(from_z(k), yy, cc), q, c_s.at[q, slot], c_r.at[q, slot], peer_core())

    def start(list_of):
        for copy in list_of:
            copy.start()

    def first(q):
        for copy in x_copies(q):
            copy.wait()
        for k in (2, 1, 3):
            start(z_sends(q, k))
        start(y_copies(q, 0, y))
        start(c_copies(q, 0, 0, core))

    def second(q):
        for k in (1, 3, 2):
            for copy in z_recvs(q, k):
                copy.wait_recv()
            start(y_copies(q, k, y))
            start(c_copies(q, k, 0, core))

    def third(q):
        for k in range(4):
            for copy in y_copies(q, k, 1 - y):
                copy.wait_recv()
            start(c_copies(q, k, 1, core))

    def last(q):
        for k in range(4):
            for far in (0, 1):
                for copy in c_copies(q, k, far, 1 - core):
                    copy.wait_recv()

    def sent(q):
        for k in range(4):
            if k > 0:
                for copy in z_sends(q, k):
                    copy.wait_send()
            for copy in y_copies(q, k, y):
                copy.wait_send()
            for far in (0, 1):
                for copy in c_copies(q, k, far, core):
                    copy.wait_send()

    return first, second, third, last, sent, x_copies


def gather_semaphores(q):
    sem = pltpu.SemaphoreType.DMA
    return [sem((q, 2))] * 2 + [sem((q, 4, 2))] * 4 + [sem((q, 8, 2))] * 2


def hidden_views(arrays, dp, b):
    up, down = arrays
    n_up, n_down = up.shape[0] // PIECES, HIDDEN_BLOCK // PIECES
    return [
        up.at[pl.ds(pl.multiple_of(dp * n_up, n_up), n_up), pl.ds(b * HIDDEN_BLOCK, HIDDEN_BLOCK)],
        down.at[pl.ds(pl.multiple_of(b * HIDDEN_BLOCK + dp * n_down, n_down), n_down)],
    ]


CROSS_FIRST = 2
ORDER = (("o", 2), ("t", 0), ("o", 3), ("t", 1), ("t", 2), ("o", 1), ("o", 0), ("t", 3))
SLOT = (0, 1, 2, 3, 4, 5, 0, 1, 2, 4, 0, 1)
S_SLOTS = 6
CROSSING = (1, 3)
DELAYED = 5
PLACE = (None, None, 0, None, 1, 2, 3, 4, 5)
HALF = len(ORDER) // 2
N_MLP = 2 * HALF
N_ALL = N_MLP + 4
VEC_ROWS = 8
A_TICKS = {
    "start": [("g_first", 0)],
    "block": [("g_second", 0)],
    "early": [("g_first", 1), ("g_third", 0)],
    "middle": [("g_first", 2), ("g_second", 1)],
    "late": [("g_first", 3), ("g_third", 1), ("g_second", 2)],
    "end": [("g_third", 2)],
}
B_START = [("g_first", 4), ("g_second", 3)]
B_TICKS = {
    1: [("g_third", 3)], 2: [("g_second", 4)], 4: [("g_third", 4)], 7: [("z_second", 0), ("second", 2)],
}
C_TICKS = {
    0: (
        [("second", 4)], [(3, [("second", 6)])], [(1, [("z_third", 0), ("third", 2)])], [(1, [("third", 4)])],
        [(3, [("second", 7)])],
    ),
    1: (
        [], [(2, [("second", 4)])], [(1, [("third", 2)])], [(3, [("second", 6)])], [(2, [("z_third", 0)])],
        [(2, [("third", 4)])], [(3, [("second", 7)])],
    ),
}
END_TICKS = [("third", 6)]
MORE_TICKS = ([("second", 8), ("third", 7)], [("vec", (0, 2)), ("second", 9)])
TAIL = [
    ("third", 8), ("vec", (1, 1)), ("push", 11), ("vec", (0, 3)), ("second", 5), ("third", 9), ("second", 10),
    ("vec", (1, 2)), ("third", 5), ("second", 11), ("vec", (1, 3)), ("third", 10), ("third", 11), ("fourth", 0),
    ("fourth", 1), ("fourth", 2), ("vec", (0, 4)), ("vec", (1, 4)),
]


def lookup(table, p):
    if isinstance(p, int):
        return table[p]
    value = jnp.int32(table[0])
    for n in range(1, len(table)):
        value = jnp.where(p == n, jnp.int32(table[n]), value)
    return value


def before(p):
    return max((n for n in range(p) if SLOT[n] == SLOT[p]), default=None)


def hidden_of(p):
    return lookup([b for _, b in ORDER], p)


def is_other(p):
    if isinstance(p, int):
        return ORDER[p][0] == "t"
    return lookup([int(s == "t") for s, _ in ORDER], p) == 1


def step_kernel(
    g1_ref, s1_ref, ob_ref, g2_ref, s2_ref, db_ref, ub_ref, qvb_ref, seg_ref,
    x_hbm, g_hbm, wqkv_hbm, wout_hbm, up_own, down_own,
    out_ref, dinr_ref, upg_ref, downg_ref, og_ref, qkvg_ref, vec_ref, qvg_ref, ubg_ref,
    a1_hbm, qkv_hbm, mix_hbm, up_oth, down_oth,
    wout_ref, mixt_ref, lse_ref, par_ref, ubo_ref, ubt_ref, din_ref, stage_ref,
    dkv_ref, dm_ref, dsend_ref, send_ref, dq_ref, grad_ref, core_ref, sum_ref, ybuf, zbuf, zf_buf, yf_buf, xfirst, xsend, xbuf,
    vsum, vrecv,
    a_s, a_r, m_s, m_r, b_s, b_r, l_sem,
    c_s, c_r, y_s, y_r, z_s, z_r, xf_s, xf_r, x_s, x_r, v_s, v_r, dm_s, dm_r, o_s, o_r, out_sem, free_sem, *gather_sems,
):
    rows, width = din_ref.shape
    seq = 2 * rows
    local = dm_ref.shape[1]
    block = rows // 2
    piece = rows // 4
    hb = HIDDEN_BLOCK
    nx = CROSS_FIRST
    half, n_mlp, n_all = HALF, N_MLP, N_ALL
    z, y, core, side = place()
    partner = peer_x()
    own = pl.multiple_of(side * rows, rows)
    theirs = pl.multiple_of((1 - side) * rows, rows)
    scale = HEAD_DIM**-0.5
    vmem = pltpu.VMEM
    sem = pltpu.SemaphoreType.DMA

    def out_views(ref, dp):
        return [ref.at[dp // 4, dp // 2 % 2, pl.ds(dp % 2 * 32, 32)]]

    def gather_source(dp, q):
        return out_views(wout_hbm, dp) if q == 0 else hidden_views((up_own, down_own), dp, q - 1)

    def gather_target(dp, q):
        return out_views(wout_ref.at[1], dp) if q == 0 else hidden_views((up_oth, down_oth), dp, q - 1)

    g_first, g_second, g_third, g_last, g_sent, g_x = gather(gather_source, gather_target, gather_sems)

    def g_start(q):
        for copy in g_x(q):
            copy.start()

    def cols_of(p):
        return 2 * hb if p <= n_mlp else hb

    def slot_of(p):
        return lookup(SLOT, p)

    def core_copy(p, cols):
        slot = p % 2
        lanes = pl.ds(0, cols)
        return remote(
            grad_ref.at[slot, :, 1 - core, :, lanes], core_ref.at[slot, :, :, lanes], c_s.at[slot], c_r.at[slot],
            peer_core(),
        )

    def place_of(p, cols):
        if isinstance(p, int) and p > n_mlp:
            n = p - n_mlp - 1
            return PLACE[n_mlp] + 1 + n // 2, pl.ds(n % 2 * hb, hb)
        return lookup([n or 0 for n in PLACE], p), pl.ds(0, cols)

    def y_copy(p, cols):
        s, lanes = place_of(p, cols)
        src = sum_ref.at[slot_of(p), :, 1 - y, :, pl.ds(0, cols)]
        return remote(src, ybuf.at[s, :, :, lanes], y_s.at[p], y_r.at[p], peer_y())

    def z_copy(p, k, cols):
        s, lanes = place_of(p, cols)
        src, dst = ybuf.at[s, (z + k) % 4, :, lanes], zbuf.at[s, k - 1, :, lanes]
        return remote(src, dst, z_s.at[p, k - 1], z_r.at[p, k - 1], peer_z(k))

    def zf_copy(k):
        return remote(sum_ref.at[SLOT[0], (z + k) % 4], zf_buf.at[k - 1], z_s.at[0, k - 1], z_r.at[0, k - 1], peer_z(k))

    def yf_copy():
        return remote(yf_buf.at[1 - y], yf_buf.at[2], y_s.at[0], y_r.at[0], peer_y())

    def z_second(p):
        for k in (1, 2, 3):
            zf_copy(k).wait_recv()
        total = sum_ref[SLOT[0], z].astype(F32)
        for k in (1, 2, 3):
            total = total + zf_buf[k - 1].astype(F32)
        yf_buf[pl.ds(0, 2)] = total.astype(BF16)
        yf_copy().start()

    def z_third(p):
        yf_copy().wait()
        mlp_write(hidden_of(p), yf_buf[y].astype(F32) + yf_buf[2].astype(F32))

    def xfirst_copy(n):
        return remote(sum_ref.at[SLOT[CROSSING[n]]], xfirst.at[n], xf_s.at[n], xf_r.at[n], partner)

    def x_copy(n):
        lanes = pl.ds(0, 2 * hb if n < half - nx else hb)
        return remote(xsend.at[n, :, lanes], xbuf.at[n, :, lanes], x_s.at[n], x_r.at[n], partner)

    def produced(p, cols):
        @pl.when(p >= 2)
        def _():
            pl.semaphore_wait(free_sem, 1)

        core_copy(p, cols).start()

    def consume(p, cols):
        slot = p % 2
        lanes = pl.ds(0, cols)
        copy = core_copy(p, cols)
        copy.wait()
        for n in range(n_all) if not isinstance(p, int) else (p,):
            if before(n) is not None and n < n_mlp - 1 and not isinstance(p, int):

                @pl.when(p == n)
                def _():
                    sent(before(n))

            elif before(n) is not None and isinstance(p, int):
                sent(before(n))
        total = grad_ref[slot, :, core, :, lanes].astype(F32) + core_ref[slot, :, :, lanes].astype(F32)
        at = sum_ref.at[slot_of(p), :, :, :, lanes]
        at[...] = total.astype(BF16).reshape(4, 2, 64, cols)

        @pl.when(p < n_all - 2)
        def _():
            pl.semaphore_signal(free_sem, inc=1, device_id=peer_core(), device_id_type=MESH)

    def sent(p):
        if p == 0:
            for k in (1, 2, 3):
                zf_copy(k).wait_send()
        elif p in CROSSING:
            xfirst_copy(CROSSING.index(p)).wait_send()
        else:
            y_copy(p, cols_of(p)).wait_send()

    def push_one(p, cols):
        if p == 0:
            for k in (2, 1, 3):
                zf_copy(k).start()
        elif p in CROSSING:
            xfirst_copy(CROSSING.index(p)).start()
        else:
            if p < n_mlp and not is_other(p) and hidden_of(p) < nx:
                add_first(p)
            y_copy(p, cols).start()

    def push(p, cols):
        if isinstance(p, int):
            push_one(p, cols)
            return
        for n in range(n_mlp - 1):
            if n not in (DELAYED, CROSSING[1]):

                @pl.when(p == n)
                def _():
                    push_one(n, cols)

    def add_first(p):
        b = hidden_of(p)
        xfirst_copy(b).wait_recv()
        sum_ref[slot_of(p)] = (
            sum_ref[slot_of(p)].astype(F32) + xfirst[b].astype(F32)
        ).astype(BF16)

    def second(p):
        cols = cols_of(p)
        s, lanes = place_of(p, cols)
        y_copy(p, cols).wait_recv()
        ybuf[s, :, :, lanes] = (
            sum_ref[slot_of(p), :, y, :, pl.ds(0, cols)].astype(F32) + ybuf[s, :, :, lanes].astype(F32)
        ).astype(BF16)
        for k in (2, 1, 3):
            z_copy(p, k, cols).start()

    def mlp_write(b, total, more=False):
        cols = pl.ds(b * hb, hb)
        for ref, part in ((upg_ref, total[:, :hb]), (downg_ref, total[:, hb:])):
            ref[:, cols] = ref[:, cols] + part if more else part

    def third(p):
        cols = cols_of(p)
        s, lanes = place_of(p, cols)
        for k in (1, 2, 3):
            z_copy(p, k, cols).wait_recv()
        total = ybuf[s, z, :, lanes].astype(F32)
        for k in (1, 2, 3):
            total = total + zbuf[s, k - 1, :, lanes].astype(F32)
        if p < n_mlp and is_other(p):
            n = hidden_of(p) - nx
            xsend[n] = total.astype(BF16)
            x_copy(n).start()
        elif p < n_mlp:
            mlp_write(hidden_of(p), total)
        elif p == n_mlp:
            og_ref[...] = total[:, :hb]
            xsend[half - nx, :, pl.ds(0, hb)] = total[:, hb:].astype(BF16)
            x_copy(half - nx).start()
        else:
            qkvg_ref[p - n_mlp - 1] = total

    def fourth(n):
        x_copy(n).wait_recv()
        if n < half - nx:
            mlp_write(n + nx, xbuf[n].astype(F32), more=True)
        else:
            og_ref[...] += xbuf[n, :, pl.ds(0, hb)].astype(F32)

    def v_copy(w, n, peer, slot):
        return remote(vsum.at[w, n], vrecv.at[w, slot], v_s.at[w, slot], v_r.at[w, slot], peer)

    def z_vec(w, k, source):
        return remote(vsum.at[w, 2], vrecv.at[w, 2 + source], v_s.at[w, 2 + k], v_r.at[w, 2 + source], peer_z(k))

    def vectors(w, n):
        if n == 0:
            v_copy(w, 0, peer_core(), 0).start()
        elif n == 1:
            v_copy(w, 0, peer_core(), 0).wait()
            vsum[w, 1] = vsum[w, 0] + vrecv[w, 0]
            v_copy(w, 1, peer_y(), 1).start()
        elif n == 2:
            v_copy(w, 1, peer_y(), 1).wait()
            vsum[w, 2] = vsum[w, 1] + vrecv[w, 1]
            for k in (1, 2, 3):
                z_vec(w, k, z).start()
        elif n == 3:
            for k in (1, 2, 3):
                z_vec(w, k, z).wait_send()
                z_vec(w, k, (z + k) % 4).wait_recv()
            vrecv[w, 2 + z] = vsum[w, 2]
            vsum[w, 3] = (vrecv[w, 2] + vrecv[w, 3]) + (vrecv[w, 4] + vrecv[w, 5])
            v_copy(w, 3, partner, 6).start()
        elif n == 4:
            v_copy(w, 3, partner, 6).wait()
            vec_ref[pl.ds(w * VEC_ROWS, VEC_ROWS)] = vsum[w, 3] + vrecv[w, 6]

    stages = dict(
        second=second, third=third, fourth=fourth, z_second=z_second, z_third=z_third,
        push=lambda p: push(p, cols_of(p)), g_first=g_first, g_second=g_second, g_third=g_third, g_last=g_last
    )

    def run(names):
        for name, arg in names:
            if name == "vec":
                vectors(*arg)
            else:
                stages[name](arg)

    dm_own = dm_ref.at[pl.ds(own, rows)]

    def dm_copy(b):
        at = pl.ds(pl.multiple_of(own + b * block, block), block)
        return remote(dsend_ref.at[b], dm_ref.at[at], dm_s.at[b], dm_r.at[b], partner)

    def dm_from(b):
        at = pl.ds(pl.multiple_of((1 - side) * rows + b * block, block), block)
        return remote(dsend_ref.at[b], dm_ref.at[at], dm_s.at[b], dm_r.at[b], partner)

    def out_copy(j):
        return pltpu.make_async_copy(send_ref.at[j], out_ref.at[j], out_sem.at[j])

    def o_copy(j):
        return remote(send_ref.at[j], xfirst.at[0, pl.ds(2 * j, 2)], o_s.at[j], o_r.at[j], partner)

    all_here = greet()
    for n, vector in enumerate((g1_ref, s1_ref, ob_ref, g2_ref, s2_ref, db_ref)):
        par_ref[pl.ds(n, 1)] = vector[...].astype(F32).reshape(1, width)
    for n in range(half):
        ubo_ref[pl.ds(n, 1)] = ub_ref[pl.ds(n * hb, hb)].astype(F32).reshape(1, hb)
    bias_copy = remote(ubo_ref, ubt_ref, b_s, b_r, partner)
    a1_ref = sum_ref

    def a1_copy(which, b):
        return remote(a1_ref.at[which, b], a1_ref.at[which, b], a_s.at[b], a_r.at[b], partner)

    def wqkv_parts(ref):
        return [(wqkv_hbm.at[n], ref.at[:, pl.ds(n * local, local)]) for n in range(3)]

    def wout_own():
        return wout_ref[0].reshape(local, width)

    def wout_other():
        return wout_ref[1].reshape(local, width)

    def ahead(x_ref, wqkv_ref, qkv_ref, mix_ref, mask_ref):
        loads = [
            pltpu.make_async_copy(src, dst, l_sem.at[n])
            for n, (src, dst) in enumerate(((x_hbm, x_ref), (wout_hbm, wout_ref.at[0]), *wqkv_parts(wqkv_ref)))
        ]
        for load in loads:
            load.start()
        gain = par_ref[pl.ds(GAIN_1, 1)]
        shift = par_ref[pl.ds(SHIFT_1, 1)]
        loads[0].wait()
        for b in range(4):
            xhat, _ = norm_parts(x_ref[pl.ds(b * piece, piece)].astype(F32))
            a1_ref[side, b] = (xhat * gain + shift).astype(BF16).reshape(2, 64, width)
            if b == 0:
                all_here()
                g_start(0)
            a1_copy(side, b).start()
            if b < 2:
                g_start(1 + b)
        bias_copy.start()
        g_start(3)

        def project(left, base, count):
            at = pl.ds(pl.multiple_of(base, block), count)
            for part in range(3):
                cols = pl.ds(part * local, local)
                value = dot_nn(left, wqkv_ref[:, cols])
                if part != 1:
                    value = value + qvb_ref[pl.ds(part // 2, 1)].astype(F32)
                qkv_ref[at, cols] = value.astype(BF16)

        for load in loads[2:]:
            load.wait()
        project(a1_ref[side].reshape(rows, width), own, rows)

        def mix_copy(j):
            at = pl.ds(pl.multiple_of(theirs + j * block, block), block)
            far = mixt_ref.at[pl.ds(j * block, block)]
            return remote(mix_ref.at[at], far, m_s.at[j], m_r.at[j], partner)

        seg_row = seg_ref[...].astype(F32)
        seg_col = jnp.broadcast_to(seg_row, (8, seq)).T[:, :1]
        run(A_TICKS["start"])

        @pl.when(side == 1)
        def _():
            run(A_TICKS["block"])

        for i in range(4):
            lo = i * block
            keys = lo + block
            is_theirs = side == (1 if i < 2 else 0)
            at = pl.ds(lo, block)
            if i == 1:

                @pl.when(side == 0)
                def _():
                    run(A_TICKS["block"])

            @pl.when(is_theirs)
            def _():
                j = i % 2
                run(A_TICKS["middle" if j else "early"])
                for b in (2 * j, 2 * j + 1):
                    a1_copy(1 - side, b).wait_recv()
                project(a1_ref[1 - side, pl.ds(2 * j, 2)].reshape(block, width), lo, block)

            same = seg_col[:keys] == seg_row[:, lo : lo + block]
            k_pos = lax.broadcasted_iota(jnp.int32, (keys, block), 0)
            q_pos = lo + lax.broadcasted_iota(jnp.int32, (keys, block), 1)
            mask_ref[pl.ds(0, keys)] = jnp.where(same & (q_pos >= k_pos), 0.0, -1e30)

            def pair(hp, _):
                base = pl.multiple_of(hp * 2 * HEAD_DIM, 2 * HEAD_DIM)
                cols = pl.ds(base, 2 * HEAD_DIM)
                q2 = qkv_ref[at, cols]
                k2 = qkv_ref[pl.ds(0, keys), pl.ds(pl.multiple_of(local + base, 128), 2 * HEAD_DIM)]
                v2 = qkv_ref[pl.ds(0, keys), pl.ds(pl.multiple_of(2 * local + base, 128), 2 * HEAD_DIM)]
                out = jnp.zeros((block, 2 * HEAD_DIM), F32)
                for h in range(2):
                    scores = dot_nt(k2, only_head(q2, h)) * scale + mask_ref[pl.ds(0, keys)]
                    top = jnp.max(scores, axis=0, keepdims=True)
                    weights = jnp.exp(scores - top)
                    total = total_of(weights)
                    lse_ref[pl.ds(2 * hp + h, 1), at] = top + jnp.log(total)
                    out += dot_tn((weights * (1.0 / total)).astype(BF16), only_head(v2, h))
                mix_ref[at, cols] = out.astype(BF16)
                return 0

            lax.fori_loop(0, local // (2 * HEAD_DIM), pair, 0)

            @pl.when(is_theirs)
            def _():
                mix_copy(i % 2).start()
                if i % 2:
                    g_start(4)
                    run(A_TICKS["late"])

        saves = [
            pltpu.make_async_copy(src, dst, l_sem.at[n])
            for n, (src, dst) in enumerate(((qkv_ref, qkv_hbm), (mix_ref, mix_hbm), (a1_ref.at[pl.ds(0, 2)], a1_hbm)), start=5)
        ]
        for save in saves:
            save.start()
        loads[1].wait()
        g_last(0)
        for j in range(2):
            at = pl.ds(j * block, block)
            mix_copy(j).wait_recv()
            mine = dot_nn(mix_ref[pl.ds(pl.multiple_of(own + j * block, block), block)], wout_own())
            din_ref[at] = (
                x_ref[at].astype(F32) + (mine + dot_nn(mixt_ref[at], wout_other())) + par_ref[pl.ds(OUT_BIAS, 1)]
            )
        run(A_TICKS["end"])
        for save in saves:
            save.wait()
        for j in range(2):
            mix_copy(j).wait_send()
        for b in range(4):
            a1_copy(side, b).wait_send()
        bias_copy.wait()

    pl.run_scoped(
        ahead,
        vmem((rows, width), BF16), vmem((width, 3 * local), BF16), vmem((seq, 3 * local), BF16), vmem((seq, local), BF16),
        vmem((seq, block), F32),
    )

    h_ref = din_ref

    def feed(g_ref, a2_ref, a2t_ref, gt_ref, wu_ref, wd_ref, in_sem, w_sem):
        load_g = pltpu.make_async_copy(g_hbm, g_ref, in_sem)
        load_g.start()

        def fetch(b, up, down, slot):
            at = pl.ds(pl.multiple_of(b * hb, hb), hb)
            return (
                pltpu.make_async_copy(up.at[:, at], wu_ref.at[slot], w_sem.at[slot, 0]),
                pltpu.make_async_copy(down.at[at], wd_ref.at[slot], w_sem.at[slot, 1]),
            )

        def fetch_start(p, slot):
            for n in range(n_mlp):
                if is_other(n):

                    @pl.when(p == n)
                    def _():
                        g_last(1 + hidden_of(n))

            @pl.when(is_other(p))
            def _():
                for copy in fetch(hidden_of(p), up_oth, down_oth, slot):
                    copy.start()

            @pl.when(jnp.logical_not(is_other(p)))
            def _():
                for copy in fetch(hidden_of(p), up_own, down_own, slot):
                    copy.start()

        fetch_start(jnp.int32(0), 0)
        gain = par_ref[pl.ds(GAIN_2, 1)]
        xhat, _ = norm_parts(h_ref[...])
        a2 = (xhat * gain + par_ref[pl.ds(SHIFT_2, 1)]).astype(BF16)
        a2_ref[...] = a2
        a2t_ref[...] = a2.T
        load_g.wait()
        gt_ref[...] = g_ref[...].T
        dkv_ref[...] = jnp.zeros_like(dkv_ref)
        acc_ref = dkv_ref.at[pl.ds(0, rows)]
        da2_ref = dkv_ref.at[pl.ds(rows, rows)]

        def step(p, _):
            slot = p % 2
            for copy in fetch(0, up_own, down_own, slot):
                copy.wait()

            @pl.when(p + 1 < n_mlp)
            def _():
                fetch_start(p + 1, 1 - slot)

            b = hidden_of(p)
            wu, wd = wu_ref[slot], wd_ref[slot]
            u = dot_nn(a2_ref[...], wu) + jnp.where(is_other(p), ubt_ref[pl.ds(b, 1)], ubo_ref[pl.ds(b, 1)])
            tanh = jnp.tanh(0.7978845608028654 * (u + 0.044715 * u * u * u))
            hidden = (0.5 * u * (1.0 + tanh)).astype(BF16)
            slope = 0.5 * (1.0 + tanh) + 0.5 * u * (1.0 - tanh * tanh) * (
                0.7978845608028654 * (1.0 + 3.0 * 0.044715 * u * u)
            )
            acc_ref[...] += dot_nn(hidden, wd)
            du = (dot_nt(g_ref[...], wd) * slope).astype(BF16)
            where_side = jnp.where(is_other(p), 1 - side, side)
            lanes = pl.ds(pl.multiple_of((b % 2) * hb, hb), hb)
            vsum[0, 0, pl.ds(4 + where_side * (half // 2) + b // 2, 1), lanes] = total_of(du.astype(F32))
            da2_ref[...] += dot_nt(du, wu)
            grad_ref[slot, :, :, :, pl.ds(0, hb)] = dot_nn(a2t_ref[...], du).astype(BF16).reshape(8, 2, 64, hb)
            grad_ref[slot, :, :, :, pl.ds(hb, hb)] = dot_nn(gt_ref[...], hidden).astype(BF16).reshape(8, 2, 64, hb)
            produced(p, 2 * hb)

            for n, names in B_TICKS.items():

                @pl.when(p == n)
                def _():
                    run(names)

            @pl.when(p >= 1)
            def _():
                consume(p - 1, 2 * hb)
                push(p - 1, 2 * hb)

            return 0

        vsum[0, 0] = jnp.zeros(vsum.shape[2:], F32)
        vsum[1, 0] = jnp.zeros(vsum.shape[2:], F32)
        run(B_START)
        lax.fori_loop(0, n_mlp, step, 0)

        piece = rows // 4
        sums = [jnp.zeros((1, width), F32) for _ in range(4)]
        for b in range(4):
            at = pl.ds(b * piece, piece)
            h = h_ref[at]
            g = g_ref[at].astype(F32)
            out = (h + acc_ref[at] + par_ref[pl.ds(DOWN_BIAS, 1)]).astype(BF16)
            send_ref[b // 2, b % 2] = out.reshape(2, 64, width)
            xhat, rstd = norm_parts(h)
            da2 = da2_ref[at]
            dh = g + norm_back(da2, gain, xhat, rstd)
            din_ref[at] = dh
            for n, term in enumerate((da2 * xhat, da2, dh.astype(BF16).astype(F32), g)):
                sums[n] = sums[n] + total_of(term)
        for n in range(4):
            vsum[0, 0, pl.ds(n, 1)] = sums[n]
        vectors(0, 0)
        for j in range(2):
            out_copy(j).start()

    pl.run_scoped(
        feed,
        vmem((rows, width), BF16), vmem((rows, width), BF16), vmem((width, rows), BF16),
        vmem((width, rows), BF16), vmem((2, width, hb), BF16), vmem((2, hb, width), BF16), sem, sem((2, 2)),
    )

    def attend(qkv_ref, mix_ref, wqkv_ref, mask_ref, dhl_ref, in_sem):
        x_ref, dqkv_ref = dhl_ref, qkv_ref
        moves = [
            pltpu.make_async_copy(src, dst, in_sem.at[n])
            for n, (src, dst) in enumerate((
                (mix_hbm, mix_ref), (qkv_hbm, qkv_ref), (x_hbm, x_ref), (a1_hbm, wout_ref), *wqkv_parts(wqkv_ref),
            ))
        ]
        for n in (0, 1, 4, 5, 6):
            moves[n].start()
        dhl_ref[...] = din_ref[...].astype(BF16)
        consume(n_mlp - 1, 2 * hb)
        push(n_mlp - 1, 2 * hb)
        for b in (1, 0):
            dsend_ref[b] = dot_nt(dhl_ref[pl.ds(b * block, block)], wout_other()).astype(BF16)
            dm_copy(b).start()
        for b in range(1, nx):
            xfirst_copy(b).start()
        dm_own[...] = dot_nt(dhl_ref[...], wout_own()).astype(BF16)
        g_sent(0)
        moves[3].start()
        moves[0].wait()
        p = n_mlp
        for part in range(2):
            mixed = mixt_ref[...] if part else mix_ref[pl.ds(own, rows)]
            grad = dot_tn(dhl_ref[...], mixed).astype(BF16)
            grad_ref[p % 2, :, :, :, pl.ds(part * hb, hb)] = grad.reshape(8, 2, 64, hb)
        produced(p, 2 * hb)
        moves[2].start()
        dkv_ref[...] = jnp.zeros_like(dkv_ref)
        seg_row = seg_ref[...].astype(F32)
        seg_col = jnp.broadcast_to(seg_row, (8, seq)).T[:, :1]
        moves[1].wait()
        for j in range(2):
            out_copy(j).wait()

        def task(i, keys, stage="all", ticks=()):
            lo, start, count = i * block, keys[0], keys[1] - keys[0]
            at, among = pl.ds(lo, block), pl.ds(start, count)
            same = seg_col[start : start + count] == seg_row[:, lo : lo + block]
            k_pos = start + lax.broadcasted_iota(jnp.int32, (count, block), 0)
            q_pos = lo + lax.broadcasted_iota(jnp.int32, (count, block), 1)
            mask_ref[pl.ds(0, count)] = jnp.where(same & (q_pos >= k_pos), 0.0, -1e30)

            def pair(hp, _):
                base = pl.multiple_of(hp * 2 * HEAD_DIM, 2 * HEAD_DIM)
                cols = pl.ds(base, 2 * HEAD_DIM)
                v_cols = pl.ds(pl.multiple_of(local + base, 128), 2 * HEAD_DIM)
                q2 = qkv_ref[at, cols]
                k2 = qkv_ref[among, v_cols]
                v2 = qkv_ref[among, pl.ds(pl.multiple_of(2 * local + base, 128), 2 * HEAD_DIM)]
                g2 = dm_ref[at, cols]
                turned = (g2.astype(F32) * mix_ref[at, cols].astype(F32)).T
                dq = jnp.zeros((block, 2 * HEAD_DIM), F32)
                dk = jnp.zeros((count, 2 * HEAD_DIM), F32)
                dv = jnp.zeros((count, 2 * HEAD_DIM), F32)
                for h in range(2):
                    qh = only_head(q2, h)
                    gh = only_head(g2, h)
                    row_dot = total_of(turned[h * HEAD_DIM : (h + 1) * HEAD_DIM])
                    offset = mask_ref[pl.ds(0, count)] - lse_ref[pl.ds(2 * hp + h, 1), at]
                    probs = jnp.exp(dot_nt(k2, qh) * scale + offset)
                    dscore = (probs * (dot_nt(v2, gh) - row_dot)).astype(BF16)
                    dv += dot_nn(probs.astype(BF16), gh)
                    dk += dot_nn(dscore, qh)
                    dq += dot_tn(dscore, only_head(k2, h))
                if stage == "first":
                    dq_ref[i - 2, :, cols] = dq
                else:
                    if stage == "last":
                        dq = dq + dq_ref[i - 2, :, cols]
                    dqkv_ref[at, cols] = (dq * scale).astype(BF16)
                dkv_ref[among, cols] += dk
                dkv_ref[among, v_cols] += dv
                for n, names in ticks:

                    @pl.when(hp == n)
                    def _():
                        run(names)

                return 0

            lax.fori_loop(0, local // (2 * HEAD_DIM), pair, 0)

        def finish(i, send):
            at = pl.ds(i * block, block)
            dqkv_ref[at, pl.ds(local, local)] = (dkv_ref[at, pl.ds(0, local)] * scale).astype(BF16)
            dqkv_ref[at, pl.ds(2 * local, local)] = dkv_ref[at, pl.ds(local, local)].astype(BF16)
            product = dot_nt(dqkv_ref[at], wqkv_ref[...])
            if send:
                send_ref[i % 2] = product.astype(BF16).reshape(send_ref.shape[1:])
                o_copy(i % 2).start()
            else:
                dkv_ref[at] = product

        def second_block():
            consume(n_mlp, 2 * hb)
            push(n_mlp, 2 * hb)
            vectors(0, 1)
            for move in moves[4:]:
                move.wait()

        @pl.when(side == 0)
        def _():
            run(C_TICKS[0][0])
            dm_from(1).wait_recv()
            task(3, (0, 4 * block), ticks=C_TICKS[0][1])
            second_block()
            finish(3, True)
            dm_from(0).wait_recv()
            task(2, (0, 3 * block), ticks=C_TICKS[0][2])
            finish(2, True)
            task(1, (0, 2 * block), ticks=C_TICKS[0][3])
            finish(1, False)
            task(0, (0, block), ticks=C_TICKS[0][4])
            finish(0, False)

        @pl.when(side == 1)
        def _():
            task(3, (0, 2 * block), "first", ticks=C_TICKS[1][1])
            task(2, (0, 2 * block), "first", ticks=C_TICKS[1][2])
            second_block()
            dm_from(1).wait_recv()
            task(1, (0, 2 * block), ticks=C_TICKS[1][3])
            finish(1, True)
            dm_from(0).wait_recv()
            task(0, (0, block), ticks=C_TICKS[1][4])
            finish(0, True)
            task(3, (2 * block, 4 * block), "last", ticks=C_TICKS[1][5])
            finish(3, False)
            task(2, (2 * block, 3 * block), "last", ticks=C_TICKS[1][6])
            finish(2, False)

        moves[3].wait()
        for part in range(3):
            p = n_mlp + 1 + part
            grad = dot_tn(wout_ref[...].reshape(seq, width), dqkv_ref[:, pl.ds(part * local, local)]).astype(BF16)
            grad_ref[p % 2, :, :, :, pl.ds(0, hb)] = grad.reshape(8, 2, 64, hb)
            produced(p, hb)
            if part == 1:
                consume(p - 1, hb)
                push(p - 1, hb)
        moves[2].wait()

        def din_copy(j):
            return pltpu.make_async_copy(stage_ref, dinr_ref.at[pl.ds(j * block, block)], in_sem.at[j])

        def finish_rows(j):
            at = pl.ds(j * block, block)
            o_copy(j).wait_recv()
            da1 = dkv_ref[pl.ds(pl.multiple_of(own + j * block, block), block)] + xfirst[0, pl.ds(2 * j, 2)].reshape(
                block, width
            ).astype(F32)
            xhat, rstd = norm_parts(x_ref[at].astype(F32))
            grad = din_ref[at] + norm_back(da1, par_ref[pl.ds(GAIN_1, 1)], xhat, rstd)
            if j == 0:
                din_copy(1).wait()
            stage_ref[...] = grad.reshape(block, 8, width // 8)
            din_copy(j).start()
            return total_of(da1 * xhat), total_of(da1)

        lanes = pl.ds(pl.multiple_of(side * local, local), local)
        vsum[1, 0, pl.ds(2, 1), lanes] = total_of(dqkv_ref[:, pl.ds(0, local)].astype(F32))
        vsum[1, 0, pl.ds(3, 1), lanes] = total_of(dqkv_ref[:, pl.ds(2 * local, local)].astype(F32))
        push(DELAYED, 2 * hb)
        consume(n_mlp + 2, hb)
        push(n_mlp + 2, hb)
        run(END_TICKS)
        consume(n_mlp + 3, hb)
        run(MORE_TICKS[0])
        gain_1, shift_1 = finish_rows(1)
        run(MORE_TICKS[1])
        gain_0, shift_0 = finish_rows(0)
        vsum[1, 0, pl.ds(0, 1)] = gain_0 + gain_1
        vsum[1, 0, pl.ds(1, 1)] = shift_0 + shift_1
        vectors(1, 0)
        din_copy(0).wait()

    pl.run_scoped(
        attend,
        vmem((seq, 3 * local), BF16), vmem((seq, local), BF16), vmem((width, 3 * local), BF16), vmem((seq, block), F32),
        vmem((rows, width), BF16), sem((7,)),
    )

    run(TAIL)
    qvg_ref[...] = vec_ref[pl.ds(VEC_ROWS + 2, 2), pl.ds(pl.multiple_of(side * local, local), local)]
    for n in range(2):
        ubg_ref[pl.ds(n, 1)] = vec_ref[pl.ds(4 + side * 2 + n, 1)]
    for q in range(1, half + 1):
        g_sent(q)
    for j in range(2):
        dm_copy(j).wait_send()
        o_copy(j).wait_send()
    for p in range(n_all):
        if all(before(n) != p for n in range(n_all)):
            sent(p)
    for p in range(n_all):
        if p > n_mlp or PLACE[p] is not None:
            for k in (1, 2, 3):
                z_copy(p, k, cols_of(p)).wait_send()
    for n in range(half - nx + 1):
        x_copy(n).wait_send()


def step_call(vectors, ub, qvb, seg, x, g, wqkv, wout, up, down):
    rows, width = x.shape
    local = wout.size // width
    seq = 2 * rows
    block = rows // 2
    hb = HIDDEN_BLOCK
    nx = CROSS_FIRST
    height = width // PIECES
    vm = pl.BlockSpec(memory_space=pltpu.VMEM)
    hbm = pl.BlockSpec(memory_space=pltpu.HBM)
    sem = pltpu.SemaphoreType.DMA
    ny = N_ALL
    places = PLACE[N_MLP] + 3
    nxl = HALF - nx + 1
    shape = jax.ShapeDtypeStruct
    return pl.pallas_call(
        step_kernel,
        out_shape=(
            shape((2, 2, 2, height, width), BF16),
            shape((rows, 8, width // 8), F32),
            shape((height, HALF * hb), F32),
            shape((height, HALF * hb), F32),
            shape((height, local), F32),
            shape((3, height, local), F32),
            shape((2 * VEC_ROWS, width), F32),
            shape((2, local), F32),
            shape((2, width), F32),
            shape((2, 4, 2, height, width), BF16),
            shape((seq, 3 * local), BF16),
            shape((seq, local), BF16),
            shape(up.shape, BF16),
            shape(down.shape, BF16),
        ),
        in_specs=[vm] * 9 + [hbm] * 6,
        out_specs=(hbm,) * 2 + (vm,) * 7 + (hbm,) * 5,
        scratch_shapes=[
            pltpu.VMEM((2, 4, 2, height, width), BF16),
            pltpu.VMEM((rows, local), BF16),
            pltpu.VMEM((local // HEAD_DIM, seq), F32),
            pltpu.VMEM((8, width), F32),
            pltpu.VMEM((8, hb), F32),
            pltpu.VMEM((8, hb), F32),
            pltpu.VMEM((rows, width), F32),
            pltpu.VMEM((block, 8, width // 8), F32),
            pltpu.VMEM((seq, width), F32),
            pltpu.VMEM((seq, local), BF16),
            pltpu.VMEM((2, block, local), BF16),
            pltpu.VMEM((2, 2, 2, height, width), BF16),
            pltpu.VMEM((2, block, local), F32),
            pltpu.VMEM((2, 8, 2, height, 2 * hb), BF16),
            pltpu.VMEM((2, 8, height, 2 * hb), BF16),
            pltpu.VMEM((S_SLOTS, 4, 2, height, 2 * hb), BF16),
            pltpu.VMEM((places, 4, height, 2 * hb), BF16),
            pltpu.VMEM((places, 3, height, 2 * hb), BF16),
            pltpu.VMEM((3, 2, height, 2 * hb), BF16),
            pltpu.VMEM((3, height, 2 * hb), BF16),
            pltpu.VMEM((nx, 4, 2, height, 2 * hb), BF16),
            pltpu.VMEM((nxl, height, 2 * hb), BF16),
            pltpu.VMEM((nxl, height, 2 * hb), BF16),
            pltpu.VMEM((2, 4, VEC_ROWS, width), F32),
            pltpu.VMEM((2, 7, VEC_ROWS, width), F32),
            sem((4,)), sem((4,)), sem((2,)), sem((2,)), sem, sem, sem((8,)),
            sem((2,)), sem((2,)), sem((ny,)), sem((ny,)), sem((ny, 3)), sem((ny, 3)),
            sem((nx,)), sem((nx,)), sem((nxl,)), sem((nxl,)), sem((2, 7)), sem((2, 7)),
            sem((2,)), sem((2,)), sem((2,)), sem((2,)), sem((2,)), pltpu.SemaphoreType.REGULAR,
            *gather_semaphores(1 + HALF),
        ],
        compiler_params=pltpu.CompilerParams(
            collective_id=0, has_side_effects=True, vmem_limit_bytes=VMEM_LIMIT
        ),
        name="train_step",
    )(*vectors, ub, qvb, seg, x, g, wqkv, wout, up, down)


def settle_kernel(*refs):
    sources, results, scratch, sems = refs[:9], refs[9:23], refs[23:29], refs[29]
    reads = [pltpu.make_async_copy(s, v, sems.at[0, n]) for n, (s, v) in enumerate(zip(sources[:6], scratch))]
    writes = [pltpu.make_async_copy(v, r, sems.at[1, n]) for n, (v, r) in enumerate(zip(scratch, results[:6]))]
    for copy in reads:
        copy.start()
    vec_ref, qv_ref, ub_ref = sources[6:]
    width = vec_ref.shape[1]
    for n, row in enumerate((VEC_ROWS, VEC_ROWS + 1, 2, 0, 1, 3)):
        results[6 + n][...] = vec_ref[pl.ds(row, 1)].reshape(width)
    results[12][...] = qv_ref[...]
    for n in range(2):
        results[13][pl.ds(n * width, width)] = ub_ref[pl.ds(n, 1)].reshape(width)
    for read, write in zip(reads, writes):
        read.wait()
        write.start()
    for copy in writes:
        copy.wait()


def settle_call(*arrays):
    vm = pl.BlockSpec(memory_space=pltpu.VMEM)
    hbm = pl.BlockSpec(memory_space=pltpu.HBM)
    width = arrays[6].shape[1]
    shapes = [a.shape for a in arrays[:6]] + [(width,)] * 6 + [arrays[7].shape, (2 * width,)]
    dtypes = [a.dtype for a in arrays[:6]] + [F32] * 8
    return pl.pallas_call(
        settle_kernel,
        out_shape=[jax.ShapeDtypeStruct(s, d) for s, d in zip(shapes, dtypes)],
        in_specs=[hbm] * 6 + [vm] * 3,
        out_specs=[hbm] * 6 + [vm] * 8,
        scratch_shapes=[*(pltpu.VMEM(a.shape, a.dtype) for a in arrays[:6]), pltpu.SemaphoreType.DMA((2, 6))],
        compiler_params=pltpu.CompilerParams(vmem_limit_bytes=VMEM_LIMIT),
        name="settle",
    )(*arrays)


def on_device_pair(
    inputs, segment_ids, first_gain, first_shift, qkv_weight, qv_bias, out_weight, out_bias,
    second_gain, second_shift, up_weight, up_bias, down_weight, down_bias, cotangent,
):
    rows, _, width = inputs.shape
    seq = segment_ids.shape[0]
    local = out_weight.shape[0]
    x = inputs.reshape(rows, width)
    g = cotangent.reshape(rows, width)
    seg = segment_ids.reshape(1, seq)
    height = width // PIECES
    wout = out_weight.reshape(4, 2, height, width)
    vectors = (first_gain, first_shift, out_bias, second_gain, second_shift, down_bias)
    wqkv = jnp.transpose(qkv_weight, (1, 0, 2))
    layer_output, input_grad, up_g, down_g, out_g, qkv_g, first_gain_g, first_shift_g, out_bias_g, second_gain_g, \
        second_shift_g, down_bias_g, qv_g, up_bias_g = settle_call(
            *step_call(vectors, up_bias, qv_bias, seg, x, g, wqkv, wout, up_weight, down_weight)[:9]
        )
    return (
        layer_output.reshape(rows, 1, width),
        input_grad.reshape(rows, 1, width),
        first_gain_g,
        first_shift_g,
        jnp.transpose(qkv_g, (1, 0, 2)),
        qv_g,
        out_g.T,
        out_bias_g,
        second_gain_g,
        second_shift_g,
        up_g,
        up_bias_g,
        down_g.T,
        down_bias_g,
    )


def solution(mesh):
    in_specs = (
        P("tensor", "dp", None),
        P(None, "dp"),
        P(),
        P(),
        P(None, None, "tensor"),
        P(None, "tensor"),
        P("tensor", None),
        P(),
        P(),
        P(),
        P(None, "tensor"),
        P("tensor"),
        P("tensor", None),
        P(),
        P("tensor", "dp", None),
    )
    out_specs = (
        P("tensor", "dp", None),
        P("tensor", "dp", None),
        P(),
        P(),
        P("dp", None, "tensor"),
        P(None, "tensor"),
        P("tensor", "dp"),
        P(),
        P(),
        P(),
        P("dp", "tensor"),
        P("tensor"),
        P("tensor", "dp"),
        P(),
    )
    pair = mesh.shape["tensor"] == 2 and mesh.shape["dp"] == Z_SIZE * Y_SIZE * CORES
    return jax.shard_map(
        on_device_pair if pair else on_device, mesh=mesh, in_specs=in_specs, out_specs=out_specs, check_vma=False
    )
```

```python
import functools

import jax
import jax.numpy as jnp
from jax import lax
from jax.experimental import pallas as pl
from jax.experimental.pallas import tpu as pltpu
from jax.sharding import PartitionSpec as P

HEAD_DIM = 64
MESH = pl.DeviceIdType.MESH
F32 = jnp.float32
BF16 = jnp.bfloat16
VMEM_LIMIT = 63 << 20


norm_eps = 1e-05


def layer_norm(value, gain, shift):
    row_mean = jnp.mean(value, axis=-1, keepdims=True)
    centred = value - row_mean
    variance = jnp.mean(centred * centred, axis=-1, keepdims=True)
    return centred * lax.rsqrt(variance + norm_eps) * gain + shift


def gelu_tanh(value):
    return (
        0.5
        * value
        * (1.0 + jnp.tanh(0.7978845608028654 * (value + 0.044715 * value * value * value)))
    )


def masked_scores(query_block, keys_all, seg_block, seg_all, row_start, block_rows, score_scale):
    scores = (
        jnp.einsum("qhd,khd->hqk", query_block, keys_all, preferred_element_type=jnp.float32)
        * score_scale
    )
    key_pos = jnp.arange(keys_all.shape[0], dtype=jnp.int32)
    query_pos = row_start + jnp.arange(block_rows, dtype=jnp.int32)
    allowed = (seg_block[:, None] == seg_all[None, :]) & (query_pos[:, None] >= key_pos[None, :])
    return jnp.where(allowed[None], scores, -1e30)


def attend_forward(queries, keys_all, values_all, seg_all, score_scale):
    seq_len = queries.shape[0]
    block_rows = min(512, seq_len)

    def one_block(block_index):
        row_start = block_index * block_rows
        query_block = lax.dynamic_slice_in_dim(queries, row_start, block_rows, 0)
        seg_block = lax.dynamic_slice_in_dim(seg_all, row_start, block_rows, 0)
        scores = masked_scores(
            query_block, keys_all, seg_block, seg_all, row_start, block_rows, score_scale
        )
        row_top = jnp.max(scores, axis=-1, keepdims=True)
        weights = jnp.exp(scores - row_top)
        row_total = jnp.sum(weights, axis=-1, keepdims=True)
        probs_low = (weights / row_total).astype(jnp.bfloat16)
        mixed = jnp.einsum(
            "hqk,khd->qhd", probs_low, values_all, preferred_element_type=jnp.float32
        )
        return (mixed, row_top + jnp.log(row_total))

    mixed, log_total = lax.map(one_block, jnp.arange(seq_len // block_rows, dtype=jnp.int32))
    return (mixed.reshape(seq_len, -1), log_total)


def attend_backward(queries, keys_all, values_all, seg_all, log_total, out_grad, score_scale):
    seq_len = queries.shape[0]
    block_rows = min(512, seq_len)

    def one_block(carry, block_index):
        key_grad, value_grad = carry
        row_start = block_index * block_rows
        query_block = lax.dynamic_slice_in_dim(queries, row_start, block_rows, 0)
        seg_block = lax.dynamic_slice_in_dim(seg_all, row_start, block_rows, 0)
        grad_block = lax.dynamic_slice_in_dim(out_grad, row_start, block_rows, 0)
        scores = masked_scores(
            query_block, keys_all, seg_block, seg_all, row_start, block_rows, score_scale
        )
        probs = jnp.exp(scores - log_total[block_index])
        probs_low = probs.astype(jnp.bfloat16)
        value_grad = value_grad + jnp.einsum(
            "hqk,qhd->khd", probs_low, grad_block, preferred_element_type=jnp.float32
        )
        prob_grad = jnp.einsum(
            "qhd,khd->hqk", grad_block, values_all, preferred_element_type=jnp.float32
        )
        row_dot = jnp.sum(probs * prob_grad, axis=-1, keepdims=True)
        score_grad = (probs * (prob_grad - row_dot)).astype(jnp.bfloat16)
        query_grad = (
            jnp.einsum("hqk,khd->qhd", score_grad, keys_all, preferred_element_type=jnp.float32)
            * score_scale
        )
        key_grad = (
            key_grad
            + jnp.einsum(
                "hqk,qhd->khd", score_grad, query_block, preferred_element_type=jnp.float32
            )
            * score_scale
        )
        return ((key_grad, value_grad), query_grad)

    zero_grads = jnp.zeros(keys_all.shape, jnp.float32)
    (key_grad, value_grad), query_grad = lax.scan(
        one_block, (zero_grads, zero_grads), jnp.arange(seq_len // block_rows, dtype=jnp.int32)
    )
    return (
        query_grad.reshape(seq_len, -1),
        key_grad.reshape(seq_len, -1),
        value_grad.reshape(seq_len, -1),
    )


def row_product(left, right, contract):
    return lax.dot_general(
        left, right, (((1,), (contract,)), ((), ())), preferred_element_type=jnp.float32
    )


def rows_contract(left, right):
    return lax.dot_general(
        left, right, (((0,), (0,)), ((), ())), preferred_element_type=jnp.float32
    )


def on_device(
    inputs,
    segment_ids,
    first_gain,
    first_shift,
    qkv_weight,
    qv_bias,
    out_weight,
    out_bias,
    second_gain,
    second_shift,
    up_weight,
    up_bias,
    down_weight,
    down_bias,
    cotangent,
):
    rows_dev, seq_count, model_width = inputs.shape
    tensor_count = lax.axis_size("tensor")
    tensor_rank = lax.axis_index("tensor")
    seq_len = rows_dev * tensor_count
    local_width = out_weight.shape[0]
    heads_dev = local_width // HEAD_DIM
    hidden_dev = up_weight.shape[1]
    local_rows = rows_dev * seq_count
    score_scale = HEAD_DIM ** (-0.5)
    residual_in = inputs.reshape(local_rows, model_width).astype(jnp.float32)
    gain_one = first_gain.astype(jnp.float32)
    shift_one = first_shift.astype(jnp.float32)
    gain_two = second_gain.astype(jnp.float32)
    shift_two = second_shift.astype(jnp.float32)
    normed_one, pull_one = jax.vjp(layer_norm, residual_in, gain_one, shift_one)
    first_local = normed_one.astype(jnp.bfloat16)
    first_rows = lax.all_gather(first_local, "tensor", axis=0, tiled=True)
    qkv_flat = qkv_weight.reshape(model_width, 3 * local_width)
    qkv_bias = jnp.concatenate(
        [
            qv_bias[0].astype(jnp.float32),
            jnp.zeros((local_width,), jnp.float32),
            qv_bias[1].astype(jnp.float32),
        ]
    )
    qkv_low = (jnp.dot(first_rows, qkv_flat, preferred_element_type=jnp.float32) + qkv_bias).astype(
        jnp.bfloat16
    )
    qkv_split = qkv_low.reshape(seq_len, seq_count, 3, heads_dev, HEAD_DIM)
    seq_index = 0
    mixed_one, log_one = attend_forward(
        qkv_split[:, seq_index, 0],
        qkv_split[:, seq_index, 1],
        qkv_split[:, seq_index, 2],
        segment_ids[:, seq_index],
        score_scale,
    )
    mixed_list = [mixed_one]
    log_list = [log_one]
    mixed_low = (
        jnp.stack(mixed_list, axis=1).reshape(seq_len * seq_count, local_width).astype(jnp.bfloat16)
    )
    attn_local = lax.psum_scatter(
        row_product(mixed_low, out_weight, 0), "tensor", scatter_dimension=0, tiled=True
    )
    residual_mid = residual_in + attn_local + out_bias.astype(jnp.float32)
    normed_two, pull_two = jax.vjp(layer_norm, residual_mid, gain_two, shift_two)
    second_local = normed_two.astype(jnp.bfloat16)
    second_rows = lax.all_gather(second_local, "tensor", axis=0, tiled=True)
    hidden_pre = jnp.dot(
        second_rows, up_weight, preferred_element_type=jnp.float32
    ) + up_bias.astype(jnp.float32)
    activated, pull_gelu = jax.vjp(gelu_tanh, hidden_pre)
    hidden_low = activated.astype(jnp.bfloat16)
    mlp_local = lax.psum_scatter(
        row_product(hidden_low, down_weight, 0).astype(jnp.bfloat16),
        "tensor",
        scatter_dimension=0,
        tiled=True,
    ).astype(jnp.float32)
    layer_output = (residual_mid + mlp_local + down_bias.astype(jnp.float32)).astype(jnp.bfloat16)
    layer_output = layer_output.reshape(rows_dev, seq_count, model_width)
    grad_local = cotangent.reshape(local_rows, model_width)
    grad_rows = lax.all_gather(grad_local, "tensor", axis=0, tiled=True)
    down_grad = rows_contract(hidden_low, grad_rows)
    hidden_grad = lax.dot_general(
        grad_rows, down_weight, (((1,), (1,)), ((), ())), preferred_element_type=jnp.float32
    )
    (pre_grad,) = pull_gelu(hidden_grad)
    pre_low = pre_grad.astype(jnp.bfloat16)
    up_sums = jnp.sum(pre_low, axis=0, dtype=jnp.float32)
    second_back = lax.all_gather(second_local, "tensor", axis=0, tiled=True)
    up_grad = rows_contract(second_back, pre_low)
    second_norm_grad = lax.psum_scatter(
        row_product(pre_low, up_weight, 1), "tensor", scatter_dimension=0, tiled=True
    )
    mid_from_norm, gain_two_grad, shift_two_grad = pull_two(second_norm_grad)
    residual_grad = grad_local.astype(jnp.float32) + mid_from_norm
    residual_low = residual_grad.astype(jnp.bfloat16)
    residual_rows = lax.all_gather(residual_low, "tensor", axis=0, tiled=True)
    out_grad_weight = rows_contract(mixed_low, residual_rows)
    mixed_grad = lax.dot_general(
        residual_rows, out_weight, (((1,), (1,)), ((), ())), preferred_element_type=jnp.float32
    ).astype(jnp.bfloat16)
    mixed_grad = mixed_grad.reshape(seq_len, seq_count, heads_dev, HEAD_DIM)
    seq_index = 0
    query_grad, key_grad, value_grad = attend_backward(
        qkv_split[:, seq_index, 0],
        qkv_split[:, seq_index, 1],
        qkv_split[:, seq_index, 2],
        segment_ids[:, seq_index],
        log_list[seq_index],
        mixed_grad[:, seq_index],
        score_scale,
    )
    query_list = [query_grad]
    key_list = [key_grad]
    value_list = [value_grad]
    qkv_grad = jnp.concatenate(
        [jnp.stack(query_list, axis=1), jnp.stack(key_list, axis=1), jnp.stack(value_list, axis=1)],
        axis=-1,
    )
    qkv_grad_low = qkv_grad.reshape(seq_len * seq_count, 3 * local_width).astype(jnp.bfloat16)
    qkv_sums = jnp.sum(qkv_grad_low, axis=0, dtype=jnp.float32)
    qv_sums = jnp.stack([qkv_sums[:local_width], qkv_sums[2 * local_width :]], axis=0)
    first_back = lax.all_gather(first_local, "tensor", axis=0, tiled=True)
    qkv_grad_weight = rows_contract(first_back, qkv_grad_low).reshape(model_width, 3, local_width)
    first_norm_grad = lax.psum_scatter(
        row_product(qkv_grad_low, qkv_flat, 1), "tensor", scatter_dimension=0, tiled=True
    )
    in_from_norm, gain_one_grad, shift_one_grad = pull_one(first_norm_grad)
    input_grad = (residual_grad + in_from_norm).reshape(rows_dev, seq_count, model_width)
    qkv_share, out_share, up_share, down_share = (
        lax.psum_scatter(qkv_grad_weight, "dp", scatter_dimension=0, tiled=True),
        lax.psum_scatter(out_grad_weight, "dp", scatter_dimension=1, tiled=True),
        lax.psum_scatter(up_grad, "dp", scatter_dimension=0, tiled=True),
        lax.psum_scatter(down_grad, "dp", scatter_dimension=1, tiled=True),
    )
    out_bias_part = jnp.sum(residual_low, axis=0, dtype=jnp.float32)
    down_bias_part = jnp.sum(grad_local, axis=0, dtype=jnp.float32)
    stacked = jnp.stack(
        [
            gain_one_grad,
            shift_one_grad,
            gain_two_grad,
            shift_two_grad,
            out_bias_part,
            down_bias_part,
        ],
        axis=0,
    )
    qv_full = lax.dynamic_update_slice(
        jnp.zeros((2, model_width), jnp.float32), qv_sums, (jnp.int32(0), tensor_rank * local_width)
    )
    up_full = lax.dynamic_update_slice(
        jnp.zeros((hidden_dev * tensor_count,), jnp.float32), up_sums, (tensor_rank * hidden_dev,)
    )
    stacked, qv_total, up_total = lax.psum((stacked, qv_full, up_full), ("dp", "tensor"))
    qv_share = lax.dynamic_slice_in_dim(qv_total, tensor_rank * local_width, local_width, 1)
    up_bias_share = lax.dynamic_slice_in_dim(up_total, tensor_rank * hidden_dev, hidden_dev, 0)
    return (
        layer_output,
        input_grad,
        stacked[0],
        stacked[1],
        qkv_share,
        qv_share,
        out_share,
        stacked[4],
        stacked[2],
        stacked[3],
        up_share,
        up_bias_share,
        down_share,
        stacked[5],
    )


Z_SIZE, Y_SIZE, CORES = 4, 2, 2


def place():
    dp = lax.axis_index("dp")
    side = lax.axis_index("tensor")
    return dp // 4, (dp // 2) % 2, dp % 2, side


def dev(z, y, core, side):
    return (z * 4 + y * 2 + core, side)


def peer_x():
    z, y, core, side = place()
    return dev(z, y, core, 1 - side)


def peer_y():
    z, y, core, side = place()
    return dev(z, 1 - y, core, side)


def peer_core():
    z, y, core, side = place()
    return dev(z, y, 1 - core, side)


def peer_z(step):
    z, y, core, side = place()
    return dev((z + step) % 4, y, core, side)


def greet():
    peers = [peer_x(), peer_y(), peer_core()] + [peer_z(k) for k in (1, 2, 3)]
    barrier = pltpu.get_barrier_semaphore()
    for peer in peers:
        pl.semaphore_signal(barrier, inc=1, device_id=peer, device_id_type=MESH)
    return lambda: pl.semaphore_wait(barrier, len(peers))


def remote(src, dst, send_sem, recv_sem, peer):
    return pltpu.make_async_remote_copy(
        src_ref=src, dst_ref=dst, send_sem=send_sem, recv_sem=recv_sem, device_id=peer, device_id_type=MESH
    )


def dot_nn(a, b):
    return lax.dot_general(a, b, (((1,), (0,)), ((), ())), preferred_element_type=F32)


def dot_nt(a, b):
    return lax.dot_general(a, b, (((1,), (1,)), ((), ())), preferred_element_type=F32)


def dot_tn(a, b):
    return lax.dot_general(a, b, (((0,), (0,)), ((), ())), preferred_element_type=F32)


def norm_parts(value):
    mean = jnp.mean(value, axis=-1, keepdims=True)
    centred = value - mean
    rstd = lax.rsqrt(jnp.mean(centred * centred, axis=-1, keepdims=True) + norm_eps)
    return centred * rstd, rstd


def norm_back(grad, gain, xhat, rstd):
    e = grad * gain
    return rstd * (e - jnp.mean(e, axis=-1, keepdims=True) - xhat * jnp.mean(e * xhat, axis=-1, keepdims=True))


def head_lanes(h):
    lane = lax.broadcasted_iota(jnp.int32, (1, 2 * HEAD_DIM), 1)
    return (lane // HEAD_DIM) == h


def only_head(value, h):
    return jnp.where(head_lanes(h), value, jnp.zeros_like(value))


def total_of(row):
    return jnp.sum(row, axis=0, keepdims=True)


GAIN_1, SHIFT_1, OUT_BIAS, GAIN_2, SHIFT_2, DOWN_BIAS = range(6)
PIECES = 16
HIDDEN_BLOCK = 512


def gather(source, target, sems):
    x_s, x_r, z_s, z_r, y_s, y_r, c_s, c_r = sems
    z, y, core, side = place()

    def copies(dp, q, send, recv, peer, views=target):
        pairs = zip(views(dp, q), target(dp, q))
        return [remote(s, d, send.at[a], recv.at[a], peer) for a, (s, d) in enumerate(pairs)]

    def number(zz, yy, cc):
        return zz * 4 + yy * 2 + cc

    def from_z(k):
        return (z + 4 - k) % 4

    def x_copies(q):
        return copies(number(z, y, core), q, x_s.at[q], x_r.at[q], peer_x(), source)

    def z_sends(q, k):
        return copies(number(z, y, core), q, z_s.at[q, k], z_r.at[q, k], peer_z(k))

    def z_recvs(q, k):
        return copies(number(from_z(k), y, core), q, z_s.at[q, k], z_r.at[q, k], peer_z(k))

    def y_copies(q, k, yy):
        return copies(number(from_z(k), yy, core), q, y_s.at[q, k], y_r.at[q, k], peer_y())

    def c_copies(q, k, far, cc):
        yy = (1 - y) if far else y
        slot = 4 * far + k
        return copies(number(from_z(k), yy, cc), q, c_s.at[q, slot], c_r.at[q, slot], peer_core())

    def start(list_of):
        for copy in list_of:
            copy.start()

    def first(q):
        for copy in x_copies(q):
            copy.wait()
        for k in (2, 1, 3):
            start(z_sends(q, k))
        start(y_copies(q, 0, y))
        start(c_copies(q, 0, 0, core))

    def second(q):
        for k in (1, 3, 2):
            for copy in z_recvs(q, k):
                copy.wait_recv()
            start(y_copies(q, k, y))
            start(c_copies(q, k, 0, core))

    def third(q):
        for k in range(4):
            for copy in y_copies(q, k, 1 - y):
                copy.wait_recv()
            start(c_copies(q, k, 1, core))

    def last(q):
        for k in range(4):
            for far in (0, 1):
                for copy in c_copies(q, k, far, 1 - core):
                    copy.wait_recv()

    def sent(q):
        for k in range(4):
            if k > 0:
                for copy in z_sends(q, k):
                    copy.wait_send()
            for copy in y_copies(q, k, y):
                copy.wait_send()
            for far in (0, 1):
                for copy in c_copies(q, k, far, core):
                    copy.wait_send()

    return first, second, third, last, sent, x_copies


def gather_semaphores(q):
    sem = pltpu.SemaphoreType.DMA
    return [sem((q, 2))] * 2 + [sem((q, 4, 2))] * 4 + [sem((q, 8, 2))] * 2


def hidden_views(arrays, dp, b):
    up, down = arrays
    n_up, n_down = up.shape[0] // PIECES, HIDDEN_BLOCK // PIECES
    return [
        up.at[pl.ds(pl.multiple_of(dp * n_up, n_up), n_up), pl.ds(b * HIDDEN_BLOCK, HIDDEN_BLOCK)],
        down.at[pl.ds(pl.multiple_of(b * HIDDEN_BLOCK + dp * n_down, n_down), n_down)],
    ]


CROSS_FIRST = 2
ORDER = (("o", 2), ("t", 0), ("o", 3), ("t", 1), ("t", 2), ("o", 1), ("o", 0), ("t", 3))
SLOT = (0, 1, 2, 3, 4, 5, 0, 1, 2, 4, 0, 1)
S_SLOTS = 6
CROSSING = (1, 3)
DELAYED = 5
PLACE = (None, None, 0, None, 1, 2, 3, 4, 5)
HALF = len(ORDER) // 2
N_MLP = 2 * HALF
N_ALL = N_MLP + 4
VEC_ROWS = 8
A_TICKS = {
    "start": [("g_first", 0)],
    "block": [("g_second", 0)],
    "early": [("g_first", 1), ("g_third", 0)],
    "middle": [("g_first", 2), ("g_second", 1)],
    "late": [("g_first", 3), ("g_third", 1), ("g_second", 2)],
    "end": [("g_third", 2)],
}
B_START = [("g_first", 4), ("g_second", 3)]
B_TICKS = {
    1: [("g_third", 3)], 2: [("g_second", 4)], 4: [("g_third", 4)], 7: [("z_second", 0), ("second", 2)],
}
C_TICKS = {
    0: ([("second", 4)], [(3, [("second", 6)])], [], [], [(3, [("second", 7)])]),
    1: ([], [(2, [("second", 4)])], [], [(3, [("second", 6)])], [], [], [(3, [("second", 7)])]),
}
END_TICKS = []
MORE_TICKS = (
    [("z_third", 0), ("third", 2), ("third", 4), ("third", 6), ("second", 8), ("third", 7)], [("vec", (0, 2)), ("second", 9)],
)
TAIL = [
    ("third", 8), ("vec", (1, 1)), ("push", 11), ("vec", (0, 3)), ("second", 5), ("third", 9), ("second", 10),
    ("vec", (1, 2)), ("third", 5), ("second", 11), ("vec", (1, 3)), ("third", 10), ("third", 11), ("fourth", 0),
    ("fourth", 1), ("fourth", 2), ("vec", (0, 4)), ("vec", (1, 4)),
]


def lookup(table, p):
    if isinstance(p, int):
        return table[p]
    value = jnp.int32(table[0])
    for n in range(1, len(table)):
        value = jnp.where(p == n, jnp.int32(table[n]), value)
    return value


def before(p):
    return max((n for n in range(p) if SLOT[n] == SLOT[p]), default=None)


def hidden_of(p):
    return lookup([b for _, b in ORDER], p)


def is_other(p):
    if isinstance(p, int):
        return ORDER[p][0] == "t"
    return lookup([int(s == "t") for s, _ in ORDER], p) == 1


def step_kernel(
    g1_ref, s1_ref, ob_ref, g2_ref, s2_ref, db_ref, ub_ref, qvb_ref, seg_ref,
    x_hbm, g_hbm, wqkv_hbm, wout_hbm, up_own, down_own,
    out_ref, dinr_ref, upg_ref, downg_ref, og_ref, qkvg_ref, vec_ref, qvg_ref, ubg_ref,
    a1_hbm, qkv_hbm, mix_hbm, up_oth, down_oth,
    wout_ref, mixt_ref, lse_ref, par_ref, ubo_ref, ubt_ref, din_ref, stage_ref,
    dkv_ref, dm_ref, dsend_ref, send_ref, dq_ref, grad_ref, core_ref, sum_ref, ybuf, zbuf, zf_buf, yf_buf, xfirst, xsend, xbuf,
    vsum, vrecv,
    a_s, a_r, m_s, m_r, b_s, b_r, l_sem,
    c_s, c_r, y_s, y_r, z_s, z_r, xf_s, xf_r, x_s, x_r, v_s, v_r, dm_s, dm_r, o_s, o_r, out_sem, free_sem, *gather_sems,
):
    rows, width = din_ref.shape
    seq = 2 * rows
    local = dm_ref.shape[1]
    block = rows // 2
    piece = rows // 4
    hb = HIDDEN_BLOCK
    nx = CROSS_FIRST
    half, n_mlp, n_all = HALF, N_MLP, N_ALL
    z, y, core, side = place()
    partner = peer_x()
    own = pl.multiple_of(side * rows, rows)
    theirs = pl.multiple_of((1 - side) * rows, rows)
    scale = HEAD_DIM**-0.5
    vmem = pltpu.VMEM
    sem = pltpu.SemaphoreType.DMA

    def out_views(ref, dp):
        return [ref.at[dp // 4, dp // 2 % 2, pl.ds(dp % 2 * 32, 32)]]

    def gather_source(dp, q):
        return out_views(wout_hbm, dp) if q == 0 else hidden_views((up_own, down_own), dp, q - 1)

    def gather_target(dp, q):
        return out_views(wout_ref.at[1], dp) if q == 0 else hidden_views((up_oth, down_oth), dp, q - 1)

    g_first, g_second, g_third, g_last, g_sent, g_x = gather(gather_source, gather_target, gather_sems)

    def g_start(q):
        for copy in g_x(q):
            copy.start()

    def cols_of(p):
        return 2 * hb if p <= n_mlp else hb

    def slot_of(p):
        return lookup(SLOT, p)

    def core_copy(p, cols):
        slot = p % 2
        lanes = pl.ds(0, cols)
        return remote(
            grad_ref.at[slot, :, 1 - core, :, lanes], core_ref.at[slot, :, :, lanes], c_s.at[slot], c_r.at[slot],
            peer_core(),
        )

    def place_of(p, cols):
        if isinstance(p, int) and p > n_mlp:
            n = p - n_mlp - 1
            return PLACE[n_mlp] + 1 + n // 2, pl.ds(n % 2 * hb, hb)
        return lookup([n or 0 for n in PLACE], p), pl.ds(0, cols)

    def y_copy(p, cols):
        s, lanes = place_of(p, cols)
        src = sum_ref.at[slot_of(p), :, 1 - y, :, pl.ds(0, cols)]
        return remote(src, ybuf.at[s, :, :, lanes], y_s.at[p], y_r.at[p], peer_y())

    def z_copy(p, k, cols):
        s, lanes = place_of(p, cols)
        src, dst = ybuf.at[s, (z + k) % 4, :, lanes], zbuf.at[s, k - 1, :, lanes]
        return remote(src, dst, z_s.at[p, k - 1], z_r.at[p, k - 1], peer_z(k))

    def zf_copy(k):
        return remote(sum_ref.at[SLOT[0], (z + k) % 4], zf_buf.at[k - 1], z_s.at[0, k - 1], z_r.at[0, k - 1], peer_z(k))

    def yf_copy():
        return remote(yf_buf.at[1 - y], yf_buf.at[2], y_s.at[0], y_r.at[0], peer_y())

    def z_second(p):
        for k in (1, 2, 3):
            zf_copy(k).wait_recv()
        total = sum_ref[SLOT[0], z].astype(F32)
        for k in (1, 2, 3):
            total = total + zf_buf[k - 1].astype(F32)
        yf_buf[pl.ds(0, 2)] = total.astype(BF16)
        yf_copy().start()

    def z_third(p):
        yf_copy().wait()
        mlp_write(hidden_of(p), yf_buf[y].astype(F32) + yf_buf[2].astype(F32))

    def xfirst_copy(n):
        return remote(sum_ref.at[SLOT[CROSSING[n]]], xfirst.at[n], xf_s.at[n], xf_r.at[n], partner)

    def x_copy(n):
        lanes = pl.ds(0, 2 * hb if n < half - nx else hb)
        return remote(xsend.at[n, :, lanes], xbuf.at[n, :, lanes], x_s.at[n], x_r.at[n], partner)

    def produced(p, cols):
        @pl.when(p >= 2)
        def _():
            pl.semaphore_wait(free_sem, 1)

        core_copy(p, cols).start()

    def consume(p, cols):
        slot = p % 2
        lanes = pl.ds(0, cols)
        copy = core_copy(p, cols)
        copy.wait()
        for n in range(n_all) if not isinstance(p, int) else (p,):
            if before(n) is not None and n < n_mlp - 1 and not isinstance(p, int):

                @pl.when(p == n)
                def _():
                    sent(before(n))

            elif before(n) is not None and isinstance(p, int):
                sent(before(n))
        total = grad_ref[slot, :, core, :, lanes] + core_ref[slot, :, :, lanes]
        at = sum_ref.at[slot_of(p), :, :, :, lanes]
        at[...] = total.reshape(4, 2, 64, cols)

        @pl.when(p < n_all - 2)
        def _():
            pl.semaphore_signal(free_sem, inc=1, device_id=peer_core(), device_id_type=MESH)

    def sent(p):
        if p == 0:
            for k in (1, 2, 3):
                zf_copy(k).wait_send()
        elif p in CROSSING:
            xfirst_copy(CROSSING.index(p)).wait_send()
        else:
            y_copy(p, cols_of(p)).wait_send()

    def push_one(p, cols):
        if p == 0:
            for k in (2, 1, 3):
                zf_copy(k).start()
        elif p in CROSSING:
            xfirst_copy(CROSSING.index(p)).start()
        else:
            if p < n_mlp and not is_other(p) and hidden_of(p) < nx:
                add_first(p)
            y_copy(p, cols).start()

    def push(p, cols):
        if isinstance(p, int):
            push_one(p, cols)
            return
        for n in range(n_mlp - 1):
            if n not in (DELAYED, CROSSING[1]):

                @pl.when(p == n)
                def _():
                    push_one(n, cols)

    def add_first(p):
        b = hidden_of(p)
        xfirst_copy(b).wait_recv()
        sum_ref[slot_of(p)] = sum_ref[slot_of(p)] + xfirst[b]

    def second(p):
        cols = cols_of(p)
        s, lanes = place_of(p, cols)
        y_copy(p, cols).wait_recv()
        ybuf[s, :, :, lanes] = sum_ref[slot_of(p), :, y, :, pl.ds(0, cols)] + ybuf[s, :, :, lanes]
        for k in (2, 1, 3):
            z_copy(p, k, cols).start()

    def mlp_write(b, total, more=False):
        cols = pl.ds(b * hb, hb)
        for ref, part in ((upg_ref, total[:, :hb]), (downg_ref, total[:, hb:])):
            ref[:, cols] = ref[:, cols] + part if more else part

    def third(p):
        cols = cols_of(p)
        s, lanes = place_of(p, cols)
        for k in (1, 2, 3):
            z_copy(p, k, cols).wait_recv()
        total = ybuf[s, z, :, lanes].astype(F32)
        for k in (1, 2, 3):
            total = total + zbuf[s, k - 1, :, lanes].astype(F32)
        if p < n_mlp and is_other(p):
            n = hidden_of(p) - nx
            xsend[n] = total.astype(BF16)
            x_copy(n).start()
        elif p < n_mlp:
            mlp_write(hidden_of(p), total)
        elif p == n_mlp:
            og_ref[...] = total[:, :hb]
            xsend[half - nx, :, pl.ds(0, hb)] = total[:, hb:].astype(BF16)
            x_copy(half - nx).start()
        else:
            qkvg_ref[p - n_mlp - 1] = total

    def fourth(n):
        x_copy(n).wait_recv()
        if n < half - nx:
            mlp_write(n + nx, xbuf[n].astype(F32), more=True)
        else:
            og_ref[...] += xbuf[n, :, pl.ds(0, hb)].astype(F32)

    def v_copy(w, n, peer, slot):
        return remote(vsum.at[w, n], vrecv.at[w, slot], v_s.at[w, slot], v_r.at[w, slot], peer)

    def z_vec(w, k, source):
        return remote(vsum.at[w, 2], vrecv.at[w, 2 + source], v_s.at[w, 2 + k], v_r.at[w, 2 + source], peer_z(k))

    def vectors(w, n):
        if n == 0:
            v_copy(w, 0, peer_core(), 0).start()
        elif n == 1:
            v_copy(w, 0, peer_core(), 0).wait()
            vsum[w, 1] = vsum[w, 0] + vrecv[w, 0]
            v_copy(w, 1, peer_y(), 1).start()
        elif n == 2:
            v_copy(w, 1, peer_y(), 1).wait()
            vsum[w, 2] = vsum[w, 1] + vrecv[w, 1]
            for k in (1, 2, 3):
                z_vec(w, k, z).start()
        elif n == 3:
            for k in (1, 2, 3):
                z_vec(w, k, z).wait_send()
                z_vec(w, k, (z + k) % 4).wait_recv()
            vrecv[w, 2 + z] = vsum[w, 2]
            vsum[w, 3] = (vrecv[w, 2] + vrecv[w, 3]) + (vrecv[w, 4] + vrecv[w, 5])
            v_copy(w, 3, partner, 6).start()
        elif n == 4:
            v_copy(w, 3, partner, 6).wait()
            vec_ref[pl.ds(w * VEC_ROWS, VEC_ROWS)] = vsum[w, 3] + vrecv[w, 6]

    stages = dict(
        second=second, third=third, fourth=fourth, z_second=z_second, z_third=z_third,
        push=lambda p: push(p, cols_of(p)), g_first=g_first, g_second=g_second, g_third=g_third, g_last=g_last
    )

    def run(names):
        for name, arg in names:
            if name == "vec":
                vectors(*arg)
            else:
                stages[name](arg)

    dm_own = dm_ref.at[pl.ds(own, rows)]

    def dm_copy(b):
        at = pl.ds(pl.multiple_of(own + b * block, block), block)
        return remote(dsend_ref.at[b], dm_ref.at[at], dm_s.at[b], dm_r.at[b], partner)

    def dm_from(b):
        at = pl.ds(pl.multiple_of((1 - side) * rows + b * block, block), block)
        return remote(dsend_ref.at[b], dm_ref.at[at], dm_s.at[b], dm_r.at[b], partner)

    def out_copy(j):
        return pltpu.make_async_copy(send_ref.at[j], out_ref.at[j], out_sem.at[j])

    def o_copy(j):
        return remote(send_ref.at[j], xfirst.at[0, pl.ds(2 * j, 2)], o_s.at[j], o_r.at[j], partner)

    all_here = greet()
    for n, vector in enumerate((g1_ref, s1_ref, ob_ref, g2_ref, s2_ref, db_ref)):
        par_ref[pl.ds(n, 1)] = vector[...].astype(F32).reshape(1, width)
    for n in range(half):
        ubo_ref[pl.ds(n, 1)] = ub_ref[pl.ds(n * hb, hb)].astype(F32).reshape(1, hb)
    bias_copy = remote(ubo_ref, ubt_ref, b_s, b_r, partner)
    a1_ref = sum_ref

    def a1_copy(which, b):
        return remote(a1_ref.at[which, b], a1_ref.at[which, b], a_s.at[b], a_r.at[b], partner)

    def wqkv_parts(ref):
        return [(wqkv_hbm.at[n], ref.at[:, pl.ds(n * local, local)]) for n in range(3)]

    def wout_own():
        return wout_ref[0].reshape(local, width)

    def wout_other():
        return wout_ref[1].reshape(local, width)

    def ahead(x_ref, wqkv_ref, qkv_ref, mix_ref, mask_ref):
        loads = [
            pltpu.make_async_copy(src, dst, l_sem.at[n])
            for n, (src, dst) in enumerate(((x_hbm, x_ref), (wout_hbm, wout_ref.at[0]), *wqkv_parts(wqkv_ref)))
        ]
        for load in loads:
            load.start()
        gain = par_ref[pl.ds(GAIN_1, 1)]
        shift = par_ref[pl.ds(SHIFT_1, 1)]
        loads[0].wait()
        for b in range(4):
            xhat, _ = norm_parts(x_ref[pl.ds(b * piece, piece)].astype(F32))
            a1_ref[side, b] = (xhat * gain + shift).astype(BF16).reshape(2, 64, width)
            if b == 0:
                all_here()
            a1_copy(side, b).start()
            if b == 0:
                g_start(0)
            if b < 2:
                g_start(1 + b)
        bias_copy.start()
        g_start(3)

        def project(left, base, count):
            at = pl.ds(pl.multiple_of(base, block), count)
            for part in range(3):
                cols = pl.ds(part * local, local)
                value = dot_nn(left, wqkv_ref[:, cols])
                if part != 1:
                    value = value + qvb_ref[pl.ds(part // 2, 1)].astype(F32)
                qkv_ref[at, cols] = value.astype(BF16)

        for load in loads[2:]:
            load.wait()
        project(a1_ref[side].reshape(rows, width), own, rows)

        def mix_copy(j):
            at = pl.ds(pl.multiple_of(theirs + j * block, block), block)
            far = mixt_ref.at[pl.ds(j * block, block)]
            return remote(mix_ref.at[at], far, m_s.at[j], m_r.at[j], partner)

        seg_row = seg_ref[...].astype(F32)
        seg_col = jnp.broadcast_to(seg_row, (8, seq)).T[:, :1]
        run(A_TICKS["start"])

        @pl.when(side == 1)
        def _():
            run(A_TICKS["block"])

        for i in range(4):
            lo = i * block
            keys = lo + block
            is_theirs = side == (1 if i < 2 else 0)
            at = pl.ds(lo, block)
            if i == 1:

                @pl.when(side == 0)
                def _():
                    run(A_TICKS["block"])

            @pl.when(is_theirs)
            def _():
                j = i % 2
                run(A_TICKS["middle" if j else "early"])
                for b in (2 * j, 2 * j + 1):
                    a1_copy(1 - side, b).wait_recv()
                project(a1_ref[1 - side, pl.ds(2 * j, 2)].reshape(block, width), lo, block)

            same = seg_col[:keys] == seg_row[:, lo : lo + block]
            k_pos = lax.broadcasted_iota(jnp.int32, (keys, block), 0)
            q_pos = lo + lax.broadcasted_iota(jnp.int32, (keys, block), 1)
            mask_ref[pl.ds(0, keys)] = jnp.where(same & (q_pos >= k_pos), 0.0, -1e30)

            def pair(hp, _):
                base = pl.multiple_of(hp * 2 * HEAD_DIM, 2 * HEAD_DIM)
                cols = pl.ds(base, 2 * HEAD_DIM)
                q2 = qkv_ref[at, cols]
                k2 = qkv_ref[pl.ds(0, keys), pl.ds(pl.multiple_of(local + base, 128), 2 * HEAD_DIM)]
                v2 = qkv_ref[pl.ds(0, keys), pl.ds(pl.multiple_of(2 * local + base, 128), 2 * HEAD_DIM)]
                out = jnp.zeros((block, 2 * HEAD_DIM), F32)
                for h in range(2):
                    scores = dot_nt(k2, only_head(q2, h)) * scale + mask_ref[pl.ds(0, keys)]
                    top = jnp.max(scores, axis=0, keepdims=True)
                    weights = jnp.exp(scores - top)
                    total = total_of(weights)
                    lse_ref[pl.ds(2 * hp + h, 1), at] = top + jnp.log(total)
                    out += dot_tn((weights * (1.0 / total)).astype(BF16), only_head(v2, h))
                mix_ref[at, cols] = out.astype(BF16)
                return 0

            lax.fori_loop(0, local // (2 * HEAD_DIM), pair, 0)

            @pl.when(is_theirs)
            def _():
                mix_copy(i % 2).start()
                if i % 2:
                    g_start(4)
                    run(A_TICKS["late"])

        saves = [
            pltpu.make_async_copy(src, dst, l_sem.at[n])
            for n, (src, dst) in enumerate(((qkv_ref, qkv_hbm), (mix_ref, mix_hbm), (a1_ref.at[pl.ds(0, 2)], a1_hbm)), start=5)
        ]
        for save in saves:
            save.start()
        loads[1].wait()
        g_last(0)
        for j in range(2):
            at = pl.ds(j * block, block)
            mix_copy(j).wait_recv()
            mine = dot_nn(mix_ref[pl.ds(pl.multiple_of(own + j * block, block), block)], wout_own())
            din_ref[at] = (
                x_ref[at].astype(F32) + (mine + dot_nn(mixt_ref[at], wout_other())) + par_ref[pl.ds(OUT_BIAS, 1)]
            )
        run(A_TICKS["end"])
        for save in saves:
            save.wait()
        for j in range(2):
            mix_copy(j).wait_send()
        for b in range(4):
            a1_copy(side, b).wait_send()
        bias_copy.wait()

    pl.run_scoped(
        ahead,
        vmem((rows, width), BF16), vmem((width, 3 * local), BF16), vmem((seq, 3 * local), BF16), vmem((seq, local), BF16),
        vmem((seq, block), F32),
    )

    h_ref = din_ref

    def feed(g_ref, a2_ref, a2t_ref, gt_ref, wu_ref, wd_ref, in_sem, w_sem):
        load_g = pltpu.make_async_copy(g_hbm, g_ref, in_sem)
        load_g.start()

        def fetch(b, up, down, slot):
            at = pl.ds(pl.multiple_of(b * hb, hb), hb)
            return (
                pltpu.make_async_copy(up.at[:, at], wu_ref.at[slot], w_sem.at[slot, 0]),
                pltpu.make_async_copy(down.at[at], wd_ref.at[slot], w_sem.at[slot, 1]),
            )

        def fetch_start(p, slot):
            for n in range(n_mlp):
                if is_other(n):

                    @pl.when(p == n)
                    def _():
                        g_last(1 + hidden_of(n))

            @pl.when(is_other(p))
            def _():
                for copy in fetch(hidden_of(p), up_oth, down_oth, slot):
                    copy.start()

            @pl.when(jnp.logical_not(is_other(p)))
            def _():
                for copy in fetch(hidden_of(p), up_own, down_own, slot):
                    copy.start()

        fetch_start(jnp.int32(0), 0)
        gain = par_ref[pl.ds(GAIN_2, 1)]
        xhat, _ = norm_parts(h_ref[...])
        a2 = (xhat * gain + par_ref[pl.ds(SHIFT_2, 1)]).astype(BF16)
        a2_ref[...] = a2
        a2t_ref[...] = a2.T
        load_g.wait()
        gt_ref[...] = g_ref[...].T
        dkv_ref[...] = jnp.zeros_like(dkv_ref)
        acc_ref = dkv_ref.at[pl.ds(0, rows)]
        da2_ref = dkv_ref.at[pl.ds(rows, rows)]

        def step(p, _):
            slot = p % 2
            for copy in fetch(0, up_own, down_own, slot):
                copy.wait()

            @pl.when(p + 1 < n_mlp)
            def _():
                fetch_start(p + 1, 1 - slot)

            b = hidden_of(p)
            wu, wd = wu_ref[slot], wd_ref[slot]
            u = dot_nn(a2_ref[...], wu) + jnp.where(is_other(p), ubt_ref[pl.ds(b, 1)], ubo_ref[pl.ds(b, 1)])
            back = dot_nt(g_ref[...], wd)
            tanh = jnp.tanh(0.7978845608028654 * (u + 0.044715 * u * u * u))
            hidden = (0.5 * u * (1.0 + tanh)).astype(BF16)
            slope = 0.5 * (1.0 + tanh) + 0.5 * u * (1.0 - tanh * tanh) * (
                0.7978845608028654 * (1.0 + 3.0 * 0.044715 * u * u)
            )
            acc_ref[...] += dot_nn(hidden, wd)
            grad_ref[slot, :, :, :, pl.ds(hb, hb)] = dot_nn(gt_ref[...], hidden).astype(BF16).reshape(8, 2, 64, hb)
            du = (back * slope).astype(BF16)
            where_side = jnp.where(is_other(p), 1 - side, side)
            lanes = pl.ds(pl.multiple_of((b % 2) * hb, hb), hb)
            vsum[0, 0, pl.ds(4 + where_side * (half // 2) + b // 2, 1), lanes] = total_of(du.astype(F32))
            da2_ref[...] += dot_nt(du, wu)
            grad_ref[slot, :, :, :, pl.ds(0, hb)] = dot_nn(a2t_ref[...], du).astype(BF16).reshape(8, 2, 64, hb)
            produced(p, 2 * hb)

            for n, names in B_TICKS.items():

                @pl.when(p == n)
                def _():
                    run(names)

            @pl.when(p >= 1)
            def _():
                consume(p - 1, 2 * hb)
                push(p - 1, 2 * hb)

            return 0

        vsum[0, 0] = jnp.zeros(vsum.shape[2:], F32)
        vsum[1, 0] = jnp.zeros(vsum.shape[2:], F32)
        run(B_START)
        lax.fori_loop(0, n_mlp, step, 0)

        piece = rows // 4
        sums = [jnp.zeros((1, width), F32) for _ in range(4)]
        for b in range(4):
            at = pl.ds(b * piece, piece)
            h = h_ref[at]
            g = g_ref[at].astype(F32)
            out = (h + acc_ref[at] + par_ref[pl.ds(DOWN_BIAS, 1)]).astype(BF16)
            send_ref[b // 2, b % 2] = out.reshape(2, 64, width)
            xhat, rstd = norm_parts(h)
            da2 = da2_ref[at]
            dh = g + norm_back(da2, gain, xhat, rstd)
            din_ref[at] = dh
            for n, term in enumerate((da2 * xhat, da2, dh.astype(BF16).astype(F32), g)):
                sums[n] = sums[n] + total_of(term)
        for n in range(4):
            vsum[0, 0, pl.ds(n, 1)] = sums[n]
        vectors(0, 0)
        for j in range(2):
            out_copy(j).start()

    pl.run_scoped(
        feed,
        vmem((rows, width), BF16), vmem((rows, width), BF16), vmem((width, rows), BF16),
        vmem((width, rows), BF16), vmem((2, width, hb), BF16), vmem((2, hb, width), BF16), sem, sem((2, 2)),
    )

    def attend(qkv_ref, mix_ref, wqkv_ref, mask_ref, dhl_ref, in_sem):
        x_ref, dqkv_ref = dhl_ref, qkv_ref
        moves = [
            pltpu.make_async_copy(src, dst, in_sem.at[n])
            for n, (src, dst) in enumerate((
                (mix_hbm, mix_ref), (qkv_hbm, qkv_ref), (x_hbm, x_ref), (a1_hbm, wout_ref), *wqkv_parts(wqkv_ref),
            ))
        ]
        for n in (0, 1, 4, 5, 6):
            moves[n].start()
        dhl_ref[...] = din_ref[...].astype(BF16)
        consume(n_mlp - 1, 2 * hb)
        push(n_mlp - 1, 2 * hb)
        for b in (1, 0):
            dsend_ref[b] = dot_nt(dhl_ref[pl.ds(b * block, block)], wout_other()).astype(BF16)
            dm_copy(b).start()
        for b in range(1, nx):
            xfirst_copy(b).start()
        dm_own[...] = dot_nt(dhl_ref[...], wout_own()).astype(BF16)
        g_sent(0)
        moves[3].start()
        moves[0].wait()
        p = n_mlp
        for part in range(2):
            mixed = mixt_ref[...] if part else mix_ref[pl.ds(own, rows)]
            grad = dot_tn(dhl_ref[...], mixed).astype(BF16)
            grad_ref[p % 2, :, :, :, pl.ds(part * hb, hb)] = grad.reshape(8, 2, 64, hb)
        produced(p, 2 * hb)
        moves[2].start()
        dkv_ref[...] = jnp.zeros_like(dkv_ref)
        seg_row = seg_ref[...].astype(F32)
        seg_col = jnp.broadcast_to(seg_row, (8, seq)).T[:, :1]
        moves[1].wait()
        for j in range(2):
            out_copy(j).wait()

        def task(i, keys, stage="all", ticks=()):
            lo, start, count = i * block, keys[0], keys[1] - keys[0]
            at, among = pl.ds(lo, block), pl.ds(start, count)
            same = seg_col[start : start + count] == seg_row[:, lo : lo + block]
            k_pos = start + lax.broadcasted_iota(jnp.int32, (count, block), 0)
            q_pos = lo + lax.broadcasted_iota(jnp.int32, (count, block), 1)
            mask_ref[pl.ds(0, count)] = jnp.where(same & (q_pos >= k_pos), 0.0, -1e30)

            def pair(hp, _):
                base = pl.multiple_of(hp * 2 * HEAD_DIM, 2 * HEAD_DIM)
                cols = pl.ds(base, 2 * HEAD_DIM)
                v_cols = pl.ds(pl.multiple_of(local + base, 128), 2 * HEAD_DIM)
                q2 = qkv_ref[at, cols]
                k2 = qkv_ref[among, v_cols]
                v2 = qkv_ref[among, pl.ds(pl.multiple_of(2 * local + base, 128), 2 * HEAD_DIM)]
                g2 = dm_ref[at, cols]
                turned = (g2.astype(F32) * mix_ref[at, cols].astype(F32)).T
                dq = jnp.zeros((block, 2 * HEAD_DIM), F32)
                dk = jnp.zeros((count, 2 * HEAD_DIM), F32)
                dv = jnp.zeros((count, 2 * HEAD_DIM), F32)
                for h in range(2):
                    qh = only_head(q2, h)
                    gh = only_head(g2, h)
                    row_dot = total_of(turned[h * HEAD_DIM : (h + 1) * HEAD_DIM])
                    offset = mask_ref[pl.ds(0, count)] - lse_ref[pl.ds(2 * hp + h, 1), at]
                    probs = jnp.exp(dot_nt(k2, qh) * scale + offset)
                    dscore = (probs * (dot_nt(v2, gh) - row_dot)).astype(BF16)
                    dv += dot_nn(probs.astype(BF16), gh)
                    dk += dot_nn(dscore, qh)
                    dq += dot_tn(dscore, only_head(k2, h))
                if stage == "first":
                    dq_ref[i - 2, :, cols] = dq
                else:
                    if stage == "last":
                        dq = dq + dq_ref[i - 2, :, cols]
                    dqkv_ref[at, cols] = (dq * scale).astype(BF16)
                dkv_ref[among, cols] += dk
                dkv_ref[among, v_cols] += dv
                for n, names in ticks:

                    @pl.when(hp == n)
                    def _():
                        run(names)

                return 0

            lax.fori_loop(0, local // (2 * HEAD_DIM), pair, 0)

        def finish(i, send):
            at = pl.ds(i * block, block)
            dqkv_ref[at, pl.ds(local, local)] = (dkv_ref[at, pl.ds(0, local)] * scale).astype(BF16)
            dqkv_ref[at, pl.ds(2 * local, local)] = dkv_ref[at, pl.ds(local, local)].astype(BF16)
            product = dot_nt(dqkv_ref[at], wqkv_ref[...])
            if send:
                send_ref[i % 2] = product.astype(BF16).reshape(send_ref.shape[1:])
                o_copy(i % 2).start()
            else:
                dkv_ref[at] = product

        def second_block():
            consume(n_mlp, 2 * hb)
            push(n_mlp, 2 * hb)
            vectors(0, 1)
            for move in moves[4:]:
                move.wait()

        @pl.when(side == 0)
        def _():
            run(C_TICKS[0][0])
            dm_from(1).wait_recv()
            task(3, (0, 4 * block), ticks=C_TICKS[0][1])
            second_block()
            finish(3, True)
            dm_from(0).wait_recv()
            task(2, (0, 3 * block), ticks=C_TICKS[0][2])
            finish(2, True)
            task(1, (0, 2 * block), ticks=C_TICKS[0][3])
            finish(1, False)
            task(0, (0, block), ticks=C_TICKS[0][4])
            finish(0, False)

        @pl.when(side == 1)
        def _():
            task(3, (0, 2 * block), "first", ticks=C_TICKS[1][1])
            task(2, (0, 2 * block), "first", ticks=C_TICKS[1][2])
            second_block()
            dm_from(1).wait_recv()
            task(1, (0, 2 * block), ticks=C_TICKS[1][3])
            finish(1, True)
            dm_from(0).wait_recv()
            task(0, (0, block), ticks=C_TICKS[1][4])
            finish(0, True)
            task(3, (2 * block, 4 * block), "last", ticks=C_TICKS[1][5])
            finish(3, False)
            task(2, (2 * block, 3 * block), "last", ticks=C_TICKS[1][6])
            finish(2, False)

        moves[3].wait()
        for part in range(3):
            p = n_mlp + 1 + part
            grad = dot_tn(wout_ref[...].reshape(seq, width), dqkv_ref[:, pl.ds(part * local, local)]).astype(BF16)
            grad_ref[p % 2, :, :, :, pl.ds(0, hb)] = grad.reshape(8, 2, 64, hb)
            produced(p, hb)
            if part == 1:
                consume(p - 1, hb)
                push(p - 1, hb)
        moves[2].wait()

        def din_copy(j):
            return pltpu.make_async_copy(stage_ref, dinr_ref.at[pl.ds(j * block, block)], in_sem.at[j])

        def finish_rows(j):
            at = pl.ds(j * block, block)
            o_copy(j).wait_recv()
            da1 = dkv_ref[pl.ds(pl.multiple_of(own + j * block, block), block)] + xfirst[0, pl.ds(2 * j, 2)].reshape(
                block, width
            ).astype(F32)
            xhat, rstd = norm_parts(x_ref[at].astype(F32))
            grad = din_ref[at] + norm_back(da1, par_ref[pl.ds(GAIN_1, 1)], xhat, rstd)
            if j == 0:
                din_copy(1).wait()
            stage_ref[...] = grad.reshape(block, 8, width // 8)
            din_copy(j).start()
            return total_of(da1 * xhat), total_of(da1)

        lanes = pl.ds(pl.multiple_of(side * local, local), local)
        vsum[1, 0, pl.ds(2, 1), lanes] = total_of(dqkv_ref[:, pl.ds(0, local)].astype(F32))
        vsum[1, 0, pl.ds(3, 1), lanes] = total_of(dqkv_ref[:, pl.ds(2 * local, local)].astype(F32))
        push(DELAYED, 2 * hb)
        consume(n_mlp + 2, hb)
        push(n_mlp + 2, hb)
        run(END_TICKS)
        consume(n_mlp + 3, hb)
        run(MORE_TICKS[0])
        gain_1, shift_1 = finish_rows(1)
        run(MORE_TICKS[1])
        gain_0, shift_0 = finish_rows(0)
        vsum[1, 0, pl.ds(0, 1)] = gain_0 + gain_1
        vsum[1, 0, pl.ds(1, 1)] = shift_0 + shift_1
        vectors(1, 0)
        din_copy(0).wait()

    pl.run_scoped(
        attend,
        vmem((seq, 3 * local), BF16), vmem((seq, local), BF16), vmem((width, 3 * local), BF16), vmem((seq, block), F32),
        vmem((rows, width), BF16), sem((7,)),
    )

    run(TAIL)
    qvg_ref[...] = vec_ref[pl.ds(VEC_ROWS + 2, 2), pl.ds(pl.multiple_of(side * local, local), local)]
    for n in range(2):
        ubg_ref[pl.ds(n, 1)] = vec_ref[pl.ds(4 + side * 2 + n, 1)]
    for q in range(1, half + 1):
        g_sent(q)
    for j in range(2):
        dm_copy(j).wait_send()
        o_copy(j).wait_send()
    for p in range(n_all):
        if all(before(n) != p for n in range(n_all)):
            sent(p)
    for p in range(n_all):
        if p > n_mlp or PLACE[p] is not None:
            for k in (1, 2, 3):
                z_copy(p, k, cols_of(p)).wait_send()
    for n in range(half - nx + 1):
        x_copy(n).wait_send()


def step_call(vectors, ub, qvb, seg, x, g, wqkv, wout, up, down):
    rows, width = x.shape
    local = wout.size // width
    seq = 2 * rows
    block = rows // 2
    hb = HIDDEN_BLOCK
    nx = CROSS_FIRST
    height = width // PIECES
    vm = pl.BlockSpec(memory_space=pltpu.VMEM)
    hbm = pl.BlockSpec(memory_space=pltpu.HBM)
    sem = pltpu.SemaphoreType.DMA
    ny = N_ALL
    places = PLACE[N_MLP] + 3
    nxl = HALF - nx + 1
    shape = jax.ShapeDtypeStruct
    return pl.pallas_call(
        step_kernel,
        out_shape=(
            shape((2, 2, 2, height, width), BF16),
            shape((rows, 8, width // 8), F32),
            shape((height, HALF * hb), F32),
            shape((height, HALF * hb), F32),
            shape((height, local), F32),
            shape((3, height, local), F32),
            shape((2 * VEC_ROWS, width), F32),
            shape((2, local), F32),
            shape((2, width), F32),
            shape((2, 4, 2, height, width), BF16),
            shape((seq, 3 * local), BF16),
            shape((seq, local), BF16),
            shape(up.shape, BF16),
            shape(down.shape, BF16),
        ),
        in_specs=[vm] * 9 + [hbm] * 6,
        out_specs=(hbm,) * 2 + (vm,) * 7 + (hbm,) * 5,
        scratch_shapes=[
            pltpu.VMEM((2, 4, 2, height, width), BF16),
            pltpu.VMEM((rows, local), BF16),
            pltpu.VMEM((local // HEAD_DIM, seq), F32),
            pltpu.VMEM((8, width), F32),
            pltpu.VMEM((8, hb), F32),
            pltpu.VMEM((8, hb), F32),
            pltpu.VMEM((rows, width), F32),
            pltpu.VMEM((block, 8, width // 8), F32),
            pltpu.VMEM((seq, width), F32),
            pltpu.VMEM((seq, local), BF16),
            pltpu.VMEM((2, block, local), BF16),
            pltpu.VMEM((2, 2, 2, height, width), BF16),
            pltpu.VMEM((2, block, local), F32),
            pltpu.VMEM((2, 8, 2, height, 2 * hb), BF16),
            pltpu.VMEM((2, 8, height, 2 * hb), BF16),
            pltpu.VMEM((S_SLOTS, 4, 2, height, 2 * hb), BF16),
            pltpu.VMEM((places, 4, height, 2 * hb), BF16),
            pltpu.VMEM((places, 3, height, 2 * hb), BF16),
            pltpu.VMEM((3, 2, height, 2 * hb), BF16),
            pltpu.VMEM((3, height, 2 * hb), BF16),
            pltpu.VMEM((nx, 4, 2, height, 2 * hb), BF16),
            pltpu.VMEM((nxl, height, 2 * hb), BF16),
            pltpu.VMEM((nxl, height, 2 * hb), BF16),
            pltpu.VMEM((2, 4, VEC_ROWS, width), F32),
            pltpu.VMEM((2, 7, VEC_ROWS, width), F32),
            sem((4,)), sem((4,)), sem((2,)), sem((2,)), sem, sem, sem((8,)),
            sem((2,)), sem((2,)), sem((ny,)), sem((ny,)), sem((ny, 3)), sem((ny, 3)),
            sem((nx,)), sem((nx,)), sem((nxl,)), sem((nxl,)), sem((2, 7)), sem((2, 7)),
            sem((2,)), sem((2,)), sem((2,)), sem((2,)), sem((2,)), pltpu.SemaphoreType.REGULAR,
            *gather_semaphores(1 + HALF),
        ],
        compiler_params=pltpu.CompilerParams(
            collective_id=0, has_side_effects=True, vmem_limit_bytes=VMEM_LIMIT
        ),
        name="train_step",
    )(*vectors, ub, qvb, seg, x, g, wqkv, wout, up, down)


def settle_kernel(*refs):
    sources, results, scratch, sems = refs[:9], refs[9:23], refs[23:29], refs[29]
    reads = [pltpu.make_async_copy(s, v, sems.at[0, n]) for n, (s, v) in enumerate(zip(sources[:6], scratch))]
    writes = [pltpu.make_async_copy(v, r, sems.at[1, n]) for n, (v, r) in enumerate(zip(scratch, results[:6]))]
    for copy in reads:
        copy.start()
    vec_ref, qv_ref, ub_ref = sources[6:]
    width = vec_ref.shape[1]
    for n, row in enumerate((VEC_ROWS, VEC_ROWS + 1, 2, 0, 1, 3)):
        results[6 + n][...] = vec_ref[pl.ds(row, 1)].reshape(width)
    results[12][...] = qv_ref[...]
    for n in range(2):
        results[13][pl.ds(n * width, width)] = ub_ref[pl.ds(n, 1)].reshape(width)
    for read, write in zip(reads, writes):
        read.wait()
        write.start()
    for copy in writes:
        copy.wait()


def settle_call(*arrays):
    vm = pl.BlockSpec(memory_space=pltpu.VMEM)
    hbm = pl.BlockSpec(memory_space=pltpu.HBM)
    width = arrays[6].shape[1]
    shapes = [a.shape for a in arrays[:6]] + [(width,)] * 6 + [arrays[7].shape, (2 * width,)]
    dtypes = [a.dtype for a in arrays[:6]] + [F32] * 8
    return pl.pallas_call(
        settle_kernel,
        out_shape=[jax.ShapeDtypeStruct(s, d) for s, d in zip(shapes, dtypes)],
        in_specs=[hbm] * 6 + [vm] * 3,
        out_specs=[hbm] * 6 + [vm] * 8,
        scratch_shapes=[*(pltpu.VMEM(a.shape, a.dtype) for a in arrays[:6]), pltpu.SemaphoreType.DMA((2, 6))],
        compiler_params=pltpu.CompilerParams(vmem_limit_bytes=VMEM_LIMIT),
        name="settle",
    )(*arrays)


def on_device_pair(
    inputs, segment_ids, first_gain, first_shift, qkv_weight, qv_bias, out_weight, out_bias,
    second_gain, second_shift, up_weight, up_bias, down_weight, down_bias, cotangent,
):
    rows, _, width = inputs.shape
    seq = segment_ids.shape[0]
    local = out_weight.shape[0]
    x = inputs.reshape(rows, width)
    g = cotangent.reshape(rows, width)
    seg = segment_ids.reshape(1, seq)
    height = width // PIECES
    wout = out_weight.reshape(4, 2, height, width)
    vectors = (first_gain, first_shift, out_bias, second_gain, second_shift, down_bias)
    wqkv = jnp.transpose(qkv_weight, (1, 0, 2))
    layer_output, input_grad, up_g, down_g, out_g, qkv_g, first_gain_g, first_shift_g, out_bias_g, second_gain_g, \
        second_shift_g, down_bias_g, qv_g, up_bias_g = settle_call(
            *step_call(vectors, up_bias, qv_bias, seg, x, g, wqkv, wout, up_weight, down_weight)[:9]
        )
    return (
        layer_output.reshape(rows, 1, width),
        input_grad.reshape(rows, 1, width),
        first_gain_g,
        first_shift_g,
        jnp.transpose(qkv_g, (1, 0, 2)),
        qv_g,
        out_g.T,
        out_bias_g,
        second_gain_g,
        second_shift_g,
        up_g,
        up_bias_g,
        down_g.T,
        down_bias_g,
    )


def solution(mesh):
    in_specs = (
        P("tensor", "dp", None),
        P(None, "dp"),
        P(),
        P(),
        P(None, None, "tensor"),
        P(None, "tensor"),
        P("tensor", None),
        P(),
        P(),
        P(),
        P(None, "tensor"),
        P("tensor"),
        P("tensor", None),
        P(),
        P("tensor", "dp", None),
    )
    out_specs = (
        P("tensor", "dp", None),
        P("tensor", "dp", None),
        P(),
        P(),
        P("dp", None, "tensor"),
        P(None, "tensor"),
        P("tensor", "dp"),
        P(),
        P(),
        P(),
        P("dp", "tensor"),
        P("tensor"),
        P("tensor", "dp"),
        P(),
    )
    pair = mesh.shape["tensor"] == 2 and mesh.shape["dp"] == Z_SIZE * Y_SIZE * CORES
    return jax.shard_map(
        on_device_pair if pair else on_device, mesh=mesh, in_specs=in_specs, out_specs=out_specs, check_vma=False
    )
```
